32 devices in a mesh: gx: 4 (over z), gy: 8 (over y, x, core).
Axes of the slice: x: 2, y: 2, z: 4, core: 2. Of those that a mesh axis runs over, the one named last changes fastest.
Arguments:
- block_input: bfloat16 [4096, 2048], P('gx', 'gy'), may hold values from -6 to 6
- out_grad: bfloat16 [4096, 2048], P('gx', 'gy'), may hold values from -6 to 6
- routes: int32 [4096, 8], P('gx'), may hold values from 0 to 31, all different within a row; in each aligned block of 1024 rows (0 to 1023, 1024 to 2047, ...) at most 288 rows name the same one
- adapter_ids: int32 [4], P('gx'), may hold values from 0 to 7
- piece_starts: int32 [4, 2], P('gx'), may hold values from 0 to 768, as said below
- attn_gain: float32 [2048], replicated, may hold values from 0.1 to 1.9
- qk_gain: float32 [2, 2048], replicated, may hold values from 0.1 to 1.9
- mlp_gain: float32 [2048], replicated, may hold values from 0.1 to 1.9
- w_qkv: bfloat16 [2048, 16, 3, 128], P('gx', 'gy'), may hold values from -0.125 to 0.125
- w_out: bfloat16 [16, 128, 2048], P('gy', None, 'gx'), may hold values from -3 to 3
- a_qkv: bfloat16 [3, 2048, 128], P(None, 'gy'), may hold values from -0.125 to 0.125
- b_out: bfloat16 [128, 2048], P(None, 'gy'), may hold values from -1 to 1
- head_pack: bfloat16 [16, 4, 128, 128], P('gy'), may hold values from -1.5 to 1.5
- router: bfloat16 [2048, 32], replicated, may hold values from -0.0625 to 0.0625
- w_gate_up: bfloat16 [32, 2048, 2, 1024], P('gy', 'gx'), may hold values from -0.125 to 0.125
- w_down: bfloat16 [32, 2048, 1024], P('gy', 'gx'), may hold values from -1.5 to 1.5
- exp_wide: bfloat16 [32, 2048, 3, 128], P('gy', 'gx'), may hold values from -0.125 to 0.125
- exp_hidden: bfloat16 [32, 1024, 3, 128], P('gy', 'gx'), may hold values from -1.5 to 1.5
Outputs:
- layer_out: bfloat16 [4096, 2048], P('gx', 'gy')
- input_grad: float32 [4096, 2048], P('gx', 'gy')
- a_qkv_grad: float32 [3, 2048, 128], P(None, 'gy')
- b_out_grad: float32 [128, 2048], P(None, 'gy')
- head_pack_grad: float32 [16, 4, 128, 128], P('gy')
- exp_wide_grad: float32 [32, 2048, 3, 128], P('gy', 'gx')
- exp_hidden_grad: float32 [32, 1024, 3, 128], P('gy', 'gx')
The draws below stay inside these ranges and needn't reach their ends.
Inputs may be any that keep to these rules, and one draw needn't show every extreme that they name: `routes`: in each aligned block of the rows that one index of gx holds, no expert is named by more than 288 rows, a bound that some block reaches. `piece_starts`: each sequence has two pieces of 256 positions; the first starts in the first half of the sequence and ends in it, the second lies in the second half.
All inputs are finite; a program needn't handle non-finite values.
Results may differ from the reference program's by a relative error of at most 0.02.
Values may be sent and summed in bfloat16 or wider, within the bound.
A program may use at most 320 MiB of HBM per device.

```python
import math
import jax
import jax.numpy as jnp
import numpy as np
from jax import lax

D = 2048
HEADS = 16
HEAD = 128
FF = 1024
TOPK = 8
EXPERTS = 32
RANK = 16
ADAPTERS = 8
AR = 128
SEQ = 1024
PIECE = 256
TOK_DEV = 128
TOKENS = 4096
NSEQ = 4
CAP = 288
N_GX = 4
N_GY = 8


def draw_piece_starts(key, part):
    key = jax.random.fold_in(key, 11)
    first_key, second_key = jax.random.split(key)
    first = jax.random.randint(first_key, (NSEQ,), 0, SEQ // 2 - PIECE + 1)
    second = SEQ // 2 + jax.random.randint(second_key, (NSEQ,), 0, SEQ // 2 - PIECE + 1)
    return jnp.stack([first, second], axis=1).astype(jnp.int32)


def plant(values, rng, low, high):
    dims = values.shape
    index_at = [jax.random.randint(jax.random.fold_in(rng, axis), (), 0, dims[axis]) for axis in range(len(dims))]
    values = values.at[tuple(index_at)].set(low)
    longest = dims.index(max(dims))
    index_at[longest] = (index_at[longest] + 1) % dims[longest]
    return values.at[tuple(index_at)].set(high)


def block_scale(key, shape, shards, low, high):
    loudness = 1.0
    for position, shards_of in shards:
        heights = jax.random.uniform(jax.random.fold_in(jax.random.fold_in(key, 6), position), (shards_of,), jnp.float32, low / len(shards), high / len(shards))
        loudness = loudness * jnp.repeat(jnp.exp(heights), shape[position] // shards_of).reshape((-1,) + (1,) * (len(shape) - 1 - position))
    return loudness


def deal_out(key, own, number, rows, amount, top, limit, skew):
    order = jax.random.permutation(key, amount)
    crowded, common = portions_of(amount, rows * top, limit, skew, True), portions_of(amount, rows * top, limit, skew, False)
    places = jnp.arange(amount)

    def named(sizes, turn):
        used = int((sizes > 0).sum())
        fixed = max(1, used // 4)
        shifted = fixed + (places - fixed + turn * (used - fixed)) % max(1, amount - fixed)
        return jnp.zeros((amount,), jnp.int32).at[order[jnp.where(places < fixed, places, shifted)]].set(jnp.asarray(sizes, jnp.int32))

    sizes = jnp.where(number % 4 == 0, named(crowded, number // 4), named(common, number - number // 4 - 1))
    mixed = jax.random.permutation(jax.random.fold_in(own, 3), amount)
    source_of, receiver = mixed[0:amount // 2 * 2:2], mixed[1:amount // 2 * 2:2]
    margin = jnp.minimum(sizes[source_of] - 1, limit - sizes[receiver]) // 2
    margin = jnp.where((source_of == order[0]) | (receiver == order[0]) | (sizes[receiver] == 0), 0, jnp.maximum(margin, 0))
    shifted = jax.random.randint(jax.random.fold_in(own, 4), (amount // 2,), 0, 1 << 20) % (margin + 1)
    sizes = sizes.at[source_of].add(-shifted).at[receiver].add(shifted)
    labels = jnp.searchsorted(jnp.cumsum(sizes), jnp.arange(rows * top), side="right").astype(jnp.int32)
    grid = labels.reshape(top, rows).T
    grid = grid[jax.random.permutation(jax.random.fold_in(own, 1), rows)]
    turn = jax.random.randint(jax.random.fold_in(own, 2), (rows, 1), 0, top)
    return jnp.take_along_axis(grid, (jnp.arange(top)[None, :] + turn) % top, axis=1)


def portions_of(count, total, bound, slope, full):
    portions = [(1 << 20) // math.isqrt(standing ** slope) + 1 for standing in range(1, count + 1)]
    largest = bound if full else min(bound, max(-(-total // count), total * portions[0] // sum(portions)))
    least = 1 if total - largest >= count - 1 else 0
    given, surplus = [largest] + [least] * (count - 1), total - largest - least * (count - 1)
    while surplus > 0:
        free = [i for i in range(1, count) if given[i] < largest] or [i for i in range(1, count) if given[i] < bound]
        mass, left = sum([portions[i] for i in free]), surplus
        for i in free:
            extra = min(bound - given[i], max(1, left * portions[i] // mass), surplus)
            given[i] = given[i] + extra
            surplus = surplus - extra
    return np.array(given)


def normal_values(stream_key, dims, scale, bound, cuts=(), kind=jnp.bfloat16):
    drawn = jax.random.normal(stream_key, dims, jnp.float32) * scale
    if len(cuts) > 0:
        drawn = block_scale(stream_key, dims, cuts, -0.22, 0.18) * drawn
    return jnp.clip(drawn, min=-bound, max=bound).astype(kind)


def setup_inputs(seed: int = 0) -> dict:
    seeds = jax.random.split(jax.random.key(seed), 19)
    block_input = normal_values(seeds[0], (TOKENS, D), 1.0, 6.0, ((0, 4), (1, 8)))
    out_grad = normal_values(seeds[1], (TOKENS, D), 1.0, 6.0, ((0, 4), (1, 8)))
    routes_keys = jax.random.split(jax.random.fold_in(seeds[2], 1), TOKENS // (TOK_DEV * N_GY))
    routes_turns = jax.random.permutation(jax.random.fold_in(seeds[2], 3), TOKENS // (TOK_DEV * N_GY))
    routes = jax.vmap(lambda own, number: deal_out(jax.random.fold_in(seeds[2], 2), own, number, TOK_DEV * N_GY, EXPERTS, TOPK, CAP, 0))(routes_keys, routes_turns).reshape((TOKENS, TOPK))
    adapter_ids = plant(jax.random.randint(seeds[3], (NSEQ,), 0, ADAPTERS), jax.random.fold_in(seeds[3], 1), 0, ADAPTERS - 1).astype(jnp.int32)
    piece_starts = draw_piece_starts(jax.random.fold_in(seeds[18], 71), 0)
    attn_gain = jnp.clip(1.0 + 0.18 * jax.random.normal(seeds[5], (D,), jnp.float32), 0.1, 1.9)
    qk_gain = jnp.clip(1.0 + 0.18 * jax.random.normal(seeds[6], (2, D), jnp.float32), 0.1, 1.9)
    mlp_gain = jnp.clip(1.0 + 0.18 * jax.random.normal(seeds[7], (D,), jnp.float32), 0.1, 1.9)
    w_qkv = normal_values(seeds[8], (D, HEADS, 3, HEAD), D ** -0.5, 0.125, ((0, 4), (1, 8)))
    w_out = normal_values(seeds[9], (HEADS, HEAD, D), (max(1, D // 512)) ** -0.5, 3.0, ((0, 8), (2, 4)))
    a_qkv = normal_values(seeds[10], (3, D, AR), D ** -0.5, 0.125, ((1, 8),))
    b_out = normal_values(seeds[11], (AR, D), (AR // 4) ** -0.5, 1.0, ((1, 8),))
    head_pack = normal_values(seeds[12], (HEADS, 4, AR, HEAD), RANK ** -0.5, 1.5, ((0, 8),))
    router = normal_values(seeds[13], (D, EXPERTS), (4 * D) ** -0.5, 0.0625)
    w_gate_up = normal_values(seeds[14], (EXPERTS, D, 2, FF), D ** -0.5, 0.125, ((0, 8), (1, 4)))
    w_down = normal_values(seeds[15], (EXPERTS, D, FF), (max(1, FF // 64)) ** -0.5, 1.5, ((0, 8), (1, 4)))
    exp_wide = normal_values(seeds[16], (EXPERTS, D, 3, AR), D ** -0.5, 0.125, ((0, 8), (1, 4)))
    exp_hidden = normal_values(seeds[17], (EXPERTS, FF, 3, AR), RANK ** -0.5, 1.5, ((0, 8), (1, 4)))
    return {"block_input": block_input, "out_grad": out_grad, "routes": routes, "adapter_ids": adapter_ids, "piece_starts": piece_starts, "attn_gain": attn_gain, "qk_gain": qk_gain, "mlp_gain": mlp_gain, "w_qkv": w_qkv, "w_out": w_out, "a_qkv": a_qkv, "b_out": b_out, "head_pack": head_pack, "router": router, "w_gate_up": w_gate_up, "w_down": w_down, "exp_wide": exp_wide, "exp_hidden": exp_hidden}


norm_eps = 1e-05
rope_theta = 10000.0
rank_scale = 0.5
down_scale = 4.0
highest = lax.Precision.HIGHEST

@jax.custom_vjp
def low(v):
    return lax.optimization_barrier(v.astype(jnp.bfloat16)).astype(jnp.float32)

@jax.custom_vjp
def low_back(v):
    return v

def low_keep(v):
    return (low(v), None)

def low_pass(kept, grad):
    return (grad,)

def back_keep(v):
    return (v, None)

def back_low(kept, grad):
    return (low(grad),)
low.defvjp(low_keep, low_pass)
low_back.defvjp(back_keep, back_low)

def rms_scale(values):
    return lax.rsqrt(lax.optimization_barrier(jnp.mean(values * values, axis=-1, keepdims=True)) + norm_eps)

def rope_tables(length, width):
    half_width = width // 2
    frequency = rope_theta ** (-2.0 * jnp.arange(half_width, dtype=jnp.float32) / width)
    angles = jnp.arange(length, dtype=jnp.float32)[:, None] * frequency[None, :]
    return (jnp.cos(angles), jnp.sin(angles))

def apply_rotary(values, cosine, sine):
    half_width = values.shape[-1] // 2
    first = values[..., :half_width]
    second = values[..., half_width:]
    return jnp.concatenate([first * cosine - second * sine, second * cosine + first * sine], axis=-1)

def allowed_mask(piece_starts):
    places = jnp.arange(SEQ, dtype=jnp.int32)
    causal = places[None, :] <= places[:, None]
    inside = (places[None, None, :] >= piece_starts[:, :, None]) & (places[None, None, :] < piece_starts[:, :, None] + PIECE)
    same_piece = jnp.any(inside[:, :, :, None] & inside[:, :, None, :], axis=1)
    return causal[None] | same_piece

def attend(pieces):
    queries, key_rows, value_rows, allowed = pieces
    scores = low_back(jnp.einsum('qhe,khe->hqk', queries, key_rows, precision=highest) * HEAD ** (-0.5))
    scores = jnp.where(allowed[None], scores, -1e+30)
    row_peak = lax.optimization_barrier(jnp.max(scores, axis=-1, keepdims=True))
    raised = jnp.exp(scores - row_peak)
    weights = raised / lax.optimization_barrier(jnp.sum(raised, axis=-1, keepdims=True))
    return jnp.einsum('hqk,khe->qhe', low(weights), value_rows, precision=highest)

def expert_term(expert_in, route_probs, rank_mask, stacked):
    gate_up, down_w, wide, hidden, slot_rows, valid, expert = stacked
    rows_in = expert_in[slot_rows]
    masks_in = rank_mask[slot_rows]
    gates = route_probs[slot_rows, expert] * valid
    rank_gu = low_back(jnp.einsum('sd,dcr->scr', rows_in, wide[:, :2], precision=highest))
    pre_gu = jnp.einsum('sd,dcf->scf', rows_in, gate_up, precision=highest)
    pre_gu = low_back(pre_gu + rank_scale * jnp.einsum('scr,fcr->scf', low(rank_gu * masks_in[:, None, :]), hidden[:, :2], precision=highest))
    gate_pre = pre_gu[:, 0]
    inner = low(gate_pre * jax.nn.sigmoid(gate_pre) * pre_gu[:, 1])
    rank_down = low_back(jnp.einsum('sf,fr->sr', inner, hidden[:, 2], precision=highest))
    outputs = jnp.einsum('sf,df->sd', inner, down_w, precision=highest) + down_scale * jnp.einsum('sr,dr->sd', low(rank_down * masks_in), wide[:, 2], precision=highest)
    outputs = low_back(outputs)
    return jnp.zeros((TOKENS, D), jnp.float32).at[slot_rows].add(gates[:, None] * outputs)

def reference(block_input, out_grad, routes, adapter_ids, piece_starts, attn_gain, qk_gain, mlp_gain, w_qkv, w_out, a_qkv, b_out, head_pack, router, w_gate_up, w_down, exp_wide, exp_hidden):
    token_adapter = jnp.repeat(adapter_ids, SEQ, total_repeat_length=TOKENS)
    rank_mask = (token_adapter[:, None] == jnp.arange(ADAPTERS * RANK, dtype=jnp.int32)[None, :] // RANK).astype(jnp.float32)
    allowed = allowed_mask(piece_starts)
    cosine, sine = rope_tables(SEQ, HEAD)
    cosine = cosine[None, :, None, :]
    sine = sine[None, :, None, :]
    hits = jnp.any(routes[:, :, None] == jnp.arange(EXPERTS, dtype=jnp.int32)[None, None, :], axis=1)
    hit_int = hits.astype(jnp.int32)
    total_slots = N_GX * CAP
    places = jnp.cumsum(hit_int, axis=0) - 1
    slot_at = jnp.where(hits, places, total_slots)
    token_ids = jnp.broadcast_to(jnp.arange(TOKENS, dtype=jnp.int32)[:, None], (TOKENS, EXPERTS))
    slot_rows = jnp.zeros((EXPERTS, total_slots), jnp.int32).at[jnp.arange(EXPERTS, dtype=jnp.int32)[None, :], slot_at].set(token_ids, mode='drop')
    valid = (jnp.arange(total_slots, dtype=jnp.int32)[None, :] < lax.optimization_barrier(jnp.sum(hit_int, axis=0))[:, None]).astype(jnp.float32)
    first_norm_gain = attn_gain.astype(jnp.float32)
    gains_qk = qk_gain.astype(jnp.float32)
    gain_two = mlp_gain.astype(jnp.float32)
    qkv_float = w_qkv.astype(jnp.float32)
    out_float = w_out.astype(jnp.float32)
    router_float = router.astype(jnp.float32)
    gate_up_float = w_gate_up.astype(jnp.float32)
    down_float = w_down.astype(jnp.float32)

    def forward(inputs, a_adapt, b_adapt, head_adapt, wide_all, hidden_all):
        normed_one = low(inputs * rms_scale(inputs) * first_norm_gain)
        base = low_back(jnp.einsum('td,dhce->thce', normed_one, qkv_float, precision=highest))
        rank_in = low_back(jnp.einsum('td,cdr->tcr', normed_one, a_adapt, precision=highest))
        projected = base + rank_scale * jnp.einsum('tcr,hcre->thce', low(rank_in * rank_mask[:, None, :]), head_adapt[:, :3], precision=highest)
        query_pre = projected[:, :, 0].reshape(TOKENS, D)
        key_pre = projected[:, :, 1].reshape(TOKENS, D)
        query_norm = (query_pre * rms_scale(query_pre) * gains_qk[0]).reshape(NSEQ, SEQ, HEADS, HEAD)
        key_norm = (key_pre * rms_scale(key_pre) * gains_qk[1]).reshape(NSEQ, SEQ, HEADS, HEAD)
        queries = low(apply_rotary(query_norm, cosine, sine))
        key_rows = low(apply_rotary(key_norm, cosine, sine))
        value_rows = low(projected[:, :, 2]).reshape(NSEQ, SEQ, HEADS, HEAD)
        attended = lax.map(jax.checkpoint(attend), (queries, key_rows, value_rows, allowed)).reshape(TOKENS, HEADS, HEAD)
        attn_low = low(low_back(attended))
        rank_out = low_back(jnp.einsum('the,hre->thr', attn_low, head_adapt[:, 3], precision=highest))
        branch = jnp.einsum('the,hed->td', attn_low, out_float, precision=highest) + rank_scale * jnp.einsum('thr,rd->td', low(rank_out * rank_mask[:, None, :]), b_adapt, precision=highest)
        middle = inputs + low_back(branch)
        middle_low = low(middle)
        expert_in = low(middle_low * rms_scale(middle_low) * gain_two)
        logits = jnp.dot(expert_in, router_float, precision=highest)
        logit_peak = lax.optimization_barrier(jnp.max(logits, axis=-1, keepdims=True))
        raised = jnp.exp(logits - logit_peak)
        route_probs = raised / lax.optimization_barrier(jnp.sum(raised, axis=-1, keepdims=True))

        def expert_step(total, stacked):
            return (total + jax.checkpoint(expert_term)(expert_in, route_probs, rank_mask, stacked), None)
        moe_total, unused = lax.scan(expert_step, jnp.zeros((TOKENS, D), jnp.float32), (gate_up_float, down_float, wide_all, hidden_all, slot_rows, valid, jnp.arange(EXPERTS, dtype=jnp.int32)))
        return middle + moe_total
    layer_float, pullback = jax.vjp(forward, block_input.astype(jnp.float32), a_qkv.astype(jnp.float32), b_out.astype(jnp.float32), head_pack.astype(jnp.float32), exp_wide.astype(jnp.float32), exp_hidden.astype(jnp.float32))
    grads = pullback(out_grad.astype(jnp.float32))
    return (layer_float.astype(jnp.bfloat16), grads[0], grads[1], grads[2], grads[3], grads[4], grads[5])
```

```python
import jax
import jax.numpy as jnp
from jax import lax
from jax.sharding import PartitionSpec as P

RANK = 16
SEQ = 1024
PIECE = 256
CAP = 288


norm_eps = 1e-05
rope_theta = 10000.0
rank_scale = 0.5
down_scale = 4.0
bf16 = jnp.bfloat16
f32 = jnp.float32


def rope_tables(length, width):
    half_width = width // 2
    frequency = rope_theta ** (-2.0 * jnp.arange(half_width, dtype=f32) / width)
    angles = jnp.arange(length, dtype=f32)[:, None] * frequency[None, :]
    return (jnp.cos(angles), jnp.sin(angles))


def apply_rotary(values, cosine, sine):
    half_width = values.shape[-1] // 2
    first = values[..., :half_width]
    second = values[..., half_width:]
    return jnp.concatenate(
        [first * cosine - second * sine, second * cosine + first * sine], axis=-1
    )


def unrotate(grads, cosine, sine):
    half_width = grads.shape[-1] // 2
    first = grads[..., :half_width]
    second = grads[..., half_width:]
    return jnp.concatenate(
        [first * cosine + second * sine, second * cosine - first * sine], axis=-1
    )


def allowed_mask(piece_starts):
    places = jnp.arange(SEQ, dtype=jnp.int32)
    causal = places[None, :] <= places[:, None]
    inside = (places[None, None, :] >= piece_starts[:, :, None]) & (
        places[None, None, :] < piece_starts[:, :, None] + PIECE
    )
    same_piece = jnp.any(inside[:, :, :, None] & inside[:, :, None, :], axis=1)
    return causal[None] | same_piece


def dot(spec, left, right):
    return jnp.einsum(spec, left, right, preferred_element_type=f32)


def after(first, *later):
    return lax.optimization_barrier((first,) + later)[1:]


def shards(
    block_input,
    out_grad,
    routes,
    adapter_ids,
    piece_starts,
    attn_gain,
    qk_gain,
    mlp_gain,
    w_qkv,
    w_out,
    a_qkv,
    b_out,
    head_pack,
    router,
    w_gate_up,
    w_down,
    exp_wide,
    exp_hidden,
):
    planes = lax.axis_size("gx")
    groups = lax.axis_size("gy")
    plane = lax.axis_index("gx")
    column = lax.axis_index("gy")
    rows, width_local = block_input.shape
    width = width_local * groups
    heads_local = head_pack.shape[0]
    rank_cols = head_pack.shape[2]
    head_width = head_pack.shape[3]
    experts_local = w_gate_up.shape[0]
    hidden_width = w_gate_up.shape[3]
    nseq = adapter_ids.shape[0]
    inv_root = head_width ** (-0.5)
    repeats = planes // experts_local
    sets = None
    if repeats > 1:
        sets = [[r * experts_local + k for k in range(experts_local)] for r in range(repeats)]
    own = lax.rem(plane, experts_local)

    def over_planes(x):
        return lax.all_gather(x, "gx", axis=0, tiled=False, axis_index_groups=sets)

    def sum_planes(x):
        parts = lax.all_to_all(x, "gx", 0, 0, tiled=True, axis_index_groups=sets)
        return jnp.sum(parts.astype(f32), axis=0)

    def own_expert(x):
        if repeats > 1:
            x = jnp.tile(x, (repeats, 1, 1))
        x = lax.all_to_all(x, "gx", 0, 0, tiled=True)
        return x.reshape((x.shape[0] * x.shape[1], x.shape[2]))

    def spread_grad(x):
        parts = lax.all_to_all(
            x.reshape(planes, x.shape[0] // planes, x.shape[1]), "gx", 0, 0, tiled=True
        )
        parts = parts.reshape((repeats, experts_local) + parts.shape[1:])
        return jnp.sum(parts.astype(f32), axis=0)

    compact = nseq * RANK

    def pick(x, axis):
        return jnp.concatenate(
            [
                lax.dynamic_slice_in_dim(x, adapter_ids[n] * RANK, RANK, axis=axis)
                for n in range(nseq)
            ],
            axis=axis,
        )

    token_seq = jnp.arange(rows, dtype=jnp.int32) // SEQ
    col_seq = jnp.arange(compact, dtype=jnp.int32) // RANK
    compact_mask = (token_seq[:, None] == col_seq[None, :]).astype(f32)
    a_pick = pick(a_qkv, 2)
    b_pick = pick(b_out, 0)
    pack_pick = pick(head_pack, 2)

    gathered = lax.all_gather(
        jnp.concatenate(
            [block_input, a_pick.transpose(0, 2, 1).reshape(3 * compact, width_local), b_pick],
            axis=0,
        ),
        "gy",
        axis=1,
        tiled=True,
    )
    full_rows = gathered[:rows]
    a_full = gathered[rows : rows + 3 * compact]
    b_full = gathered[rows + 3 * compact :]
    qkv_weight = lax.all_gather(w_qkv, "gx", axis=0, tiled=True)
    (w_out_later,) = after(qkv_weight, w_out)
    out_weight = lax.all_gather(w_out_later, "gx", axis=2, tiled=True)
    routes_all = over_planes(routes)
    adapters_all = lax.all_gather(adapter_ids, "gx", axis=0, tiled=False)

    out_grad_later, gate_up_later, wide_later, down_later, hidden_later = after(
        out_weight, out_grad, w_gate_up, exp_wide, w_down, exp_hidden
    )
    grad_planes = over_planes(out_grad_later)
    dl = w_gate_up.shape[1]
    wide_flat = exp_wide.reshape(experts_local, dl, 3 * rank_cols)
    first_shard = jnp.concatenate(
        [w_gate_up.reshape(experts_local, dl, 2 * hidden_width), wide_flat[:, :, : 2 * rank_cols]],
        axis=2,
    )
    second_shard = jnp.concatenate([w_down, wide_flat[:, :, 2 * rank_cols :]], axis=2)
    hidden_shard = exp_hidden.reshape(experts_local, exp_hidden.shape[1], 3 * rank_cols)
    (first_shard,) = after(grad_planes, first_shard)
    first_weight = own_expert(first_shard)
    second_shard, hidden_shard = after(first_weight, second_shard, hidden_shard)
    hidden_weight = own_expert(hidden_shard)
    second_weight = own_expert(second_shard)

    expert_ids = own + experts_local * jnp.arange(groups, dtype=jnp.int32)
    hits = jnp.any(routes_all[:, :, :, None] == expert_ids, axis=2)
    order = jnp.arange(rows, dtype=jnp.int32)
    earlier = (order[None, :] < order[:, None]).astype(bf16)
    places = dot("ts,gsc->gct", earlier, hits.astype(bf16))
    slot_key = jnp.where(hits.transpose(0, 2, 1), places.astype(jnp.int32), -1)
    slots = jnp.arange(CAP, dtype=jnp.int32)
    slot_pick = (slot_key[:, :, None, :] == slots[None, None, :, None]).astype(bf16)
    own_key = lax.dynamic_index_in_dim(slot_key, column, 1, keepdims=False)
    own_pick = (own_key[:, None, :] == slots[None, :, None]).astype(bf16)
    set_start = (plane // experts_local) * experts_local
    set_adapters = lax.dynamic_slice_in_dim(adapters_all, set_start, experts_local, axis=0)
    token_adapter = jnp.repeat(set_adapters, SEQ, axis=1, total_repeat_length=rows)
    rank_mask = (
        token_adapter[:, :, None] == jnp.arange(rank_cols, dtype=jnp.int32)[None, None, :] // RANK
    ).astype(bf16)
    slot_total = experts_local * CAP
    mask_slot = dot("gst,gtr->gsr", own_pick, rank_mask).reshape(slot_total, rank_cols)
    valid = jnp.max(mask_slot, axis=1)

    def to_experts(x):
        picked = dot("gcst,gtd->cgsd", slot_pick, x).astype(bf16)
        sent = lax.all_to_all(
            picked.reshape(groups, slot_total, width_local), "gy", 0, 0, tiled=True
        )
        return sent.transpose(1, 0, 2).reshape(slot_total, width)

    def from_experts(x):
        sent = x.astype(bf16).reshape(slot_total, groups, width_local).transpose(1, 0, 2)
        sent = lax.all_to_all(sent, "gy", 0, 0, tiled=True)
        placed = dot(
            "gcst,cgsd->gtd", slot_pick, sent.reshape(groups, experts_local, CAP, width_local)
        )
        return sum_planes(placed.astype(bf16))

    grad_slot = to_experts(grad_planes)

    col_start = column * width_local
    first_norm_gain = lax.dynamic_slice_in_dim(attn_gain, col_start, width_local)
    input_f = full_rows.astype(f32)
    scale_one = lax.rsqrt(jnp.mean(input_f * input_f, axis=-1, keepdims=True) + norm_eps)
    hat_one = input_f * scale_one
    normed_bf = (hat_one * attn_gain).astype(bf16)
    base = dot("td,dhce->thce", normed_bf, qkv_weight)
    rank_in = dot("td,kd->tk", normed_bf, a_full).reshape(rows, 3, compact)
    rank_low = (rank_in * compact_mask[:, None, :]).astype(bf16)
    projected = base + rank_scale * dot("tcr,hcre->thce", rank_low, pack_pick[:, :3])
    query_pre = projected[:, :, 0]
    key_pre = projected[:, :, 1]
    value_bf = projected[:, :, 2].astype(bf16)
    square_sums = lax.psum(
        jnp.stack(
            [
                jnp.sum(query_pre * query_pre, axis=(1, 2)),
                jnp.sum(key_pre * key_pre, axis=(1, 2)),
            ]
        ),
        "gy",
    )
    query_scale = lax.rsqrt(square_sums[0] / width + norm_eps)[:, None, None]
    key_scale = lax.rsqrt(square_sums[1] / width + norm_eps)[:, None, None]
    head_start = column * heads_local * head_width
    gains_local = lax.dynamic_slice_in_dim(
        qk_gain, head_start, heads_local * head_width, axis=1
    ).reshape(2, heads_local, head_width)
    query_hat = query_pre * query_scale
    key_hat = key_pre * key_scale
    cosine, sine = rope_tables(SEQ, head_width)
    cosine = cosine[None, :, None, :]
    sine = sine[None, :, None, :]
    query_bf = apply_rotary(
        (query_hat * gains_local[0]).reshape(nseq, SEQ, heads_local, head_width), cosine, sine
    ).astype(bf16)
    key_bf = apply_rotary(
        (key_hat * gains_local[1]).reshape(nseq, SEQ, heads_local, head_width), cosine, sine
    ).astype(bf16)
    values_seq = value_bf.reshape(nseq, SEQ, heads_local, head_width)
    allowed = allowed_mask(piece_starts)[:, None]
    scores = dot("nqhe,nkhe->nhqk", query_bf, key_bf) * inv_root
    scores = jnp.where(allowed, scores, -1e30)
    row_peak = jnp.max(scores, axis=-1, keepdims=True)
    raised = jnp.exp(scores - row_peak)
    row_total = jnp.sum(raised, axis=-1, keepdims=True)
    log_total = row_peak + jnp.log(row_total)
    weights = raised / row_total
    attended = dot("nhqk,nkhe->nqhe", weights.astype(bf16), values_seq)
    attn_bf = attended.reshape(rows, heads_local, head_width).astype(bf16)
    rank_out = dot("the,hre->thr", attn_bf, pack_pick[:, 3])
    rank_out_low = (rank_out * compact_mask[:, None, :]).astype(bf16)
    out_terms = dot("the,hed->td", attn_bf, out_weight) + rank_scale * dot(
        "thr,rd->td", rank_out_low, b_full
    )
    branch = lax.psum_scatter(out_terms.astype(bf16), "gy", scatter_dimension=1, tiled=True)
    middle = block_input.astype(f32) + branch.astype(f32)
    middle_low = middle.astype(bf16)

    middle_slot = to_experts(over_planes(middle_low)).astype(f32)
    slot_scale = lax.rsqrt(jnp.mean(middle_slot * middle_slot, axis=-1, keepdims=True) + norm_eps)
    expert_in = (middle_slot * slot_scale * mlp_gain).astype(bf16)
    logits = jnp.dot(expert_in, router, preferred_element_type=f32)
    logit_raised = jnp.exp(logits - jnp.max(logits, axis=-1, keepdims=True))
    route_probs = logit_raised / jnp.sum(logit_raised, axis=-1, keepdims=True)
    own_id = column * experts_local + own
    is_own = (jnp.arange(router.shape[1], dtype=jnp.int32) == own_id).astype(f32)[None, :]
    gate = jnp.sum(route_probs * is_own, axis=1, keepdims=True) * valid[:, None]
    two_masks = jnp.concatenate([mask_slot, mask_slot], axis=1)
    pre_wide = jnp.dot(expert_in, first_weight, preferred_element_type=f32)
    rank_gu_low = (pre_wide[:, 2 * hidden_width :] * two_masks).astype(bf16)
    hidden_gate = hidden_weight[:, :rank_cols]
    hidden_up = hidden_weight[:, rank_cols : 2 * rank_cols]
    hidden_down = hidden_weight[:, 2 * rank_cols :]
    gate_pre = pre_wide[:, :hidden_width] + rank_scale * dot(
        "sr,fr->sf", rank_gu_low[:, :rank_cols], hidden_gate
    )
    up_pre = pre_wide[:, hidden_width : 2 * hidden_width] + rank_scale * dot(
        "sr,fr->sf", rank_gu_low[:, rank_cols:], hidden_up
    )
    sigma = jax.nn.sigmoid(gate_pre)
    activated = gate_pre * sigma
    inner_bf = (activated * up_pre).astype(bf16)
    rank_down = dot("sf,fr->sr", inner_bf, hidden_down)
    rank_down_low = (rank_down * mask_slot).astype(bf16)
    inner_wide = jnp.concatenate([inner_bf, (down_scale * rank_down_low).astype(bf16)], axis=1)
    expert_output = dot("sf,df->sd", inner_wide, second_weight)
    moe_part = from_experts(gate * expert_output)
    layer_out = (middle + moe_part).astype(bf16)

    grad_slot_f = grad_slot.astype(f32)
    gate_grad = jnp.sum(grad_slot_f * expert_output, axis=-1, keepdims=True)
    out_grad_bf = (gate * grad_slot_f).astype(bf16)
    inner_wide_grad = dot("sd,df->sf", out_grad_bf, second_weight)
    rank_down_grad = (down_scale * inner_wide_grad[:, hidden_width:] * mask_slot).astype(bf16)
    inner_grad = inner_wide_grad[:, :hidden_width] + dot("sr,fr->sf", rank_down_grad, hidden_down)
    gate_pre_grad = (inner_grad * up_pre * sigma * (1.0 + gate_pre * (1.0 - sigma))).astype(bf16)
    up_pre_grad = (inner_grad * activated).astype(bf16)
    rank_gu_grad = (
        rank_scale
        * jnp.concatenate(
            [
                dot("sf,fr->sr", gate_pre_grad, hidden_gate),
                dot("sf,fr->sr", up_pre_grad, hidden_up),
            ],
            axis=1,
        )
        * two_masks
    ).astype(bf16)
    logit_grad = (is_own - route_probs) * (gate * gate_grad)
    logit_high = logit_grad.astype(bf16)
    logit_rest = (logit_grad - logit_high.astype(f32)).astype(bf16)
    pre_wide_grad = jnp.concatenate([gate_pre_grad, up_pre_grad, rank_gu_grad], axis=1)
    rows_grad = dot("sf,df->sd", pre_wide_grad, first_weight) + dot(
        "se,de->sd",
        jnp.concatenate([logit_high, logit_rest], axis=1),
        jnp.concatenate([router, router], axis=1),
    )
    normed_two_part = from_experts(rows_grad)

    wide_grad = jnp.concatenate(
        [
            dot("sd,sr->dr", expert_in, rank_gu_grad),
            down_scale * dot("sd,sr->dr", out_grad_bf, rank_down_low),
        ],
        axis=1,
    )
    hidden_grad = jnp.concatenate(
        [
            rank_scale * dot("sf,sr->fr", gate_pre_grad, rank_gu_low[:, :rank_cols]),
            rank_scale * dot("sf,sr->fr", up_pre_grad, rank_gu_low[:, rank_cols:]),
            dot("sf,sr->fr", inner_bf, rank_down_grad),
        ],
        axis=1,
    )
    wide_sum = spread_grad(wide_grad.astype(bf16)).reshape(exp_wide.shape)
    hidden_sum = spread_grad(hidden_grad.astype(bf16)).reshape(exp_hidden.shape)

    middle_rows = lax.all_gather(middle_low, "gy", axis=1, tiled=True).astype(f32)
    grad_rows = lax.all_gather(out_grad, "gy", axis=1, tiled=True).astype(f32)
    scale_two = lax.rsqrt(jnp.mean(middle_rows * middle_rows, axis=-1, keepdims=True) + norm_eps)
    normed_two_grad = lax.all_gather(
        normed_two_part.astype(bf16), "gy", axis=1, tiled=True
    ).astype(f32)
    hat_two = middle_rows * scale_two
    scaled_two = normed_two_grad * mlp_gain
    stat_two = jnp.mean(scaled_two * hat_two, axis=-1, keepdims=True)
    branch_rows = (grad_rows + scale_two * (scaled_two - hat_two * stat_two)).astype(bf16)
    gain_two_local = lax.dynamic_slice_in_dim(mlp_gain, col_start, width_local)
    middle_grad = out_grad.astype(f32) + scale_two * (
        normed_two_part * gain_two_local - middle_low.astype(f32) * scale_two * stat_two
    )
    rank_out_grad = rank_scale * dot("td,rd->tr", branch_rows, b_full)
    rank_out_bf = (rank_out_grad * compact_mask).astype(bf16)
    b_out_part = rank_scale * dot("thr,td->rd", rank_out_low, branch_rows)
    pack_out_grad = dot("the,tr->hre", attn_bf, rank_out_bf)
    attention_gradient = dot("td,hed->the", branch_rows, out_weight) + dot(
        "tr,hre->the", rank_out_bf, pack_pick[:, 3]
    )
    attn_grad_bf = attention_gradient.reshape(nseq, SEQ, heads_local, head_width).astype(bf16)
    scores_again = dot("nqhe,nkhe->nhqk", query_bf, key_bf) * inv_root
    scores_again = jnp.where(allowed, scores_again, -1e30)
    weights_again = jnp.exp(scores_again - log_total)
    value_grad = dot("nhqk,nqhe->nkhe", weights_again.astype(bf16), attn_grad_bf)
    weight_grad = dot("nqhe,nkhe->nhqk", attn_grad_bf, values_seq)
    row_dot = jnp.sum(weight_grad * weights_again, axis=-1, keepdims=True)
    score_grad = (weights_again * (weight_grad - row_dot)).astype(bf16)
    query_grad = dot("nhqk,nkhe->nqhe", score_grad, key_bf) * inv_root
    key_grad = dot("nhqk,nqhe->nkhe", score_grad, query_bf) * inv_root
    query_hat_grad = (
        unrotate(query_grad, cosine, sine).reshape(rows, heads_local, head_width) * gains_local[0]
    )
    key_hat_grad = (
        unrotate(key_grad, cosine, sine).reshape(rows, heads_local, head_width) * gains_local[1]
    )
    value_pre_grad = value_grad.reshape(rows, heads_local, head_width)
    stat_query = jnp.sum(query_hat_grad * query_hat, axis=(1, 2))
    stat_key = jnp.sum(key_hat_grad * key_hat, axis=(1, 2))

    def rank_terms(values, which):
        return dot("the,hre->rt", values.astype(bf16), pack_pick[:, which])

    sums = jnp.concatenate(
        [
            rank_terms(query_hat_grad, 0),
            rank_terms(key_hat_grad, 1),
            rank_terms(value_pre_grad, 2),
            rank_terms(query_hat, 0),
            rank_terms(key_hat, 1),
            jnp.stack([stat_query, stat_key]),
        ],
        axis=0,
    )
    sums = lax.psum(sums, "gy")
    first_total = sums[: 3 * compact].reshape(3, compact, rows)
    second_total = sums[3 * compact : 5 * compact].reshape(2, compact, rows)
    mean_qk = sums[5 * compact :] / width
    scales_qk = jnp.stack([query_scale[:, 0, 0], key_scale[:, 0, 0]])
    rank_qk = scales_qk[:, None, :] * (first_total[:2] - second_total * mean_qk[:, None, :])
    rank_grad_full = rank_scale * jnp.concatenate([rank_qk, first_total[2:]], axis=0)
    rank_grad_bf = (rank_grad_full * compact_mask.T[None]).astype(bf16)
    query_pre_grad = query_scale * (query_hat_grad - query_hat * mean_qk[0][:, None, None])
    key_pre_grad = key_scale * (key_hat_grad - key_hat * mean_qk[1][:, None, None])
    pre_grad = jnp.stack([query_pre_grad, key_pre_grad, value_pre_grad], axis=2).astype(bf16)
    pack_b_grad = rank_scale * dot("tcr,thce->rhce", rank_low, pre_grad)
    normed_one_grad = dot("thce,dhce->td", pre_grad, qkv_weight)
    adapter_input_gradient = dot("crt,cdr->td", rank_grad_bf, a_pick)
    first_normalized_shard = lax.dynamic_slice_in_dim(hat_one, col_start, width_local, axis=1)
    normed_local_bf = lax.dynamic_slice_in_dim(normed_bf, col_start, width_local, axis=1)
    a_rows_grad = dot("td,crt->rcd", normed_local_bf, rank_grad_bf)
    stat_one = jnp.sum(normed_one_grad * attn_gain * hat_one, axis=-1) + jnp.sum(
        adapter_input_gradient * first_norm_gain * first_normalized_shard, axis=-1
    )
    stat_rows = stat_one.reshape(rows // width_local, width_local)
    stat_high = stat_rows.astype(bf16)
    stat_low = (stat_rows - stat_high.astype(f32)).astype(bf16)
    summed = lax.psum_scatter(
        jnp.concatenate(
            [
                normed_one_grad.astype(bf16),
                b_out_part.astype(bf16),
                jnp.tile(jnp.concatenate([stat_high, stat_low]), (1, groups)),
            ],
            axis=0,
        ),
        "gy",
        scatter_dimension=1,
        tiled=True,
    ).astype(f32)
    first_portion = summed[:rows]
    b_out_sum = summed[rows : rows + compact]
    stat_sum = summed[rows + compact :].reshape(2, rows)
    stat_one_sum = (stat_sum[0] + stat_sum[1])[:, None]
    normalized_shard_rows = first_portion + adapter_input_gradient
    input_grad = middle_grad + scale_one * (
        normalized_shard_rows * first_norm_gain - first_normalized_shard * stat_one_sum / width
    )

    pack_grad = jnp.concatenate(
        [
            pack_b_grad.transpose(1, 2, 0, 3),
            pack_out_grad[:, None],
        ],
        axis=1,
    )
    small = jnp.concatenate(
        [
            a_rows_grad.reshape(compact, 3 * width_local),
            b_out_sum,
            pack_grad.transpose(2, 0, 1, 3).reshape(compact, heads_local * 4 * head_width),
        ],
        axis=1,
    )
    small_all = lax.all_gather(small, "gx", axis=0, tiled=True)
    row_at = (
        adapters_all[:, :, None] * RANK + jnp.arange(RANK, dtype=jnp.int32)[None, None, :]
    ).reshape(-1)
    put = (jnp.arange(rank_cols, dtype=jnp.int32)[:, None] == row_at[None, :]).astype(f32)
    small_sum = jnp.dot(put, small_all, precision=lax.Precision.HIGHEST)
    a_end = 3 * width_local
    b_end = a_end + width_local
    a_sum = small_sum[:, :a_end].reshape(rank_cols, 3, width_local).transpose(1, 2, 0)
    b_sum = small_sum[:, a_end:b_end]
    head_sum = small_sum[:, b_end:].reshape(rank_cols, heads_local, 4, head_width)
    head_sum = head_sum.transpose(1, 2, 0, 3)
    return (layer_out, input_grad, a_sum, b_sum, head_sum, wide_sum, hidden_sum)


def solution(mesh):
    return jax.shard_map(
        shards,
        mesh=mesh,
        in_specs=(
            P("gx", "gy"),
            P("gx", "gy"),
            P("gx", None),
            P("gx"),
            P("gx", None),
            P(),
            P(),
            P(),
            P("gx", "gy", None, None),
            P("gy", None, "gx"),
            P(None, "gy", None),
            P(None, "gy"),
            P("gy", None, None, None),
            P(),
            P("gy", "gx", None, None),
            P("gy", "gx", None),
            P("gy", "gx", None, None),
            P("gy", "gx", None, None),
        ),
        out_specs=(
            P("gx", "gy"),
            P("gx", "gy"),
            P(None, "gy", None),
            P(None, "gy"),
            P("gy", None, None, None),
            P("gy", "gx", None, None),
            P("gy", "gx", None, None),
        ),
        check_vma=False,
    )
```

```python
import functools
import jax
import jax.numpy as jnp
from jax import lax
from jax.experimental import pallas as pl
from jax.experimental.pallas import tpu as pltpu
from jax.sharding import PartitionSpec as P

RANK = 16
SEQ = 1024
PIECE = 256
CAP = 288
DOWN_PARTS = 2


norm_eps = 1e-05
rope_theta = 10000.0
rank_scale = 0.5
down_scale = 4.0
bf16 = jnp.bfloat16
f32 = jnp.float32
VMEM = pl.BlockSpec(memory_space=pltpu.VMEM)
DMA = pltpu.SemaphoreType.DMA
MESH = pl.DeviceIdType.MESH
SMALL = pl.CostEstimate(flops=0, bytes_accessed=1 << 16, transcendentals=0)
CAP = 288
DOWN_PARTS = 2
SMALL = pl.CostEstimate(flops=0, bytes_accessed=1 << 16, transcendentals=0)


def place_in_column():
    me = lax.axis_index("gy")
    chip, core = lax.div(me, 2), lax.rem(me, 2)
    return me, chip, core, me + 1 - 2 * core


def chip_peer(chip, core, step, chips):
    return lax.rem(chip + step, chips) * 2 + core


def greet_chips(chip, core, sibling, chips):
    barrier = pltpu.get_barrier_semaphore()
    pl.semaphore_signal(barrier, inc=1, device_id={"gy": sibling}, device_id_type=MESH)
    for step in range(1, chips):
        pl.semaphore_signal(
            barrier,
            inc=1,
            device_id={"gy": chip_peer(chip, core, step, chips)},
            device_id_type=MESH,
        )
    pl.semaphore_wait(barrier, chips)


def remote(src, dst, send_sem, recv_sem, target):
    return pltpu.make_async_remote_copy(
        src_ref=src,
        dst_ref=dst,
        send_sem=send_sem,
        recv_sem=recv_sem,
        device_id={"gy": target},
        device_id_type=MESH,
    )


def gather_kernel(chips, x_ref, o_ref, own_sem, send_sem, recv_sem, pass_sem, passed_sem):
    me, chip, core, sibling = place_in_column()
    width = x_ref.shape[1]

    def columns(owner):
        return o_ref.at[:, pl.ds(pl.multiple_of(owner * width, width), width)]

    own = pltpu.make_async_copy(x_ref, columns(me), own_sem)
    own.start()
    greet_chips(chip, core, sibling, chips)
    out = []
    for step in list(range(1, chips)) + [0]:
        target = sibling if step == 0 else chip_peer(chip, core, step, chips)
        copy = remote(x_ref, columns(me), send_sem.at[step], recv_sem.at[step], target)
        copy.start()
        out.append(copy)
    for step in range(1, chips):
        out[step - 1].wait_recv()
        source = chip_peer(chip, core, chips - step, chips)
        copy = remote(
            columns(source), columns(source), pass_sem.at[step], passed_sem.at[step], sibling
        )
        copy.start()
        out.append(copy)
    own.wait()
    out[chips - 1].wait_recv()
    for copy in out[chips:]:
        copy.wait_recv()
    for copy in out:
        copy.wait_send()


def gather_columns(x, groups, collective_id):
    chips = groups // 2
    rows, width = x.shape
    return pl.pallas_call(
        functools.partial(gather_kernel, chips),
        out_shape=jax.ShapeDtypeStruct((rows, groups * width), x.dtype),
        in_specs=[VMEM],
        out_specs=VMEM,
        scratch_shapes=[DMA, DMA((chips,)), DMA((chips,)), DMA((chips,)), DMA((chips,))],
        compiler_params=pltpu.CompilerParams(
            collective_id=collective_id, has_side_effects=True, vmem_limit_bytes=48 << 20
        ),
        cost_estimate=SMALL,
    )(x)


def scatter_kernel(
    chips, tile, l_ref, r_ref, o_ref, part, got, pair, far, part_s, got_s, pair_s, far_s
):
    me, chip, core, sibling = place_in_column()
    rows, width = o_ref.shape
    greet_chips(chip, core, sibling, chips)
    steps = list(range(1, chips)) + [0]

    def product(owner, row):
        chunk = r_ref[pl.ds(pl.multiple_of(owner * width, width), width), :]
        return lax.dot_general(
            l_ref[pl.ds(row, tile), :],
            chunk,
            (((1,), (1,)), ((), ())),
            preferred_element_type=f32,
        )

    copies = []
    for step in steps:
        owner = chip_peer(chip, 1 - core, step, chips)

        @pl.loop(0, rows // tile)
        def _(i, owner=owner, step=step):
            row = pl.multiple_of(i * tile, tile)
            part[step, pl.ds(row, tile), :] = product(owner, row).astype(bf16)

        copy = remote(part.at[step], got.at[step], part_s.at[step], got_s.at[step], sibling)
        copy.start()
        copies.append(copy)
    for step in steps:
        owner = chip_peer(chip, core, step, chips)
        copies[steps.index(step)].wait_recv()

        @pl.loop(0, rows // tile)
        def _(i, owner=owner, step=step):
            row = pl.multiple_of(i * tile, tile)
            total = product(owner, row) + got[step, pl.ds(row, tile), :].astype(f32)
            if step == 0:
                o_ref[pl.ds(row, tile), :] = total
            else:
                pair[step - 1, pl.ds(row, tile), :] = total.astype(bf16)

        if step > 0:
            copy = remote(
                pair.at[step - 1], far.at[step - 1], pair_s.at[step - 1], far_s.at[step - 1], owner
            )
            copy.start()
            copies.append(copy)
    for step in range(1, chips):
        copies[chips + step - 1].wait_recv()

        @pl.loop(0, rows // tile)
        def _(i, step=step):
            row = pl.multiple_of(i * tile, tile)
            o_ref[pl.ds(row, tile), :] += far[step - 1, pl.ds(row, tile), :].astype(f32)

    for copy in copies:
        copy.wait_send()


def scatter_product(left, right, groups, collective_id):
    chips = groups // 2
    rows, inner = left.shape
    width = right.shape[0] // groups
    tile = min(256, rows)
    return pl.pallas_call(
        functools.partial(scatter_kernel, chips, tile),
        out_shape=jax.ShapeDtypeStruct((rows, width), f32),
        in_specs=[VMEM, VMEM],
        out_specs=VMEM,
        scratch_shapes=[
            pltpu.VMEM((chips, rows, width), bf16),
            pltpu.VMEM((chips, rows, width), bf16),
            pltpu.VMEM((chips - 1, rows, width), bf16),
            pltpu.VMEM((chips - 1, rows, width), bf16),
            DMA((chips,)),
            DMA((chips,)),
            DMA((chips - 1,)),
            DMA((chips - 1,)),
        ],
        compiler_params=pltpu.CompilerParams(
            collective_id=collective_id, has_side_effects=True, vmem_limit_bytes=48 << 20
        ),
        cost_estimate=SMALL,
    )(left, right)


def add_kernel(groups, x_ref, o_ref, got, send_sem, recv_sem):
    me = lax.axis_index("gy")
    barrier = pltpu.get_barrier_semaphore()
    for step in range(1, groups):
        target = lax.rem(me + step, groups)
        pl.semaphore_signal(barrier, inc=1, device_id={"gy": target}, device_id_type=MESH)
    pl.semaphore_wait(barrier, groups - 1)
    copies = []
    for step in range(1, groups):
        target = lax.rem(me + step, groups)
        copy = remote(
            x_ref, got.at[step - 1], send_sem.at[step - 1], recv_sem.at[step - 1], target
        )
        copy.start()
        copies.append(copy)
    total = x_ref[...]
    for step in range(1, groups):
        copies[step - 1].wait_recv()
        total = total + got[step - 1]
    o_ref[...] = total
    for copy in copies:
        copy.wait_send()


def add_small(x, groups, collective_id):
    return pl.pallas_call(
        functools.partial(add_kernel, groups),
        out_shape=jax.ShapeDtypeStruct(x.shape, f32),
        in_specs=[VMEM],
        out_specs=VMEM,
        scratch_shapes=[
            pltpu.VMEM((groups - 1,) + x.shape, f32),
            DMA((groups - 1,)),
            DMA((groups - 1,)),
        ],
        compiler_params=pltpu.CompilerParams(collective_id=collective_id, has_side_effects=True),
        cost_estimate=SMALL,
    )(x)


def add_pairs_kernel(
    chips, x_ref, o_ref, got, pair, far, done, got_s, far_s, done_s
):
    me, chip, core, sibling = place_in_column()
    half = x_ref.shape[0] // 2
    greet_chips(chip, core, sibling, chips)
    first = remote(x_ref, got, got_s.at[0], got_s.at[1], sibling)
    first.start()
    first.wait_recv()
    own = pl.ds(pl.multiple_of(core * half, 16), half)
    total = x_ref[own, :].astype(f32) + got[own, :].astype(f32)
    pair[...] = total.astype(bf16)
    copies = []
    for step in range(1, chips):
        copy = remote(
            pair,
            far.at[step - 1],
            far_s.at[0, step - 1],
            far_s.at[1, step - 1],
            chip_peer(chip, core, step, chips),
        )
        copy.start()
        copies.append(copy)
    for step in range(1, chips):
        copies[step - 1].wait_recv()
        total = total + far[step - 1].astype(f32)
    done[own, :] = total.astype(bf16)
    last = remote(done.at[own, :], done.at[own, :], done_s.at[0], done_s.at[1], sibling)
    last.start()
    last.wait_recv()
    o_ref[...] = done[...].astype(f32)
    first.wait_send()
    for copy in copies:
        copy.wait_send()
    last.wait_send()


def add_pairs(x, groups, collective_id):
    chips = groups // 2
    rows, width = x.shape
    return pl.pallas_call(
        functools.partial(add_pairs_kernel, chips),
        out_shape=jax.ShapeDtypeStruct(x.shape, f32),
        in_specs=[VMEM],
        out_specs=VMEM,
        scratch_shapes=[
            pltpu.VMEM(x.shape, bf16),
            pltpu.VMEM((rows // 2, width), bf16),
            pltpu.VMEM((chips - 1, rows // 2, width), bf16),
            pltpu.VMEM(x.shape, bf16),
            DMA((2,)),
            DMA((2, chips - 1)),
            DMA((2,)),
        ],
        compiler_params=pltpu.CompilerParams(collective_id=collective_id, has_side_effects=True),
        cost_estimate=SMALL,
    )(x)


def plane_place(planes_in_set):
    plane = lax.axis_index("gx")
    own = lax.rem(plane, planes_in_set)
    return plane, own, plane - own


def to_plane(src, dst, send_sem, recv_sem, target):
    return pltpu.make_async_remote_copy(
        src_ref=src,
        dst_ref=dst,
        send_sem=send_sem,
        recv_sem=recv_sem,
        device_id={"gx": target},
        device_id_type=MESH,
    )


def greet_all(planes, groups):
    barrier = pltpu.get_barrier_semaphore()
    plane, me = lax.axis_index("gx"), lax.axis_index("gy")

    @pl.loop(1, planes)
    def _(step):
        target = lax.rem(plane + step, planes)
        pl.semaphore_signal(barrier, inc=1, device_id={"gx": target}, device_id_type=MESH)

    @pl.loop(1, groups)
    def _(step):
        target = lax.rem(me + step, groups)
        pl.semaphore_signal(barrier, inc=1, device_id={"gy": target}, device_id_type=MESH)

    pl.semaphore_wait(barrier, planes + groups - 2)


def spread_kernel(
    planes,
    groups,
    in_set,
    x_ref,
    key_ref,
    w_ref,
    o_ref,
    full_ref,
    from_plane,
    picked,
    own_sem,
    w_send,
    w_recv,
    z_send,
    z_recv,
    g_send,
    g_recv,
):
    plane, own, base = plane_place(in_set)
    me = lax.axis_index("gy")
    width = x_ref.shape[1] // 2
    depth, inner = w_ref.shape[1], w_ref.shape[2]
    greet_all(planes, groups)
    z_copies = []
    for step in range(1, in_set):
        copy = to_plane(
            x_ref,
            from_plane.at[step - 1],
            z_send.at[step - 1],
            z_recv.at[step - 1],
            base + lax.rem(own + step, in_set),
        )
        copy.start()
        z_copies.append(copy)
    mine = full_ref.at[pl.ds(pl.multiple_of(plane * depth, depth), depth), pl.ds(0, inner)]
    own_copy = pltpu.make_async_copy(w_ref.at[own], mine, own_sem)
    own_copy.start()
    w_copies = []
    for step in range(1, planes):
        target = lax.rem(plane + step, planes)
        copy = to_plane(
            w_ref.at[lax.rem(target, in_set)],
            mine,
            w_send.at[step - 1],
            w_recv.at[step - 1],
            target,
        )
        copy.start()
        w_copies.append(copy)

    def sent(step, turn):
        target = lax.rem(me + turn, groups)
        return remote(
            picked.at[step, turn],
            o_ref.at[
                :,
                pl.ds(step * CAP, CAP),
                pl.ds(pl.multiple_of(me * width, width), width),
            ],
            g_send.at[step, turn],
            g_recv.at[step, turn],
            target,
        )

    for step in range(in_set):
        if step:
            z_copies[step - 1].wait_recv()
        block = from_plane.at[step - 1] if step else x_ref

        def choose(target):
            key = key_ref[step, pl.ds(target, 1), :]
            slot = lax.broadcasted_iota(jnp.int32, (CAP, key.shape[1]), 0)
            pick = jnp.where(slot == key, 1.0, 0.0).astype(bf16)
            return jnp.dot(pick, block[...], preferred_element_type=f32).astype(bf16)

        @pl.loop(1, groups)
        def _(turn, step=step, choose=choose):
            rows = choose(lax.rem(me + turn, groups))
            picked[step, turn, 0] = rows[:, :width]
            picked[step, turn, 1] = rows[:, width:]
            sent(step, turn).start()

        rows = choose(me)
        columns = pl.ds(pl.multiple_of(me * width, width), width)
        o_ref[0, pl.ds(step * CAP, CAP), columns] = rows[:, :width]
        o_ref[1, pl.ds(step * CAP, CAP), columns] = rows[:, width:]

    for step in range(in_set):

        @pl.loop(1, groups)
        def _(turn, step=step):
            copy = sent(step, turn)
            copy.wait_recv()
            copy.wait_send()

    for copy in z_copies:
        copy.wait_send()
    own_copy.wait()
    for copy in w_copies:
        copy.wait_recv()
        copy.wait_send()


def spread(x, key, weight, planes, groups, pad_to, collective_id):
    in_set, depth, inner = weight.shape
    rows, two = x.shape
    width = two // 2
    return pl.pallas_call(
        functools.partial(spread_kernel, planes, groups, in_set),
        out_shape=(
            jax.ShapeDtypeStruct((2, in_set * CAP, groups * width), bf16),
            jax.ShapeDtypeStruct((planes * depth, pad_to), bf16),
        ),
        in_specs=[VMEM, VMEM, pl.BlockSpec(memory_space=pl.ANY)],
        out_specs=(VMEM, pl.BlockSpec(memory_space=pl.ANY)),
        scratch_shapes=[
            pltpu.VMEM((in_set - 1, rows, two), bf16),
            pltpu.VMEM((in_set, groups, 2, CAP, width), bf16),
            DMA,
            DMA((planes - 1,)),
            DMA((planes - 1,)),
            DMA((in_set - 1,)),
            DMA((in_set - 1,)),
            DMA((in_set, groups)),
            DMA((in_set, groups)),
        ],
        compiler_params=pltpu.CompilerParams(
            collective_id=collective_id, has_side_effects=True, vmem_limit_bytes=48 << 20
        ),
        cost_estimate=SMALL,
    )(x, key, weight)


def collect_kernel(
    planes,
    groups,
    in_set,
    tile,
    u_ref,
    m_ref,
    key_ref,
    shard_ref,
    rows_ref,
    placed_ref,
    got,
    other,
    out_z,
    in_z,
    low,
    g_send,
    g_recv,
    own_sem,
    m_sem,
    z_send,
    z_recv,
    c_own,
    c_send,
    c_recv,
    p_send,
    p_recv,
):
    plane, own, base = plane_place(in_set)
    me, chip, core, sibling = place_in_column()
    chips = groups // 2
    rows, width = shard_ref.shape
    greet_all(planes, groups)
    order = list(range(1, in_set)) + [0]

    def block_of(step, owner):
        return u_ref.at[
            pl.ds(step * CAP, CAP), pl.ds(pl.multiple_of(owner * width, width), width)
        ]

    def slots_of(buffer, step, owner):
        return buffer.at[step, pl.ds(pl.multiple_of(owner * CAP, 16), CAP), :]

    def sent(step, turn):
        target = lax.rem(me + turn, groups)
        return remote(
            block_of(step, target),
            slots_of(got, step, me),
            g_send.at[step, turn],
            g_recv.at[step, turn],
            target,
        )

    def own_copy(step):
        return pltpu.make_async_copy(block_of(step, me), slots_of(got, step, me), own_sem.at[step])

    def other_copy(step, owner):
        return pltpu.make_async_copy(
            m_ref.at[owner, pl.ds(step * CAP, CAP), :],
            slots_of(other, step, owner),
            m_sem.at[step, owner],
        )

    for step in order:

        @pl.loop(1, groups)
        def _(turn, step=step):
            sent(step, turn).start()

        own_copy(step).start()

    for step in order:

        @pl.loop(0, groups)
        def _(owner, step=step):
            other_copy(step, owner).start()

    def placed(step, row, buffer):
        keys = key_ref[step, pl.ds(row, tile), :]
        pieces = []
        for start in range(0, groups * CAP, 128):
            slot = lax.broadcasted_iota(jnp.int32, (tile, 128), 1) + start
            hit = None
            for owner in range(start // CAP, min(groups, (start + 127) // CAP + 1)):
                same = slot == keys[:, owner : owner + 1]
                hit = same if hit is None else hit | same
            pieces.append(jnp.where(hit, 1.0, 0.0).astype(bf16))
        return jnp.dot(
            jnp.concatenate(pieces, axis=1), buffer[step], preferred_element_type=f32
        )

    for step in order:

        @pl.loop(0, groups)
        def _(owner, step=step):
            other_copy(step, owner).wait()

        @pl.loop(0, rows // tile)
        def _(i, step=step):
            row = pl.multiple_of(i * tile, tile)
            placed_ref[step, pl.ds(row, tile), :] = placed(step, row, other).astype(bf16)

    z_copies = []
    for step in order:
        own_copy(step).wait()

        @pl.loop(1, groups)
        def _(turn, step=step):
            sent(step, turn).wait_recv()

        @pl.loop(0, rows // tile)
        def _(i, step=step):
            row = pl.multiple_of(i * tile, tile)
            total = placed(step, row, got)
            if step:
                out_z[step - 1, pl.ds(row, tile), :] = total.astype(bf16)
            else:
                shard_ref[pl.ds(row, tile), :] = total

        if step:
            copy = to_plane(
                out_z.at[step - 1],
                in_z.at[step - 1],
                z_send.at[step - 1],
                z_recv.at[step - 1],
                base + lax.rem(own - step + in_set, in_set),
            )
            copy.start()
            z_copies.append(copy)
    for copy in z_copies:
        copy.wait_recv()

    @pl.loop(0, rows // tile)
    def _(i):
        row = pl.multiple_of(i * tile, tile)
        total = shard_ref[pl.ds(row, tile), :]
        for step in range(1, in_set):
            total = total + in_z[step - 1, pl.ds(row, tile), :].astype(f32)
        shard_ref[pl.ds(row, tile), :] = total
        low[pl.ds(row, tile), :] = total.astype(bf16)

    def columns(owner):
        return rows_ref.at[:, pl.ds(pl.multiple_of(owner * width, width), width)]

    mine = pltpu.make_async_copy(low, columns(me), c_own)
    mine.start()
    out = []
    for step in list(range(1, chips)) + [0]:
        target = sibling if step == 0 else chip_peer(chip, core, step, chips)
        copy = remote(low, columns(me), c_send.at[step], c_recv.at[step], target)
        copy.start()
        out.append(copy)
    for step in range(1, chips):
        out[step - 1].wait_recv()
        source = chip_peer(chip, core, chips - step, chips)
        copy = remote(
            columns(source), columns(source), p_send.at[step], p_recv.at[step], sibling
        )
        copy.start()
        out.append(copy)
    mine.wait()
    out[chips - 1].wait_recv()
    for copy in out[chips:]:
        copy.wait_recv()
    for copy in out + z_copies:
        copy.wait_send()
    for step in order:

        @pl.loop(1, groups)
        def _(turn, step=step):
            sent(step, turn).wait_send()


def collect(u, other, key, planes, groups, collective_id):
    in_set, rows = key.shape[0], key.shape[1]
    slot_total, full = u.shape
    width = full // groups
    chips = groups // 2
    tile = min(256, rows)
    return pl.pallas_call(
        functools.partial(collect_kernel, planes, groups, in_set, tile),
        out_shape=(
            jax.ShapeDtypeStruct((rows, width), f32),
            jax.ShapeDtypeStruct((rows, full), bf16),
            jax.ShapeDtypeStruct((in_set, rows, width), bf16),
        ),
        in_specs=[VMEM, pl.BlockSpec(memory_space=pl.ANY), VMEM],
        out_specs=(VMEM, VMEM, VMEM),
        scratch_shapes=[
            pltpu.VMEM((in_set, groups * CAP, width), bf16),
            pltpu.VMEM((in_set, groups * CAP, width), bf16),
            pltpu.VMEM((in_set - 1, rows, width), bf16),
            pltpu.VMEM((in_set - 1, rows, width), bf16),
            pltpu.VMEM((rows, width), bf16),
            DMA((in_set, groups)),
            DMA((in_set, groups)),
            DMA((in_set,)),
            DMA((in_set, groups)),
            DMA((in_set - 1,)),
            DMA((in_set - 1,)),
            DMA,
            DMA((chips,)),
            DMA((chips,)),
            DMA((chips,)),
            DMA((chips,)),
        ],
        compiler_params=pltpu.CompilerParams(
            collective_id=collective_id, has_side_effects=True, vmem_limit_bytes=48 << 20
        ),
        cost_estimate=SMALL,
    )(u, other, key)


def planes_kernel(planes, x_ref, o_ref, own_sem, send_sem, recv_sem):
    plane = lax.axis_index("gx")
    barrier = pltpu.get_barrier_semaphore()
    own = pltpu.make_async_copy(x_ref, o_ref.at[plane], own_sem)
    own.start()
    for step in range(1, planes):
        target = lax.rem(plane + step, planes)
        pl.semaphore_signal(barrier, inc=1, device_id={"gx": target}, device_id_type=MESH)
    pl.semaphore_wait(barrier, planes - 1)
    copies = []
    for step in range(1, planes):
        copy = to_plane(
            x_ref,
            o_ref.at[plane],
            send_sem.at[step - 1],
            recv_sem.at[step - 1],
            lax.rem(plane + step, planes),
        )
        copy.start()
        copies.append(copy)
    own.wait()
    for copy in copies:
        copy.wait_recv()
        copy.wait_send()


def gather_planes(x, planes, collective_id):
    return pl.pallas_call(
        functools.partial(planes_kernel, planes),
        out_shape=jax.ShapeDtypeStruct((planes,) + x.shape, x.dtype),
        in_specs=[VMEM],
        out_specs=VMEM,
        scratch_shapes=[DMA, DMA((planes - 1,)), DMA((planes - 1,))],
        compiler_params=pltpu.CompilerParams(collective_id=collective_id, has_side_effects=True),
        cost_estimate=SMALL,
    )(x)


def rope_tables(length, width):
    half_width = width // 2
    frequency = rope_theta ** (-2.0 * jnp.arange(half_width, dtype=f32) / width)
    angles = jnp.arange(length, dtype=f32)[:, None] * frequency[None, :]
    return (jnp.cos(angles), jnp.sin(angles))


def apply_rotary(values, cosine, sine):
    half_width = values.shape[-1] // 2
    first = values[..., :half_width]
    second = values[..., half_width:]
    return jnp.concatenate(
        [first * cosine - second * sine, second * cosine + first * sine], axis=-1
    )


def unrotate(grads, cosine, sine):
    half_width = grads.shape[-1] // 2
    first = grads[..., :half_width]
    second = grads[..., half_width:]
    return jnp.concatenate(
        [first * cosine + second * sine, second * cosine - first * sine], axis=-1
    )


def allowed_mask(piece_starts):
    places = jnp.arange(SEQ, dtype=jnp.int32)
    causal = places[None, :] <= places[:, None]
    inside = (places[None, None, :] >= piece_starts[:, :, None]) & (
        places[None, None, :] < piece_starts[:, :, None] + PIECE
    )
    same_piece = jnp.any(inside[:, :, :, None] & inside[:, :, None, :], axis=1)
    return causal[None] | same_piece


def dot(spec, left, right):
    return jnp.einsum(spec, left, right, preferred_element_type=f32)


def after(first, *later):
    return lax.optimization_barrier((first,) + later)[1:]


def shards(
    block_input,
    out_grad,
    routes,
    adapter_ids,
    piece_starts,
    attn_gain,
    qk_gain,
    mlp_gain,
    w_qkv,
    w_out,
    a_qkv,
    b_out,
    head_pack,
    router,
    w_gate_up,
    w_down,
    exp_wide,
    exp_hidden,
):
    planes = lax.axis_size("gx")
    groups = lax.axis_size("gy")
    plane = lax.axis_index("gx")
    column = lax.axis_index("gy")
    rows, width_local = block_input.shape
    width = width_local * groups
    heads_local = head_pack.shape[0]
    rank_cols = head_pack.shape[2]
    head_width = head_pack.shape[3]
    experts_local = w_gate_up.shape[0]
    hidden_width = w_gate_up.shape[3]
    nseq = adapter_ids.shape[0]
    inv_root = head_width ** (-0.5)
    repeats = planes // experts_local
    steps = range(experts_local)
    own = lax.rem(plane, experts_local)

    def shifted(x, step):
        if step % experts_local == 0:
            return x
        pairs = []
        for p in range(planes):
            base = p // experts_local * experts_local
            pairs.append((p, base + (p - base + step) % experts_local))
        return lax.ppermute(x, "gx", pairs)

    def own_pieces(piece_for):
        pieces = []
        for step in range(planes):
            piece = piece_for(lax.rem(plane + step, planes))
            if step:
                pairs = [(p, (p + step) % planes) for p in range(planes)]
                piece = lax.ppermute(piece, "gx", pairs)
            pieces.append((lax.rem(plane - step + planes, planes), piece))
        return pieces

    def assembled(pieces, buffer, start=0):
        for source, piece in pieces:
            buffer = lax.dynamic_update_slice(buffer, piece, (source * piece.shape[0], start))
        return buffer

    compact = nseq * RANK

    def pick(x, axis):
        return jnp.concatenate(
            [
                lax.dynamic_slice_in_dim(x, adapter_ids[n] * RANK, RANK, axis=axis)
                for n in range(nseq)
            ],
            axis=axis,
        )

    token_seq = jnp.arange(rows, dtype=jnp.int32) // SEQ
    col_seq = jnp.arange(compact, dtype=jnp.int32) // RANK
    compact_mask = (token_seq[:, None] == col_seq[None, :]).astype(f32)
    a_pick = pick(a_qkv, 2)
    b_pick = pick(b_out, 0)
    pack_pick = pick(head_pack, 2)

    routes_all = lax.all_gather(routes, "gx", axis=0, tiled=False)
    adapters_all = lax.all_gather(adapter_ids, "gx", axis=0, tiled=False)
    dl = w_gate_up.shape[1]
    hl = exp_hidden.shape[1]
    qkv_width = 3 * heads_local * head_width
    weight_shard = jnp.concatenate(
        [
            w_qkv.reshape(w_qkv.shape[0], qkv_width),
            w_out.reshape(heads_local * head_width, w_out.shape[2]).T,
        ],
        axis=1,
    )
    attn_weight = lax.all_gather(weight_shard, "gx", axis=0, tiled=True)
    gathered = gather_columns(
        jnp.concatenate(
            [block_input, a_pick.transpose(0, 2, 1).reshape(3 * compact, width_local), b_pick],
            axis=0,
        ),
        groups,
        1,
    )
    full_rows = gathered[:rows]
    a_full = gathered[rows : rows + 3 * compact]
    b_full = gathered[rows + 3 * compact :]

    set_cols = experts_local * compact
    fold = max(1, 128 // set_cols)
    sets_adapters = adapters_all.reshape(repeats, experts_local * nseq)
    rank_index = jnp.arange(rank_cols, dtype=jnp.int32)
    set_index = jnp.arange(set_cols, dtype=jnp.int32)
    set_pick = (
        (rank_index // RANK)[None, :, None] == jnp.repeat(sets_adapters, RANK, axis=1)[:, None, :]
    ) & ((rank_index % RANK)[None, :, None] == (set_index % RANK)[None, None, :])
    set_pick = set_pick.astype(bf16)

    def folded(x):
        return jnp.concatenate(jnp.split(x, fold, axis=1), axis=2)

    def unfolded(x):
        return jnp.concatenate(jnp.split(x, fold, axis=2), axis=1)

    rank_rows = jnp.concatenate(
        [exp_wide[:, :, c] for c in range(3)] + [exp_hidden[:, :, c] for c in range(3)], axis=1
    )
    rank_shard = folded(
        dot("emr,srk->semk", rank_rows, set_pick)
        .reshape(planes, rank_rows.shape[1], set_cols)
        .astype(bf16)
    )
    (rank_shard,) = after(attn_weight, rank_shard)
    rank_weight = unfolded(lax.all_to_all(rank_shard, "gx", 0, 0, tiled=True))
    down_pieces = []
    waited = attn_weight
    part_rows = dl // DOWN_PARTS
    for part in range(DOWN_PARTS):
        (down_later,) = after(waited, w_down)
        pieces = own_pieces(
            lambda p: lax.dynamic_slice(
                down_later,
                (lax.rem(p, experts_local), part * part_rows, 0),
                (1, part_rows, hidden_width),
            )[0]
        )
        waited = tuple(piece for _, piece in pieces)
        down_pieces.append(pieces)

    def rank_part(start, count):
        return rank_weight[:, start : start + count].reshape(planes * count, set_cols)

    wide_parts = [rank_part(c * dl, dl) for c in range(3)]
    hidden_gate, hidden_up, hidden_down = [rank_part(3 * dl + c * hl, hl) for c in range(3)]
    rank_end = 2 * hidden_width + 2 * set_cols
    second_weight = jnp.zeros((width, hidden_width + set_cols), bf16)
    second_weight = lax.dynamic_update_slice(second_weight, wide_parts[2], (0, hidden_width))
    for part, pieces in enumerate(down_pieces):
        for source, piece in pieces:
            second_weight = lax.dynamic_update_slice(
                second_weight, piece, (source * dl + part * part_rows, 0)
            )

    expert_ids = own + experts_local * jnp.arange(groups, dtype=jnp.int32)
    set_start = (plane // experts_local) * experts_local
    step_plane = lax.rem(own - jnp.arange(experts_local) + experts_local, experts_local)
    routes_set = routes_all[set_start + step_plane]
    hits = jnp.any(routes_set[:, :, :, None] == expert_ids, axis=2)
    order = jnp.arange(rows, dtype=jnp.int32)
    earlier = (order[None, :] < order[:, None]).astype(bf16)
    places = dot("ts,gsc->gct", earlier, hits.astype(bf16))
    slot_key = jnp.where(hits.transpose(0, 2, 1), places.astype(jnp.int32), -1)
    slots = jnp.arange(CAP, dtype=jnp.int32)
    column_key = slot_key + CAP * jnp.arange(groups, dtype=jnp.int32)[None, :, None]
    column_key = jnp.where(slot_key >= 0, column_key, -1).transpose(0, 2, 1)
    own_key = lax.dynamic_index_in_dim(slot_key, column, 1, keepdims=False)
    own_pick = (own_key[:, None, :] == slots[None, :, None]).astype(bf16)
    rank_mask = (
        (step_plane[:, None] * nseq + token_seq[None, :])[:, :, None]
        == (set_index // RANK)[None, None, :]
    ).astype(bf16)
    slot_total = experts_local * CAP
    mask_slot = dot("gst,gtr->gsr", own_pick, rank_mask).reshape(slot_total, set_cols)
    valid = jnp.max(mask_slot, axis=1)

    col_start = column * width_local
    first_norm_gain = lax.dynamic_slice_in_dim(attn_gain, col_start, width_local)
    input_f = full_rows.astype(f32)
    scale_one = lax.rsqrt(jnp.mean(input_f * input_f, axis=-1, keepdims=True) + norm_eps)
    hat_one = input_f * scale_one
    normed_bf = (hat_one * attn_gain).astype(bf16)
    base = dot("td,de->te", normed_bf, attn_weight[:, :qkv_width]).reshape(
        rows, heads_local, 3, head_width
    )
    rank_in = dot("td,kd->tk", normed_bf, a_full).reshape(rows, 3, compact)
    rank_low = (rank_in * compact_mask[:, None, :]).astype(bf16)
    projected = base + rank_scale * dot("tcr,hcre->thce", rank_low, pack_pick[:, :3])
    query_pre = projected[:, :, 0]
    key_pre = projected[:, :, 1]
    value_bf = projected[:, :, 2].astype(bf16)
    square_sums = jnp.stack(
        [jnp.sum(query_pre * query_pre, axis=(1, 2)), jnp.sum(key_pre * key_pre, axis=(1, 2))]
    )
    square_sums = add_small(square_sums.reshape(-1, 128), groups, 2).reshape(2, rows)
    query_scale = lax.rsqrt(square_sums[0] / width + norm_eps)[:, None, None]
    key_scale = lax.rsqrt(square_sums[1] / width + norm_eps)[:, None, None]
    head_start = column * heads_local * head_width
    gains_local = lax.dynamic_slice_in_dim(
        qk_gain, head_start, heads_local * head_width, axis=1
    ).reshape(2, heads_local, head_width)
    query_hat = query_pre * query_scale
    key_hat = key_pre * key_scale
    cosine, sine = rope_tables(SEQ, head_width)
    cosine = cosine[None, :, None, :]
    sine = sine[None, :, None, :]
    query_bf = apply_rotary(
        (query_hat * gains_local[0]).reshape(nseq, SEQ, heads_local, head_width), cosine, sine
    ).astype(bf16)
    key_bf = apply_rotary(
        (key_hat * gains_local[1]).reshape(nseq, SEQ, heads_local, head_width), cosine, sine
    ).astype(bf16)
    values_seq = value_bf.reshape(nseq, SEQ, heads_local, head_width)
    allowed = allowed_mask(piece_starts)[:, None]
    scores = dot("nqhe,nkhe->nhqk", query_bf, key_bf) * inv_root
    scores = jnp.where(allowed, scores, -1e30)
    row_peak = jnp.max(scores, axis=-1, keepdims=True)
    raised = jnp.exp(scores - row_peak)
    row_total = jnp.sum(raised, axis=-1, keepdims=True)
    log_total = row_peak + jnp.log(row_total)
    weights = raised / row_total
    attended = dot("nhqk,nkhe->nqhe", weights.astype(bf16), values_seq)
    attn_bf = attended.reshape(rows, heads_local, head_width).astype(bf16)
    rank_out = dot("the,hre->thr", attn_bf, pack_pick[:, 3])
    rank_out_low = (rank_out * compact_mask[:, None, :]).astype(bf16)
    out_weight = attn_weight[:, qkv_width:]
    b_turned = (rank_scale * b_full.T).astype(bf16)
    branch = scatter_product(
        jnp.concatenate(
            [
                attn_bf.reshape(rows, heads_local * head_width),
                rank_out_low.reshape(rows, heads_local * compact),
            ],
            axis=1,
        ),
        jnp.concatenate([out_weight] + [b_turned] * heads_local, axis=1),
        groups,
        3,
    )
    middle = block_input.astype(f32) + branch
    middle_low = middle.astype(bf16)

    (spread_rows,) = after(waited, jnp.concatenate([middle_low, out_grad], axis=1))
    slot_rows, first_weight = spread(
        spread_rows,
        slot_key,
        w_gate_up.reshape(experts_local, dl, 2 * hidden_width),
        planes,
        groups,
        rank_end + 2 * router.shape[1],
        4,
    )
    middle_slot, grad_slot = slot_rows[0], slot_rows[1]
    first_weight = lax.dynamic_update_slice(
        first_weight,
        jnp.concatenate([wide_parts[0], wide_parts[1], router, router], axis=1),
        (0, 2 * hidden_width),
    )
    both_rows = lax.all_gather(
        jnp.concatenate([middle_low, out_grad], axis=0), "gy", axis=1, tiled=True
    )
    middle_slot = middle_slot.astype(f32)
    slot_scale = lax.rsqrt(jnp.mean(middle_slot * middle_slot, axis=-1, keepdims=True) + norm_eps)
    expert_in = (middle_slot * slot_scale * mlp_gain).astype(bf16)
    pre_wide = jnp.dot(expert_in, first_weight, preferred_element_type=f32)
    logits = pre_wide[:, rank_end : rank_end + router.shape[1]]
    logit_raised = jnp.exp(logits - jnp.max(logits, axis=-1, keepdims=True))
    route_probs = logit_raised / jnp.sum(logit_raised, axis=-1, keepdims=True)
    own_id = column * experts_local + own
    is_own = (jnp.arange(router.shape[1], dtype=jnp.int32) == own_id).astype(f32)[None, :]
    gate = jnp.sum(route_probs * is_own, axis=1, keepdims=True) * valid[:, None]
    two_masks = jnp.concatenate([mask_slot, mask_slot], axis=1)
    rank_gu_low = (pre_wide[:, 2 * hidden_width : rank_end] * two_masks).astype(bf16)
    gate_pre = pre_wide[:, :hidden_width] + rank_scale * dot(
        "sr,fr->sf", rank_gu_low[:, :set_cols], hidden_gate
    )
    up_pre = pre_wide[:, hidden_width : 2 * hidden_width] + rank_scale * dot(
        "sr,fr->sf", rank_gu_low[:, set_cols:], hidden_up
    )
    sigma = jax.nn.sigmoid(gate_pre)
    activated = gate_pre * sigma
    inner_bf = (activated * up_pre).astype(bf16)
    rank_down = dot("sf,fr->sr", inner_bf, hidden_down)
    rank_down_low = (rank_down * mask_slot).astype(bf16)
    inner_wide = jnp.concatenate([inner_bf, (down_scale * rank_down_low).astype(bf16)], axis=1)
    expert_output = dot("sf,df->sd", inner_wide, second_weight)
    grad_slot_f = grad_slot.astype(f32)
    gate_grad = jnp.sum(grad_slot_f * expert_output, axis=-1, keepdims=True)
    out_grad_bf = (gate * grad_slot_f).astype(bf16)
    inner_wide_grad = dot("sd,df->sf", out_grad_bf, second_weight)
    rank_down_grad = (down_scale * inner_wide_grad[:, hidden_width:] * mask_slot).astype(bf16)
    inner_grad = inner_wide_grad[:, :hidden_width] + dot("sr,fr->sf", rank_down_grad, hidden_down)
    gate_pre_grad = (inner_grad * up_pre * sigma * (1.0 + gate_pre * (1.0 - sigma))).astype(bf16)
    up_pre_grad = (inner_grad * activated).astype(bf16)
    rank_gu_grad = (
        rank_scale
        * jnp.concatenate(
            [
                dot("sf,fr->sr", gate_pre_grad, hidden_gate),
                dot("sf,fr->sr", up_pre_grad, hidden_up),
            ],
            axis=1,
        )
        * two_masks
    ).astype(bf16)
    logit_grad = (is_own - route_probs) * (gate * gate_grad)
    logit_high = logit_grad.astype(bf16)
    logit_rest = (logit_grad - logit_high.astype(f32)).astype(bf16)
    pre_wide_grad = jnp.concatenate(
        [gate_pre_grad, up_pre_grad, rank_gu_grad, logit_high, logit_rest], axis=1
    )
    rows_grad = dot("sf,df->sd", pre_wide_grad, first_weight)
    weighted = (gate * expert_output).astype(bf16)
    weighted = weighted.reshape(slot_total, groups, width_local).transpose(1, 0, 2)
    normed_two_part, normed_two_rows, moe_planes = collect(
        rows_grad.astype(bf16),
        lax.all_to_all(weighted, "gy", 0, 0, tiled=True),
        column_key,
        planes,
        groups,
        5,
    )
    moe_part = moe_planes[0].astype(f32)
    for step in range(1, experts_local):
        moe_part = moe_part + shifted(moe_planes[step], experts_local - step).astype(f32)
    layer_out = (middle + moe_part).astype(bf16)

    wide_grads = [
        dot("sd,sr->dr", expert_in, rank_gu_grad[:, :set_cols]),
        dot("sd,sr->dr", expert_in, rank_gu_grad[:, set_cols:]),
        down_scale * dot("sd,sr->dr", out_grad_bf, rank_down_low),
    ]
    hidden_grads = [
        rank_scale * dot("sf,sr->fr", gate_pre_grad, rank_gu_low[:, :set_cols]),
        rank_scale * dot("sf,sr->fr", up_pre_grad, rank_gu_low[:, set_cols:]),
        dot("sf,sr->fr", inner_bf, rank_down_grad),
    ]
    rank_grads = jnp.concatenate(
        [x.astype(bf16).reshape(planes, dl, set_cols) for x in wide_grads]
        + [x.astype(bf16).reshape(planes, hl, set_cols) for x in hidden_grads],
        axis=1,
    )
    (rank_grads,) = after(normed_two_rows, rank_grads)
    rank_grads = unfolded(lax.all_to_all(folded(rank_grads), "gx", 0, 0, tiled=True))
    rank_grads = rank_grads.reshape((repeats, experts_local) + rank_grads.shape[1:])
    wide_sum = jnp.stack(
        [
            dot("semk,srk->emr", rank_grads[:, :, c * dl : (c + 1) * dl], set_pick)
            for c in range(3)
        ],
        axis=2,
    )
    hidden_sum = jnp.stack(
        [
            dot(
                "semk,srk->emr",
                rank_grads[:, :, 3 * dl + c * hl : 3 * dl + (c + 1) * hl],
                set_pick,
            )
            for c in range(3)
        ],
        axis=2,
    )

    middle_rows = both_rows[:rows].astype(f32)
    grad_rows = both_rows[rows:].astype(f32)
    scale_two = lax.rsqrt(jnp.mean(middle_rows * middle_rows, axis=-1, keepdims=True) + norm_eps)
    normed_two_grad = normed_two_rows.astype(f32)
    hat_two = middle_rows * scale_two
    scaled_two = normed_two_grad * mlp_gain
    stat_two = jnp.mean(scaled_two * hat_two, axis=-1, keepdims=True)
    branch_rows = (grad_rows + scale_two * (scaled_two - hat_two * stat_two)).astype(bf16)
    gain_two_local = lax.dynamic_slice_in_dim(mlp_gain, col_start, width_local)
    middle_grad = out_grad.astype(f32) + scale_two * (
        normed_two_part * gain_two_local - middle_low.astype(f32) * scale_two * stat_two
    )
    rank_out_grad = rank_scale * dot("td,rd->tr", branch_rows, b_full)
    rank_out_bf = (rank_out_grad * compact_mask).astype(bf16)
    pack_out_grad = dot("the,tr->hre", attn_bf, rank_out_bf)
    attention_gradient = dot("td,de->te", branch_rows, out_weight).reshape(
        rows, heads_local, head_width
    ) + dot(
        "tr,hre->the", rank_out_bf, pack_pick[:, 3]
    )
    attn_grad_bf = attention_gradient.reshape(nseq, SEQ, heads_local, head_width).astype(bf16)
    scores_again = dot("nqhe,nkhe->nhqk", query_bf, key_bf) * inv_root
    scores_again = jnp.where(allowed, scores_again, -1e30)
    weights_again = jnp.exp(scores_again - log_total)
    value_grad = dot("nhqk,nqhe->nkhe", weights_again.astype(bf16), attn_grad_bf)
    weight_grad = dot("nqhe,nkhe->nhqk", attn_grad_bf, values_seq)
    row_dot = jnp.sum(weight_grad * weights_again, axis=-1, keepdims=True)
    score_grad = (weights_again * (weight_grad - row_dot)).astype(bf16)
    query_grad = dot("nhqk,nkhe->nqhe", score_grad, key_bf) * inv_root
    key_grad = dot("nhqk,nqhe->nkhe", score_grad, query_bf) * inv_root
    query_hat_grad = (
        unrotate(query_grad, cosine, sine).reshape(rows, heads_local, head_width) * gains_local[0]
    )
    key_hat_grad = (
        unrotate(key_grad, cosine, sine).reshape(rows, heads_local, head_width) * gains_local[1]
    )
    value_pre_grad = value_grad.reshape(rows, heads_local, head_width)
    stat_query = jnp.sum(query_hat_grad * query_hat, axis=(1, 2))
    stat_key = jnp.sum(key_hat_grad * key_hat, axis=(1, 2))

    def rank_terms(values, which):
        return dot("the,hre->rt", values.astype(bf16), pack_pick[:, which])

    sums = jnp.concatenate(
        [
            rank_terms(query_hat_grad, 0),
            rank_terms(key_hat_grad, 1),
            rank_terms(value_pre_grad, 2),
            rank_terms(query_hat, 0),
            rank_terms(key_hat, 1),
            jnp.sum(rank_out_low.astype(f32), axis=1).T,
            jnp.stack([stat_query, stat_key]),
        ],
        axis=0,
    )
    padding = -sums.shape[0] % 32
    sums = add_pairs(jnp.pad(sums.astype(bf16), ((0, padding), (0, 0))), groups, 6)
    first_total = sums[: 3 * compact].reshape(3, compact, rows)
    second_total = sums[3 * compact : 5 * compact].reshape(2, compact, rows)
    mean_qk = sums[6 * compact : 6 * compact + 2] / width
    branch_local = lax.dynamic_slice_in_dim(branch_rows, col_start, width_local, axis=1)
    b_out_sum = rank_scale * dot(
        "rt,td->rd", sums[5 * compact : 6 * compact].astype(bf16), branch_local
    )
    scales_qk = jnp.stack([query_scale[:, 0, 0], key_scale[:, 0, 0]])
    rank_qk = scales_qk[:, None, :] * (first_total[:2] - second_total * mean_qk[:, None, :])
    rank_grad_full = rank_scale * jnp.concatenate([rank_qk, first_total[2:]], axis=0)
    rank_grad_bf = (rank_grad_full * compact_mask.T[None]).astype(bf16)
    query_pre_grad = query_scale * (query_hat_grad - query_hat * mean_qk[0][:, None, None])
    key_pre_grad = key_scale * (key_hat_grad - key_hat * mean_qk[1][:, None, None])
    pre_grad = jnp.stack([query_pre_grad, key_pre_grad, value_pre_grad], axis=2).astype(bf16)
    pack_b_grad = rank_scale * dot("tcr,thce->rhce", rank_low, pre_grad)
    normed_one_grad = scatter_product(
        pre_grad.reshape(rows, qkv_width), attn_weight[:, :qkv_width], groups, 7
    )
    adapter_input_gradient = dot("crt,cdr->td", rank_grad_bf, a_pick)
    first_normalized_shard = lax.dynamic_slice_in_dim(hat_one, col_start, width_local, axis=1)
    normed_local_bf = lax.dynamic_slice_in_dim(normed_bf, col_start, width_local, axis=1)
    a_rows_grad = dot("td,crt->rcd", normed_local_bf, rank_grad_bf)
    scaled_one = (normed_one_grad + adapter_input_gradient) * first_norm_gain
    stat_one = jnp.sum(scaled_one * first_normalized_shard, axis=-1)
    stat_one_sum = add_small(stat_one.reshape(-1, 128), groups, 8).reshape(rows, 1)
    input_grad = middle_grad + scale_one * (
        scaled_one - first_normalized_shard * stat_one_sum / width
    )
    pack_grad = jnp.concatenate(
        [
            pack_b_grad.transpose(1, 2, 0, 3),
            pack_out_grad[:, None],
        ],
        axis=1,
    )
    small = jnp.concatenate(
        [
            a_rows_grad.reshape(compact, 3 * width_local),
            b_out_sum,
            pack_grad.transpose(2, 0, 1, 3).reshape(compact, heads_local * 4 * head_width),
        ],
        axis=1,
    )
    small_all = gather_planes(small.astype(bf16), planes, 9)
    small_all = small_all.reshape(planes * compact, small.shape[1])
    row_at = (
        adapters_all[:, :, None] * RANK + jnp.arange(RANK, dtype=jnp.int32)[None, None, :]
    ).reshape(-1)
    put = (jnp.arange(rank_cols, dtype=jnp.int32)[:, None] == row_at[None, :]).astype(bf16)
    small_sum = jnp.dot(put, small_all, preferred_element_type=f32)
    a_end = 3 * width_local
    b_end = a_end + width_local
    a_sum = small_sum[:, :a_end].reshape(rank_cols, 3, width_local).transpose(1, 2, 0)
    b_sum = small_sum[:, a_end:b_end]
    head_sum = small_sum[:, b_end:].reshape(rank_cols, heads_local, 4, head_width)
    head_sum = head_sum.transpose(1, 2, 0, 3)
    return (layer_out, input_grad, a_sum, b_sum, head_sum, wide_sum, hidden_sum)


def solution(mesh):
    return jax.shard_map(
        shards,
        mesh=mesh,
        in_specs=(
            P("gx", "gy"),
            P("gx", "gy"),
            P("gx", None),
            P("gx"),
            P("gx", None),
            P(),
            P(),
            P(),
            P("gx", "gy", None, None),
            P("gy", None, "gx"),
            P(None, "gy", None),
            P(None, "gy"),
            P("gy", None, None, None),
            P(),
            P("gy", "gx", None, None),
            P("gy", "gx", None),
            P("gy", "gx", None, None),
            P("gy", "gx", None, None),
        ),
        out_specs=(
            P("gx", "gy"),
            P("gx", "gy"),
            P(None, "gy", None),
            P(None, "gy"),
            P("gy", None, None, None),
            P("gy", "gx", None, None),
            P("gy", "gx", None, None),
        ),
        check_vma=False,
    )
```

```python
import functools
import jax
import jax.numpy as jnp
from jax import lax
from jax.experimental import pallas as pl
from jax.experimental.pallas import tpu as pltpu
from jax.sharding import PartitionSpec as P

RANK = 16
SEQ = 1024
PIECE = 256
CAP = 288


norm_eps = 1e-05
rope_theta = 10000.0
rank_scale = 0.5
down_scale = 4.0
bf16 = jnp.bfloat16
f32 = jnp.float32
VMEM = pl.BlockSpec(memory_space=pltpu.VMEM)
DMA = pltpu.SemaphoreType.DMA
MESH = pl.DeviceIdType.MESH
SMALL = pl.CostEstimate(flops=0, bytes_accessed=1 << 16, transcendentals=0)
CAP = 288
SMALL = pl.CostEstimate(flops=0, bytes_accessed=1 << 16, transcendentals=0)


def place_in_column():
    me = lax.axis_index("gy")
    chip, core = lax.div(me, 2), lax.rem(me, 2)
    return me, chip, core, me + 1 - 2 * core


def chip_peer(chip, core, step, chips):
    return lax.rem(chip + step, chips) * 2 + core


def greet_chips(chip, core, sibling, chips, planes=1):
    barrier = pltpu.get_barrier_semaphore()
    for step in range(1, planes):
        target = lax.rem(lax.axis_index("gx") + step, planes)
        pl.semaphore_signal(barrier, inc=1, device_id={"gx": target}, device_id_type=MESH)
    pl.semaphore_signal(barrier, inc=1, device_id={"gy": sibling}, device_id_type=MESH)
    for step in range(1, chips):
        pl.semaphore_signal(
            barrier,
            inc=1,
            device_id={"gy": chip_peer(chip, core, step, chips)},
            device_id_type=MESH,
        )
    pl.semaphore_wait(barrier, chips + planes - 1)


def remote(src, dst, send_sem, recv_sem, target):
    return pltpu.make_async_remote_copy(
        src_ref=src,
        dst_ref=dst,
        send_sem=send_sem,
        recv_sem=recv_sem,
        device_id={"gy": target},
        device_id_type=MESH,
    )


def gather_kernel(
    chips,
    rows,
    tile,
    x_ref,
    gain_ref,
    normed_ref,
    scale_ref,
    rest_ref,
    whole,
    own_sem,
    send_sem,
    recv_sem,
    pass_sem,
    passed_sem,
):
    me, chip, core, sibling = place_in_column()
    width = x_ref.shape[1]

    def columns(owner):
        return whole.at[:, pl.ds(pl.multiple_of(owner * width, width), width)]

    own = pltpu.make_async_copy(x_ref, columns(me), own_sem)
    own.start()
    greet_chips(chip, core, sibling, chips)
    out = []
    for step in list(range(1, chips)) + [0]:
        target = sibling if step == 0 else chip_peer(chip, core, step, chips)
        copy = remote(x_ref, columns(me), send_sem.at[step], recv_sem.at[step], target)
        copy.start()
        out.append(copy)
    for step in range(1, chips):
        out[step - 1].wait_recv()
        source = chip_peer(chip, core, chips - step, chips)
        copy = remote(
            columns(source), columns(source), pass_sem.at[step], passed_sem.at[step], sibling
        )
        copy.start()
        out.append(copy)
    own.wait()
    out[chips - 1].wait_recv()
    for copy in out[chips:]:
        copy.wait_recv()

    @pl.loop(0, rows // tile)
    def _(i):
        at = pl.ds(pl.multiple_of(i * tile, tile), tile)
        values = whole[at, :].astype(f32)
        scale = lax.rsqrt(jnp.mean(values * values, axis=-1, keepdims=True) + norm_eps)
        scale_ref[at, :] = jnp.broadcast_to(scale, (tile, 128))
        normed_ref[at, :] = (values * scale * gain_ref[...]).astype(bf16)

    rest_ref[...] = whole[pl.ds(rows, rest_ref.shape[0]), :]
    for copy in out:
        copy.wait_send()


def gather_normed(x, gain, rows, groups, collective_id):
    chips = groups // 2
    total, width = x.shape
    full = groups * width
    return pl.pallas_call(
        functools.partial(gather_kernel, chips, rows, 64),
        out_shape=(
            jax.ShapeDtypeStruct((rows, full), bf16),
            jax.ShapeDtypeStruct((rows, 128), f32),
            jax.ShapeDtypeStruct((total - rows, full), bf16),
        ),
        in_specs=[VMEM, VMEM],
        out_specs=(VMEM, VMEM, VMEM),
        scratch_shapes=[
            pltpu.VMEM((total, full), bf16),
            DMA,
            DMA((chips,)),
            DMA((chips,)),
            DMA((chips,)),
            DMA((chips,)),
        ],
        compiler_params=pltpu.CompilerParams(
            collective_id=collective_id, has_side_effects=True, vmem_limit_bytes=48 << 20
        ),
        cost_estimate=SMALL,
    )(x, gain.reshape(1, full))


def scatter_and_carry_kernel(
    planes, first, chips, tile, l_ref, r_ref, w_ref, o_ref, w_out, *rest
):
    *scratch, w_own, w_send, w_recv = rest
    plane = lax.axis_index("gx")
    in_set, count = w_ref.shape[0], w_out.shape[1]

    def piece(target):
        return w_ref.at[lax.rem(target, in_set), pl.ds(first, count), :]

    def carry():
        own = pltpu.make_async_copy(piece(plane), w_out.at[plane], w_own)
        own.start()
        copies = []
        for step in range(1, planes):
            target = lax.rem(plane + step, planes)
            copy = to_plane(
                piece(target), w_out.at[plane], w_send.at[step - 1], w_recv.at[step - 1], target
            )
            copy.start()
            copies.append(copy)
        return own, copies

    own, copies = scatter_kernel(
        chips, tile, l_ref, r_ref, o_ref, *scratch, planes=planes, after_greeting=carry
    )
    own.wait()
    for copy in copies:
        copy.wait_recv()
        copy.wait_send()


def scatter_kernel(
    chips,
    tile,
    l_ref,
    r_ref,
    o_ref,
    part,
    got,
    pair,
    far,
    part_s,
    got_s,
    pair_s,
    far_s,
    planes=1,
    after_greeting=None,
):
    me, chip, core, sibling = place_in_column()
    rows, width = o_ref.shape
    greet_chips(chip, core, sibling, chips, planes)
    carried = after_greeting() if after_greeting else None
    steps = list(range(1, chips)) + [0]

    def product(owner, row):
        chunk = r_ref[pl.ds(pl.multiple_of(owner * width, width), width), :]
        return lax.dot_general(
            l_ref[pl.ds(row, tile), :],
            chunk,
            (((1,), (1,)), ((), ())),
            preferred_element_type=f32,
        )

    copies = []
    for step in steps:
        owner = chip_peer(chip, 1 - core, step, chips)

        @pl.loop(0, rows // tile)
        def _(i, owner=owner, step=step):
            row = pl.multiple_of(i * tile, tile)
            part[step, pl.ds(row, tile), :] = product(owner, row).astype(bf16)

        copy = remote(part.at[step], got.at[step], part_s.at[step], got_s.at[step], sibling)
        copy.start()
        copies.append(copy)
    for step in steps:
        owner = chip_peer(chip, core, step, chips)
        copies[steps.index(step)].wait_recv()

        @pl.loop(0, rows // tile)
        def _(i, owner=owner, step=step):
            row = pl.multiple_of(i * tile, tile)
            total = product(owner, row) + got[step, pl.ds(row, tile), :].astype(f32)
            if step == 0:
                o_ref[pl.ds(row, tile), :] = total
            else:
                pair[step - 1, pl.ds(row, tile), :] = total.astype(bf16)

        if step > 0:
            copy = remote(
                pair.at[step - 1], far.at[step - 1], pair_s.at[step - 1], far_s.at[step - 1], owner
            )
            copy.start()
            copies.append(copy)
    for step in range(1, chips):
        copies[chips + step - 1].wait_recv()

        @pl.loop(0, rows // tile)
        def _(i, step=step):
            row = pl.multiple_of(i * tile, tile)
            o_ref[pl.ds(row, tile), :] += far[step - 1, pl.ds(row, tile), :].astype(f32)

    for copy in copies:
        copy.wait_send()
    return carried


def scatter_product(left, right, groups, collective_id, weight=None, first=0, planes=1):
    chips = groups // 2
    rows, inner = left.shape
    width = right.shape[0] // groups
    tile = min(256, rows)
    body = functools.partial(scatter_kernel, chips, tile)
    out_shape = (jax.ShapeDtypeStruct((rows, width), f32),)
    in_specs, out_specs = [VMEM, VMEM], (VMEM,)
    scratch = [
        pltpu.VMEM((chips, rows, width), bf16),
        pltpu.VMEM((chips, rows, width), bf16),
        pltpu.VMEM((chips - 1, rows, width), bf16),
        pltpu.VMEM((chips - 1, rows, width), bf16),
        DMA((chips,)),
        DMA((chips,)),
        DMA((chips - 1,)),
        DMA((chips - 1,)),
    ]
    operands = (left, right)
    if weight is not None:
        body = functools.partial(scatter_and_carry_kernel, planes, first, chips, tile)
        carried = (planes, weight.shape[1] - first, weight.shape[2])
        out_shape += (jax.ShapeDtypeStruct(carried, bf16),)
        in_specs = in_specs + [pl.BlockSpec(memory_space=pl.ANY)]
        out_specs += (pl.BlockSpec(memory_space=pl.ANY),)
        scratch = scratch + [DMA, DMA((planes - 1,)), DMA((planes - 1,))]
        operands += (weight,)
    return pl.pallas_call(
        body,
        out_shape=out_shape,
        in_specs=in_specs,
        out_specs=out_specs,
        scratch_shapes=scratch,
        compiler_params=pltpu.CompilerParams(
            collective_id=collective_id, has_side_effects=True, vmem_limit_bytes=48 << 20
        ),
        cost_estimate=SMALL,
    )(*operands)


def add_kernel(groups, x_ref, o_ref, got, send_sem, recv_sem):
    me = lax.axis_index("gy")
    barrier = pltpu.get_barrier_semaphore()
    for step in range(1, groups):
        target = lax.rem(me + step, groups)
        pl.semaphore_signal(barrier, inc=1, device_id={"gy": target}, device_id_type=MESH)
    pl.semaphore_wait(barrier, groups - 1)
    copies = []
    for step in range(1, groups):
        target = lax.rem(me + step, groups)
        copy = remote(
            x_ref, got.at[step - 1], send_sem.at[step - 1], recv_sem.at[step - 1], target
        )
        copy.start()
        copies.append(copy)
    total = x_ref[...]
    for step in range(1, groups):
        copies[step - 1].wait_recv()
        total = total + got[step - 1]
    o_ref[...] = total
    for copy in copies:
        copy.wait_send()


def add_small(x, groups, collective_id):
    return pl.pallas_call(
        functools.partial(add_kernel, groups),
        out_shape=jax.ShapeDtypeStruct(x.shape, f32),
        in_specs=[VMEM],
        out_specs=VMEM,
        scratch_shapes=[
            pltpu.VMEM((groups - 1,) + x.shape, f32),
            DMA((groups - 1,)),
            DMA((groups - 1,)),
        ],
        compiler_params=pltpu.CompilerParams(collective_id=collective_id, has_side_effects=True),
        cost_estimate=SMALL,
    )(x)


def add_pairs_kernel(
    chips, x_ref, o_ref, got, pair, far, done, got_s, far_s, done_s
):
    me, chip, core, sibling = place_in_column()
    half = x_ref.shape[0] // 2
    greet_chips(chip, core, sibling, chips)
    first = remote(x_ref, got, got_s.at[0], got_s.at[1], sibling)
    first.start()
    first.wait_recv()
    own = pl.ds(pl.multiple_of(core * half, 16), half)
    total = x_ref[own, :].astype(f32) + got[own, :].astype(f32)
    pair[...] = total.astype(bf16)
    copies = []
    for step in range(1, chips):
        copy = remote(
            pair,
            far.at[step - 1],
            far_s.at[0, step - 1],
            far_s.at[1, step - 1],
            chip_peer(chip, core, step, chips),
        )
        copy.start()
        copies.append(copy)
    for step in range(1, chips):
        copies[step - 1].wait_recv()
        total = total + far[step - 1].astype(f32)
    done[own, :] = total.astype(bf16)
    last = remote(done.at[own, :], done.at[own, :], done_s.at[0], done_s.at[1], sibling)
    last.start()
    last.wait_recv()
    o_ref[...] = done[...].astype(f32)
    first.wait_send()
    for copy in copies:
        copy.wait_send()
    last.wait_send()


def add_pairs(x, groups, collective_id):
    chips = groups // 2
    rows, width = x.shape
    return pl.pallas_call(
        functools.partial(add_pairs_kernel, chips),
        out_shape=jax.ShapeDtypeStruct(x.shape, f32),
        in_specs=[VMEM],
        out_specs=VMEM,
        scratch_shapes=[
            pltpu.VMEM(x.shape, bf16),
            pltpu.VMEM((rows // 2, width), bf16),
            pltpu.VMEM((chips - 1, rows // 2, width), bf16),
            pltpu.VMEM(x.shape, bf16),
            DMA((2,)),
            DMA((2, chips - 1)),
            DMA((2,)),
        ],
        compiler_params=pltpu.CompilerParams(collective_id=collective_id, has_side_effects=True),
        cost_estimate=SMALL,
    )(x)


def plane_place(planes_in_set):
    plane = lax.axis_index("gx")
    own = lax.rem(plane, planes_in_set)
    return plane, own, plane - own


def to_plane(src, dst, send_sem, recv_sem, target):
    return pltpu.make_async_remote_copy(
        src_ref=src,
        dst_ref=dst,
        send_sem=send_sem,
        recv_sem=recv_sem,
        device_id={"gx": target},
        device_id_type=MESH,
    )


def greet_all(planes, groups):
    barrier = pltpu.get_barrier_semaphore()
    plane, me = lax.axis_index("gx"), lax.axis_index("gy")

    @pl.loop(1, planes)
    def _(step):
        target = lax.rem(plane + step, planes)
        pl.semaphore_signal(barrier, inc=1, device_id={"gx": target}, device_id_type=MESH)

    @pl.loop(1, groups)
    def _(step):
        target = lax.rem(me + step, groups)
        pl.semaphore_signal(barrier, inc=1, device_id={"gy": target}, device_id_type=MESH)

    pl.semaphore_wait(barrier, planes + groups - 2)


def spread_kernel(
    planes,
    groups,
    in_set,
    x_ref,
    key_ref,
    w_ref,
    o_ref,
    full_ref,
    from_plane,
    picked,
    own_sem,
    w_send,
    w_recv,
    z_send,
    z_recv,
    g_send,
    g_recv,
):
    plane, own, base = plane_place(in_set)
    me = lax.axis_index("gy")
    width = x_ref.shape[1] // 2
    depth, inner = w_ref.shape[1], w_ref.shape[2]
    greet_all(planes, groups)
    last = in_set - 1

    def handed(step, up):
        side = 0 if up else 1
        distance = step if up else in_set - step
        there = own + (1 if up else -1)
        holds = own - (step - 1) if up else own + (step - 1)
        here = own - step if up else own + step
        sends = (there <= last) & (there >= 0) & (holds >= 0) & (holds <= last)
        waits = (here >= 0) & (here <= last)
        before = step - 1 if up else in_set - (step - 1)
        source = x_ref if step == 1 else from_plane.at[before - 1]
        copy = to_plane(
            source,
            from_plane.at[distance - 1],
            z_send.at[side, step - 1],
            z_recv.at[side, step - 1],
            base + lax.rem(there + in_set, in_set),
        )
        return copy, sends, waits

    def start_hand(step):
        for up in (True, False):
            copy, sends, _ = handed(step, up)
            pl.when(sends)(copy.start)

    def await_hand(step):
        for up in (True, False):
            copy, _, waits = handed(step, up)
            pl.when(waits)(copy.wait_recv)

    def end_hands():
        for step in range(1, in_set):
            for up in (True, False):
                copy, sends, _ = handed(step, up)
                pl.when(sends)(copy.wait_send)

    start_hand(1)
    mine = full_ref.at[pl.ds(pl.multiple_of(plane * depth, depth), depth), pl.ds(0, inner)]
    own_copy = pltpu.make_async_copy(w_ref.at[own], mine, own_sem)
    own_copy.start()

    def sent(step, turn):
        target = lax.rem(me + turn, groups)
        return remote(
            picked.at[step, turn],
            o_ref.at[
                :,
                pl.ds(step * CAP, CAP),
                pl.ds(pl.multiple_of(me * width, width), width),
            ],
            g_send.at[step, turn],
            g_recv.at[step, turn],
            target,
        )

    def work(step):
        block = from_plane.at[step - 1] if step else x_ref

        def choose(target):
            key = key_ref[step, pl.ds(target, 1), :]
            slot = lax.broadcasted_iota(jnp.int32, (CAP, key.shape[1]), 0)
            pick = jnp.where(slot == key, 1.0, 0.0).astype(bf16)
            return jnp.dot(pick, block[...], preferred_element_type=f32).astype(bf16)

        @pl.loop(1, groups)
        def _(turn):
            rows = choose(lax.rem(me + turn, groups))
            picked[step, turn, 0] = rows[:, :width]
            picked[step, turn, 1] = rows[:, width:]
            sent(step, turn).start()

        rows = choose(me)
        columns = pl.ds(pl.multiple_of(me * width, width), width)
        o_ref[0, pl.ds(step * CAP, CAP), columns] = rows[:, :width]
        o_ref[1, pl.ds(step * CAP, CAP), columns] = rows[:, width:]

    for step in range(1, in_set - 1):
        await_hand(step)
        start_hand(step + 1)
    w_copies = []
    for step in range(1, planes):
        target = lax.rem(plane + step, planes)
        copy = to_plane(
            w_ref.at[lax.rem(target, in_set)],
            mine,
            w_send.at[step - 1],
            w_recv.at[step - 1],
            target,
        )
        copy.start()
        w_copies.append(copy)
    work(0)
    await_hand(in_set - 1)
    for step in range(1, in_set):
        work(step)

    for step in range(in_set):

        @pl.loop(1, groups)
        def _(turn, step=step):
            copy = sent(step, turn)
            copy.wait_recv()
            copy.wait_send()

    end_hands()
    own_copy.wait()
    for copy in w_copies:
        copy.wait_recv()
        copy.wait_send()


def spread(x, key, weight, planes, groups, pad_to, collective_id):
    in_set, depth, inner = weight.shape
    rows, two = x.shape
    width = two // 2
    return pl.pallas_call(
        functools.partial(spread_kernel, planes, groups, in_set),
        out_shape=(
            jax.ShapeDtypeStruct((2, in_set * CAP, groups * width), bf16),
            jax.ShapeDtypeStruct((planes * depth, pad_to), bf16),
        ),
        in_specs=[VMEM, VMEM, pl.BlockSpec(memory_space=pl.ANY)],
        out_specs=(VMEM, pl.BlockSpec(memory_space=pl.ANY)),
        scratch_shapes=[
            pltpu.VMEM((in_set - 1, rows, two), bf16),
            pltpu.VMEM((in_set, groups, 2, CAP, width), bf16),
            DMA,
            DMA((planes - 1,)),
            DMA((planes - 1,)),
            DMA((2, in_set - 1)),
            DMA((2, in_set - 1)),
            DMA((in_set, groups)),
            DMA((in_set, groups)),
        ],
        compiler_params=pltpu.CompilerParams(
            collective_id=collective_id, has_side_effects=True, vmem_limit_bytes=48 << 20
        ),
        cost_estimate=SMALL,
    )(x, key, weight)


def experts_kernel(
    planes,
    groups,
    in_set,
    tile,
    names,
    slots_ref,
    w1_ref,
    w2_ref,
    hg_ref,
    hu_ref,
    hd_ref,
    mask_ref,
    mask_down_ref,
    own_ref,
    gain_ref,
    key_ref,
    shard_ref,
    rows_ref,
    placed_ref,
    wide_ref,
    wide_down_ref,
    hg_grad_ref,
    hu_grad_ref,
    hd_grad_ref,
    slot_buf,
    u_stage,
    m_stage,
    got,
    other,
    out_z,
    in_z,
    low,
    slot_sem,
    g_send,
    g_recv,
    m_send,
    m_recv,
    own_sem,
    z_send,
    z_recv,
    c_own,
    c_send,
    c_recv,
    p_send,
    p_recv,
):
    plane, own, base = plane_place(in_set)
    me, chip, core, sibling = place_in_column()
    chips = groups // 2
    rows, width = shard_ref.shape
    hidden = hd_ref.shape[0]
    rank = mask_ref.shape[1]
    order = list(range(1, in_set)) + [0]
    last = in_set - 1

    def columns_of(owner):
        return pl.ds(pl.multiple_of(owner * width, width), width)

    def slots_of(buffer, step, owner):
        return buffer.at[step, pl.ds(pl.multiple_of(owner * CAP, 16), CAP), :]

    def load(index):
        return pltpu.make_async_copy(
            slots_ref.at[:, pl.ds(order[index] * CAP, CAP), :],
            slot_buf.at[index % 2],
            slot_sem.at[index % 2],
        )

    def sent(index, turn, stage, landing, send_sem, recv_sem):
        target = lax.rem(me + turn, groups)
        step = order[index]
        return remote(
            stage.at[index % 2, :, columns_of(target)],
            slots_of(landing, step, me),
            send_sem.at[step, turn],
            recv_sem.at[step, turn],
            target,
        )

    def kept(index, stage, landing, which):
        step = order[index]
        return pltpu.make_async_copy(
            stage.at[index % 2, :, columns_of(me)],
            slots_of(landing, step, me),
            own_sem.at[which, step],
        )

    flows = (
        (u_stage, got, g_send, g_recv, 0),
        (m_stage, other, m_send, m_recv, 1),
    )

    def start_flow(index, flow):
        stage, landing, send_sem, recv_sem, which = flow

        @pl.loop(1, groups)
        def _(turn):
            sent(index, turn, stage, landing, send_sem, recv_sem).start()

        kept(index, stage, landing, which).start()

    def left_flow(index, flow):
        stage, landing, send_sem, recv_sem, which = flow

        @pl.loop(1, groups)
        def _(turn):
            sent(index, turn, stage, landing, send_sem, recv_sem).wait_send()

        if index < last - 1:
            kept(index, stage, landing, which).wait()

    def await_flow(index, flow):
        stage, landing, send_sem, recv_sem, which = flow

        @pl.loop(1, groups)
        def _(turn):
            sent(index, turn, stage, landing, send_sem, recv_sem).wait_recv()

        if index >= last - 1:
            kept(index, stage, landing, which).wait()

    def mul(left, right, over_left, over_right):
        return lax.dot_general(
            left, right, (((over_left,), (over_right,)), ((), ())), preferred_element_type=f32
        )

    def placed(step, row, buffer):
        keys = jnp.transpose(key_ref[step, :, pl.ds(row, tile)])
        pieces = []
        for start in range(0, groups * CAP, 128):
            slot = lax.broadcasted_iota(jnp.int32, (tile, 128), 1) + start
            hit = None
            for owner in range(start // CAP, min(groups, (start + 127) // CAP + 1)):
                same = slot == keys[:, owner : owner + 1]
                hit = same if hit is None else hit | same
            pieces.append(jnp.where(hit, 1.0, 0.0).astype(bf16))
        return jnp.dot(
            jnp.concatenate(pieces, axis=1), buffer[step], preferred_element_type=f32
        )

    def back(step):
        return to_plane(
            out_z.at[step - 1],
            in_z.at[step - 1],
            z_send.at[step - 1],
            z_recv.at[step - 1],
            base + lax.rem(own - step + in_set, in_set),
        )

    def gather_own(index):
        step = order[index]
        await_flow(index, flows[0])

        @pl.loop(0, rows // tile)
        def _(i):
            row = pl.multiple_of(i * tile, tile)
            total = placed(step, row, got)
            if step:
                out_z[step - 1, pl.ds(row, tile), :] = total.astype(bf16)
            else:
                shard_ref[pl.ds(row, tile), :] = total

        if step:
            back(step).start()

    def gather_other(index):
        step = order[index]
        await_flow(index, flows[1])

        @pl.loop(0, rows // tile)
        def _(i):
            row = pl.multiple_of(i * tile, tile)
            placed_ref[step, pl.ds(row, tile), :] = placed(step, row, other).astype(bf16)

    load(0).start()
    load(1).start()
    greet_all(planes, groups)
    lane = lax.broadcasted_iota(jnp.int32, (CAP, 128), 1)
    for index, step in enumerate(order):
        at = pl.ds(step * CAP, CAP)
        load(index).wait()
        middle = slot_buf[index % 2, 0].astype(f32)
        scale = lax.rsqrt(jnp.mean(middle * middle, axis=-1, keepdims=True) + norm_eps)
        expert_in = (middle * scale * gain_ref[...]).astype(bf16)
        pre = mul(expert_in, w1_ref[...], 1, 0)
        both_masks = mask_ref[at, :]
        mask_down = mask_down_ref[at, :]
        valid = jnp.max(mask_down, axis=1, keepdims=True)
        rank_gu = (pre[:, 2 * hidden : 2 * hidden + rank] * both_masks).astype(bf16)
        logits = pre[:, 2 * hidden + rank :]
        first = lane < names // 2
        peak = jnp.max(jnp.where(first, logits, -1e30), axis=1, keepdims=True)
        raised = jnp.exp(jnp.where(lane < names, logits, -1e30) - peak)
        probs = raised / jnp.sum(jnp.where(first, raised, 0.0), axis=1, keepdims=True)
        is_own = own_ref[...]
        gate = jnp.sum(jnp.where(first, probs * is_own, 0.0), axis=1, keepdims=True) * valid
        gate_pre = pre[:, :hidden] + rank_scale * mul(rank_gu, hg_ref[...], 1, 1)
        up_pre = pre[:, hidden : 2 * hidden] + rank_scale * mul(rank_gu, hu_ref[...], 1, 1)
        sigma = 1.0 / (1.0 + jnp.exp(-gate_pre))
        activated = gate_pre * sigma
        inner = (activated * up_pre).astype(bf16)
        rank_down = (mul(inner, hd_ref[...], 1, 0) * mask_down).astype(bf16)
        inner_wide = jnp.concatenate(
            [inner, (down_scale * rank_down.astype(f32)).astype(bf16)], axis=1
        )
        output = mul(inner_wide, w2_ref[...], 1, 1)
        cotangent = slot_buf[index % 2, 1].astype(f32)
        gate_grad = jnp.sum(cotangent * output, axis=1, keepdims=True)
        if index >= 2:
            left_flow(index - 2, flows[1])
            left_flow(index - 2, flows[0])
        m_stage[index % 2] = (gate * output).astype(bf16)
        if index < last:
            start_flow(index, flows[1])
        weighted = (gate * cotangent).astype(bf16)
        inner_grads = mul(weighted, w2_ref[...], 1, 0)
        rank_down_grad = (down_scale * inner_grads[:, hidden:] * mask_down).astype(bf16)
        inner_grad = inner_grads[:, :hidden] + mul(rank_down_grad, hd_ref[...], 1, 1)
        gate_pre_grad = (
            inner_grad * up_pre * sigma * (1.0 + gate_pre * (1.0 - sigma))
        ).astype(bf16)
        up_pre_grad = (inner_grad * activated).astype(bf16)
        rank_gu_grad = (
            rank_scale
            * (mul(gate_pre_grad, hg_ref[...], 1, 0) + mul(up_pre_grad, hu_ref[...], 1, 0))
            * both_masks
        ).astype(bf16)
        logit_grad = (is_own - probs) * (gate * gate_grad)
        logit_high = logit_grad.astype(bf16)
        logit_rest = logit_grad - logit_high.astype(f32)
        logit_two = jnp.where(first, logit_high.astype(f32), logit_rest)
        logit_two = jnp.where(lane < names, logit_two, 0.0).astype(bf16)
        wide = jnp.concatenate([gate_pre_grad, up_pre_grad, rank_gu_grad, logit_two], axis=1)
        u_stage[index % 2] = mul(wide, w1_ref[...], 1, 1).astype(bf16)
        start_flow(index, flows[0])
        if index == last:
            start_flow(index, flows[1])
        if index + 2 <= last:
            load(index + 2).start()

        def add(ref, value):
            if index:
                ref[...] += value
            else:
                ref[...] = value

        add(wide_ref, mul(rank_gu_grad, expert_in, 0, 0))
        add(wide_down_ref, down_scale * mul(rank_down, weighted, 0, 0))
        add(hg_grad_ref, rank_scale * mul(rank_gu, gate_pre_grad, 0, 0))
        add(hu_grad_ref, rank_scale * mul(rank_gu, up_pre_grad, 0, 0))
        add(hd_grad_ref, mul(rank_down_grad, inner, 0, 0))
        if index >= 2:
            gather_own(index - 2)
    for index in range(max(0, last - 1), last):
        gather_own(index)
    for index in range(max(0, last - 1)):
        gather_other(index)
    gather_own(last)
    for step in range(1, in_set):
        back(step).wait_recv()

    @pl.loop(0, rows // tile)
    def _(i):
        row = pl.multiple_of(i * tile, tile)
        total = shard_ref[pl.ds(row, tile), :]
        for step in range(1, in_set):
            total = total + in_z[step - 1, pl.ds(row, tile), :].astype(f32)
        shard_ref[pl.ds(row, tile), :] = total
        low[pl.ds(row, tile), :] = total.astype(bf16)

    def columns(owner):
        return rows_ref.at[:, columns_of(owner)]

    mine = pltpu.make_async_copy(low, columns(me), c_own)
    mine.start()
    out = []
    for step in list(range(1, chips)) + [0]:
        target = sibling if step == 0 else chip_peer(chip, core, step, chips)
        copy = remote(low, columns(me), c_send.at[step], c_recv.at[step], target)
        copy.start()
        out.append(copy)
    for index in range(max(0, last - 1), last + 1):
        gather_other(index)
    for step in range(1, chips):
        out[step - 1].wait_recv()
        source = chip_peer(chip, core, chips - step, chips)
        copy = remote(
            columns(source), columns(source), p_send.at[step], p_recv.at[step], sibling
        )
        copy.start()
        out.append(copy)
    mine.wait()
    out[chips - 1].wait_recv()
    for copy in out[chips:]:
        copy.wait_recv()
    for copy in out:
        copy.wait_send()
    for step in range(1, in_set):
        back(step).wait_send()
    for index in range(max(0, last - 1), last + 1):
        left_flow(index, flows[0])
        left_flow(index, flows[1])


def experts(
    slots, w1, w2, hg, hu, hd, masks, mask_down, own, gain, key, names, planes, groups, collective_id
):
    in_set, rows = key.shape[0], key.shape[2]
    full = slots.shape[2]
    width = full // groups
    chips = groups // 2
    tile = min(256, rows)
    hidden, rank = hg.shape
    down = hd.shape[1]
    anywhere = pl.BlockSpec(memory_space=pl.ANY)
    return pl.pallas_call(
        functools.partial(experts_kernel, planes, groups, in_set, tile, names),
        out_shape=(
            jax.ShapeDtypeStruct((rows, width), f32),
            jax.ShapeDtypeStruct((rows, full), bf16),
            jax.ShapeDtypeStruct((in_set, rows, width), bf16),
            jax.ShapeDtypeStruct((rank, full), f32),
            jax.ShapeDtypeStruct((down, full), f32),
            jax.ShapeDtypeStruct((rank, hidden), f32),
            jax.ShapeDtypeStruct((rank, hidden), f32),
            jax.ShapeDtypeStruct((down, hidden), f32),
        ),
        in_specs=[anywhere] + [VMEM] * 10,
        out_specs=(VMEM, anywhere) + (VMEM,) * 6,
        scratch_shapes=[
            pltpu.VMEM((2, 2, CAP, full), bf16),
            pltpu.VMEM((2, CAP, full), bf16),
            pltpu.VMEM((2, CAP, full), bf16),
            pltpu.VMEM((in_set, groups * CAP, width), bf16),
            pltpu.VMEM((in_set, groups * CAP, width), bf16),
            pltpu.VMEM((in_set - 1, rows, width), bf16),
            pltpu.VMEM((in_set - 1, rows, width), bf16),
            pltpu.VMEM((rows, width), bf16),
            DMA((2,)),
            DMA((in_set, groups)),
            DMA((in_set, groups)),
            DMA((in_set, groups)),
            DMA((in_set, groups)),
            DMA((2, in_set)),
            DMA((in_set - 1,)),
            DMA((in_set - 1,)),
            DMA,
            DMA((chips,)),
            DMA((chips,)),
            DMA((chips,)),
            DMA((chips,)),
        ],
        compiler_params=pltpu.CompilerParams(
            collective_id=collective_id, has_side_effects=True, vmem_limit_bytes=62 << 20
        ),
        cost_estimate=SMALL,
    )(slots, w1, w2, hg, hu, hd, masks, mask_down, own, gain, key)


def planes_kernel(planes, x_ref, o_ref, own_sem, send_sem, recv_sem):
    plane = lax.axis_index("gx")
    barrier = pltpu.get_barrier_semaphore()
    own = pltpu.make_async_copy(x_ref, o_ref.at[plane], own_sem)
    own.start()
    for step in range(1, planes):
        target = lax.rem(plane + step, planes)
        pl.semaphore_signal(barrier, inc=1, device_id={"gx": target}, device_id_type=MESH)
    pl.semaphore_wait(barrier, planes - 1)
    copies = []
    for step in range(1, planes):
        copy = to_plane(
            x_ref,
            o_ref.at[plane],
            send_sem.at[step - 1],
            recv_sem.at[step - 1],
            lax.rem(plane + step, planes),
        )
        copy.start()
        copies.append(copy)
    own.wait()
    for copy in copies:
        copy.wait_recv()
        copy.wait_send()


def gather_planes(x, planes, collective_id):
    return pl.pallas_call(
        functools.partial(planes_kernel, planes),
        out_shape=jax.ShapeDtypeStruct((planes,) + x.shape, x.dtype),
        in_specs=[VMEM],
        out_specs=VMEM,
        scratch_shapes=[DMA, DMA((planes - 1,)), DMA((planes - 1,))],
        compiler_params=pltpu.CompilerParams(collective_id=collective_id, has_side_effects=True),
        cost_estimate=SMALL,
    )(x)


def rope_tables(length, width):
    half_width = width // 2
    frequency = rope_theta ** (-2.0 * jnp.arange(half_width, dtype=f32) / width)
    angles = jnp.arange(length, dtype=f32)[:, None] * frequency[None, :]
    return (jnp.cos(angles), jnp.sin(angles))


def apply_rotary(values, cosine, sine):
    half_width = values.shape[-1] // 2
    first = values[..., :half_width]
    second = values[..., half_width:]
    return jnp.concatenate(
        [first * cosine - second * sine, second * cosine + first * sine], axis=-1
    )


def unrotate(grads, cosine, sine):
    half_width = grads.shape[-1] // 2
    first = grads[..., :half_width]
    second = grads[..., half_width:]
    return jnp.concatenate(
        [first * cosine + second * sine, second * cosine - first * sine], axis=-1
    )


def allowed_mask(piece_starts):
    places = jnp.arange(SEQ, dtype=jnp.int32)
    causal = places[None, :] <= places[:, None]
    inside = (places[None, None, :] >= piece_starts[:, :, None]) & (
        places[None, None, :] < piece_starts[:, :, None] + PIECE
    )
    same_piece = jnp.any(inside[:, :, :, None] & inside[:, :, None, :], axis=1)
    return causal[None] | same_piece


def dot(spec, left, right):
    return jnp.einsum(spec, left, right, preferred_element_type=f32)


def after(first, *later):
    return lax.optimization_barrier((first,) + later)[1:]


def shards(
    block_input,
    out_grad,
    routes,
    adapter_ids,
    piece_starts,
    attn_gain,
    qk_gain,
    mlp_gain,
    w_qkv,
    w_out,
    a_qkv,
    b_out,
    head_pack,
    router,
    w_gate_up,
    w_down,
    exp_wide,
    exp_hidden,
):
    planes = lax.axis_size("gx")
    groups = lax.axis_size("gy")
    plane = lax.axis_index("gx")
    column = lax.axis_index("gy")
    rows, width_local = block_input.shape
    width = width_local * groups
    heads_local = head_pack.shape[0]
    rank_cols = head_pack.shape[2]
    head_width = head_pack.shape[3]
    experts_local = w_gate_up.shape[0]
    hidden_width = w_gate_up.shape[3]
    nseq = adapter_ids.shape[0]
    inv_root = head_width ** (-0.5)
    repeats = planes // experts_local
    steps = range(experts_local)
    own = lax.rem(plane, experts_local)

    def shifted(x, step):
        if step % experts_local == 0:
            return x
        pairs = []
        for p in range(planes):
            base = p // experts_local * experts_local
            pairs.append((p, base + (p - base + step) % experts_local))
        return lax.ppermute(x, "gx", pairs)

    def own_pieces(piece_for):
        pieces = []
        for step in range(planes):
            piece = piece_for(lax.rem(plane + step, planes))
            if step:
                pairs = [(p, (p + step) % planes) for p in range(planes)]
                piece = lax.ppermute(piece, "gx", pairs)
            pieces.append((lax.rem(plane - step + planes, planes), piece))
        return pieces

    def assembled(pieces, buffer, start=0):
        for source, piece in pieces:
            buffer = lax.dynamic_update_slice(buffer, piece, (source * piece.shape[0], start))
        return buffer

    compact = nseq * RANK

    def pick(x, axis):
        return jnp.concatenate(
            [
                lax.dynamic_slice_in_dim(x, adapter_ids[n] * RANK, RANK, axis=axis)
                for n in range(nseq)
            ],
            axis=axis,
        )

    token_seq = jnp.arange(rows, dtype=jnp.int32) // SEQ
    col_seq = jnp.arange(compact, dtype=jnp.int32) // RANK
    compact_mask = (token_seq[:, None] == col_seq[None, :]).astype(f32)
    a_pick = pick(a_qkv, 2)
    b_pick = pick(b_out, 0)
    pack_pick = pick(head_pack, 2)

    top = routes.shape[1]
    whole = jnp.concatenate(
        [routes.reshape(rows * top // 128, 128), jnp.zeros((8, 128), jnp.int32)], axis=0
    )
    whole = lax.dynamic_update_slice(whole, adapter_ids[None, :], (rows * top // 128, 0))
    whole = gather_planes(whole, planes, 10)
    routes_all = whole[:, : rows * top // 128].reshape(planes, rows, top)
    adapters_all = whole[:, rows * top // 128, :nseq]
    dl = w_gate_up.shape[1]
    hl = exp_hidden.shape[1]
    qkv_width = 3 * heads_local * head_width
    weight_shard = jnp.concatenate(
        [
            w_qkv.reshape(w_qkv.shape[0], qkv_width),
            w_out.reshape(heads_local * head_width, w_out.shape[2]).T,
        ],
        axis=1,
    )
    attn_weight = lax.all_gather(weight_shard, "gx", axis=0, tiled=True)
    normed_bf, scale_one, gathered = gather_normed(
        jnp.concatenate(
            [block_input, a_pick.transpose(0, 2, 1).reshape(3 * compact, width_local), b_pick],
            axis=0,
        ),
        attn_gain,
        rows,
        groups,
        1,
    )
    scale_one = scale_one[:, :1]
    a_full = gathered[: 3 * compact]
    b_full = gathered[3 * compact :]

    set_cols = experts_local * compact
    fold = max(1, 128 // set_cols)
    sets_adapters = adapters_all.reshape(repeats, experts_local * nseq)
    rank_index = jnp.arange(rank_cols, dtype=jnp.int32)
    set_index = jnp.arange(set_cols, dtype=jnp.int32)
    set_pick = (
        (rank_index // RANK)[None, :, None] == jnp.repeat(sets_adapters, RANK, axis=1)[:, None, :]
    ) & ((rank_index % RANK)[None, :, None] == (set_index % RANK)[None, None, :])
    set_pick = set_pick.astype(bf16)

    def folded(x):
        return jnp.concatenate(jnp.split(x, fold, axis=1), axis=2)

    def unfolded(x):
        return jnp.concatenate(jnp.split(x, fold, axis=2), axis=1)

    rank_rows = jnp.concatenate(
        [exp_wide[:, :, c] for c in range(3)] + [exp_hidden[:, :, c] for c in range(3)], axis=1
    )
    rank_shard = folded(
        dot("emr,srk->semk", rank_rows, set_pick)
        .reshape(planes, rank_rows.shape[1], set_cols)
        .astype(bf16)
    )
    (rank_shard,) = after(attn_weight, rank_shard)
    rank_weight = unfolded(lax.all_to_all(rank_shard, "gx", 0, 0, tiled=True))
    (down_later,) = after(attn_weight, w_down)
    early_rows = dl * 5 // 8
    early_pieces = own_pieces(
        lambda p: lax.dynamic_slice(
            down_later, (lax.rem(p, experts_local), 0, 0), (1, early_rows, hidden_width)
        )[0]
    )

    def rank_part(start, count):
        return rank_weight[:, start : start + count].reshape(planes * count, set_cols)

    wide_parts = [rank_part(c * dl, dl) for c in range(3)]
    hidden_gate, hidden_up, hidden_down = [rank_part(3 * dl + c * hl, hl) for c in range(3)]
    down_pad = -set_cols % 128
    second_weight = jnp.zeros((width, hidden_width + set_cols + down_pad), bf16)
    second_weight = lax.dynamic_update_slice(second_weight, wide_parts[2], (0, hidden_width))
    expert_ids = own + experts_local * jnp.arange(groups, dtype=jnp.int32)
    set_start = (plane // experts_local) * experts_local
    step_plane = lax.rem(own - jnp.arange(experts_local) + experts_local, experts_local)
    routes_set = routes_all[set_start + step_plane]
    hits = jnp.any(routes_set[:, :, :, None] == expert_ids, axis=2)
    order = jnp.arange(rows, dtype=jnp.int32)
    earlier = (order[None, :] < order[:, None]).astype(bf16)
    places = dot("ts,gsc->gct", earlier, hits.astype(bf16))
    slot_key = jnp.where(hits.transpose(0, 2, 1), places.astype(jnp.int32), -1)
    slots = jnp.arange(CAP, dtype=jnp.int32)
    column_key = slot_key + CAP * jnp.arange(groups, dtype=jnp.int32)[None, :, None]
    column_key = jnp.where(slot_key >= 0, column_key, -1)
    own_key = lax.dynamic_index_in_dim(slot_key, column, 1, keepdims=False)
    own_pick = (own_key[:, None, :] == slots[None, :, None]).astype(bf16)
    rank_mask = (
        (step_plane[:, None] * nseq + token_seq[None, :])[:, :, None]
        == (set_index // RANK)[None, None, :]
    ).astype(bf16)
    slot_total = experts_local * CAP
    mask_slot = dot("gst,gtr->gsr", own_pick, rank_mask).reshape(slot_total, set_cols)

    gate_up_flat = w_gate_up.reshape(experts_local, dl, 2 * hidden_width)
    attn_weight, slot_key, column_key, mask_slot, gate_up_flat = lax.optimization_barrier(
        (attn_weight, slot_key, column_key, mask_slot, gate_up_flat)
    )

    col_start = column * width_local
    first_norm_gain = lax.dynamic_slice_in_dim(attn_gain, col_start, width_local)
    base = dot("td,de->te", normed_bf, attn_weight[:, :qkv_width]).reshape(
        rows, heads_local, 3, head_width
    )
    rank_in = dot("td,kd->tk", normed_bf, a_full).reshape(rows, 3, compact)
    rank_low = (rank_in * compact_mask[:, None, :]).astype(bf16)
    projected = base + rank_scale * dot("tcr,hcre->thce", rank_low, pack_pick[:, :3])
    query_pre = projected[:, :, 0]
    key_pre = projected[:, :, 1]
    value_bf = projected[:, :, 2].astype(bf16)
    square_sums = jnp.stack(
        [jnp.sum(query_pre * query_pre, axis=(1, 2)), jnp.sum(key_pre * key_pre, axis=(1, 2))]
    )
    square_sums = add_small(square_sums.reshape(-1, 128), groups, 2).reshape(2, rows)
    query_scale = lax.rsqrt(square_sums[0] / width + norm_eps)[:, None, None]
    key_scale = lax.rsqrt(square_sums[1] / width + norm_eps)[:, None, None]
    head_start = column * heads_local * head_width
    gains_local = lax.dynamic_slice_in_dim(
        qk_gain, head_start, heads_local * head_width, axis=1
    ).reshape(2, heads_local, head_width)
    query_hat = query_pre * query_scale
    key_hat = key_pre * key_scale
    cosine, sine = rope_tables(SEQ, head_width)
    cosine = cosine[None, :, None, :]
    sine = sine[None, :, None, :]
    query_bf = apply_rotary(
        (query_hat * gains_local[0]).reshape(nseq, SEQ, heads_local, head_width), cosine, sine
    ).astype(bf16)
    key_bf = apply_rotary(
        (key_hat * gains_local[1]).reshape(nseq, SEQ, heads_local, head_width), cosine, sine
    ).astype(bf16)
    values_seq = value_bf.reshape(nseq, SEQ, heads_local, head_width)
    allowed = allowed_mask(piece_starts)[:, None]
    scores = dot("nqhe,nkhe->nhqk", query_bf, key_bf) * inv_root
    scores = jnp.where(allowed, scores, -1e30)
    row_peak = jnp.max(scores, axis=-1, keepdims=True)
    raised = jnp.exp(scores - row_peak)
    row_total = jnp.sum(raised, axis=-1, keepdims=True)
    log_total = row_peak + jnp.log(row_total)
    weights = raised / row_total
    attended = dot("nhqk,nkhe->nqhe", weights.astype(bf16), values_seq)
    attn_bf = attended.reshape(rows, heads_local, head_width).astype(bf16)
    rank_out = dot("the,hre->thr", attn_bf, pack_pick[:, 3])
    rank_out_low = (rank_out * compact_mask[:, None, :]).astype(bf16)
    out_weight = attn_weight[:, qkv_width:]
    b_turned = (rank_scale * b_full.T).astype(bf16)
    branch_left = jnp.concatenate(
        [
            attn_bf.reshape(rows, heads_local * head_width),
            rank_out_low.reshape(rows, heads_local * compact),
        ],
        axis=1,
    )
    branch_left, *early = after(
        query_scale, branch_left, *[piece for _, piece in early_pieces]
    )
    branch, late_pieces = scatter_product(
        branch_left,
        jnp.concatenate([out_weight] + [b_turned] * heads_local, axis=1),
        groups,
        3,
        w_down,
        early_rows,
        planes,
    )
    for (source, _), piece in zip(early_pieces, early):
        second_weight = lax.dynamic_update_slice(second_weight, piece, (source * dl, 0))
    for p in range(planes):
        second_weight = lax.dynamic_update_slice(
            second_weight, late_pieces[p], (p * dl + early_rows, 0)
        )
    middle = block_input.astype(f32) + branch
    middle_low = middle.astype(bf16)

    slot_rows, first_weight = spread(
        jnp.concatenate([middle_low, out_grad], axis=1),
        slot_key,
        gate_up_flat,
        planes,
        groups,
        2 * hidden_width + 2 * set_cols + 128,
        4,
    )
    names = 2 * router.shape[1]
    first_weight = lax.dynamic_update_slice(
        first_weight,
        jnp.pad(
            jnp.concatenate([wide_parts[0], wide_parts[1], router, router], axis=1),
            ((0, 0), (0, 128 - names)),
        ),
        (0, 2 * hidden_width),
    )
    both_rows = lax.all_gather(
        jnp.concatenate([middle_low, out_grad], axis=0), "gy", axis=1, tiled=True
    )
    no_rank = jnp.zeros((hidden_width, set_cols), bf16)
    own_id = column * experts_local + own
    is_own = (jnp.arange(names, dtype=jnp.int32) % router.shape[1] == own_id).astype(f32)
    (
        normed_two_part,
        normed_two_rows,
        moe_planes,
        wide_gu_grad,
        wide_down_grad,
        gate_rank_grad,
        up_rank_grad,
        down_rank_grad,
    ) = experts(
        slot_rows,
        first_weight,
        second_weight,
        jnp.concatenate([hidden_gate, no_rank], axis=1),
        jnp.concatenate([no_rank, hidden_up], axis=1),
        jnp.pad(hidden_down, ((0, 0), (0, down_pad))),
        jnp.concatenate([mask_slot, mask_slot], axis=1),
        jnp.pad(mask_slot, ((0, 0), (0, down_pad))),
        jnp.pad(is_own, (0, 128 - names)).reshape(1, 128),
        mlp_gain.reshape(1, width),
        column_key,
        names,
        planes,
        groups,
        5,
    )
    moe_pieces = [
        shifted(moe_planes[step], experts_local - step) for step in range(1, experts_local)
    ]

    wide_grads = [
        wide_gu_grad[:set_cols],
        wide_gu_grad[set_cols:],
        wide_down_grad[:set_cols],
    ]
    hidden_grads = [
        gate_rank_grad[:set_cols],
        up_rank_grad[set_cols:],
        down_rank_grad[:set_cols],
    ]
    rank_grads = jnp.concatenate(
        [x.astype(bf16).T.reshape(planes, dl, set_cols) for x in wide_grads]
        + [x.astype(bf16).T.reshape(planes, hl, set_cols) for x in hidden_grads],
        axis=1,
    )
    rank_grads = lax.all_to_all(folded(rank_grads), "gx", 0, 0, tiled=True)

    middle_rows = both_rows[:rows].astype(f32)
    grad_rows = both_rows[rows:].astype(f32)
    scale_two = lax.rsqrt(jnp.mean(middle_rows * middle_rows, axis=-1, keepdims=True) + norm_eps)
    normed_two_grad = normed_two_rows.astype(f32)
    hat_two = middle_rows * scale_two
    scaled_two = normed_two_grad * mlp_gain
    stat_two = jnp.mean(scaled_two * hat_two, axis=-1, keepdims=True)
    branch_rows = (grad_rows + scale_two * (scaled_two - hat_two * stat_two)).astype(bf16)
    gain_two_local = lax.dynamic_slice_in_dim(mlp_gain, col_start, width_local)
    middle_grad = out_grad.astype(f32) + scale_two * (
        normed_two_part * gain_two_local - middle_low.astype(f32) * scale_two * stat_two
    )
    rank_out_grad = rank_scale * dot("td,rd->tr", branch_rows, b_full)
    rank_out_bf = (rank_out_grad * compact_mask).astype(bf16)
    pack_out_grad = dot("the,tr->hre", attn_bf, rank_out_bf)
    attention_gradient = dot("td,de->te", branch_rows, out_weight).reshape(
        rows, heads_local, head_width
    ) + dot(
        "tr,hre->the", rank_out_bf, pack_pick[:, 3]
    )
    attn_grad_bf = attention_gradient.reshape(nseq, SEQ, heads_local, head_width).astype(bf16)
    scores_again = dot("nqhe,nkhe->nhqk", query_bf, key_bf) * inv_root
    scores_again = jnp.where(allowed, scores_again, -1e30)
    weights_again = jnp.exp(scores_again - log_total)
    value_grad = dot("nhqk,nqhe->nkhe", weights_again.astype(bf16), attn_grad_bf)
    weight_grad = dot("nqhe,nkhe->nhqk", attn_grad_bf, values_seq)
    row_dot = jnp.sum(weight_grad * weights_again, axis=-1, keepdims=True)
    score_grad = (weights_again * (weight_grad - row_dot)).astype(bf16)
    query_grad = dot("nhqk,nkhe->nqhe", score_grad, key_bf) * inv_root
    key_grad = dot("nhqk,nqhe->nkhe", score_grad, query_bf) * inv_root
    query_hat_grad = (
        unrotate(query_grad, cosine, sine).reshape(rows, heads_local, head_width) * gains_local[0]
    )
    key_hat_grad = (
        unrotate(key_grad, cosine, sine).reshape(rows, heads_local, head_width) * gains_local[1]
    )
    value_pre_grad = value_grad.reshape(rows, heads_local, head_width)
    stat_query = jnp.sum(query_hat_grad * query_hat, axis=(1, 2))
    stat_key = jnp.sum(key_hat_grad * key_hat, axis=(1, 2))

    def rank_terms(values, which):
        return dot("the,hre->rt", values.astype(bf16), pack_pick[:, which])

    sums = jnp.concatenate(
        [
            rank_terms(query_hat_grad, 0),
            rank_terms(key_hat_grad, 1),
            rank_terms(value_pre_grad, 2),
            rank_terms(query_hat, 0),
            rank_terms(key_hat, 1),
            jnp.sum(rank_out_low.astype(f32), axis=1).T,
            jnp.stack([stat_query, stat_key]),
        ],
        axis=0,
    )
    padding = -sums.shape[0] % 32
    sums = add_pairs(jnp.pad(sums.astype(bf16), ((0, padding), (0, 0))), groups, 6)
    first_total = sums[: 3 * compact].reshape(3, compact, rows)
    second_total = sums[3 * compact : 5 * compact].reshape(2, compact, rows)
    mean_qk = sums[6 * compact : 6 * compact + 2] / width
    branch_local = lax.dynamic_slice_in_dim(branch_rows, col_start, width_local, axis=1)
    b_out_sum = rank_scale * dot(
        "rt,td->rd", sums[5 * compact : 6 * compact].astype(bf16), branch_local
    )
    scales_qk = jnp.stack([query_scale[:, 0, 0], key_scale[:, 0, 0]])
    rank_qk = scales_qk[:, None, :] * (first_total[:2] - second_total * mean_qk[:, None, :])
    rank_grad_full = rank_scale * jnp.concatenate([rank_qk, first_total[2:]], axis=0)
    rank_grad_bf = (rank_grad_full * compact_mask.T[None]).astype(bf16)
    query_pre_grad = query_scale * (query_hat_grad - query_hat * mean_qk[0][:, None, None])
    key_pre_grad = key_scale * (key_hat_grad - key_hat * mean_qk[1][:, None, None])
    pre_grad = jnp.stack([query_pre_grad, key_pre_grad, value_pre_grad], axis=2).astype(bf16)
    pack_b_grad = rank_scale * dot("tcr,thce->rhce", rank_low, pre_grad)
    normed_one_grad = scatter_product(
        pre_grad.reshape(rows, qkv_width), attn_weight[:, :qkv_width], groups, 7
    )[0]
    adapter_input_gradient = dot("crt,cdr->td", rank_grad_bf, a_pick)
    first_normalized_shard = block_input.astype(f32) * scale_one
    normed_local_bf = lax.dynamic_slice_in_dim(normed_bf, col_start, width_local, axis=1)
    a_rows_grad = dot("td,crt->rcd", normed_local_bf, rank_grad_bf)
    scaled_one = (normed_one_grad + adapter_input_gradient) * first_norm_gain
    stat_one = jnp.sum(scaled_one * first_normalized_shard, axis=-1)
    stat_one_sum = add_small(stat_one.reshape(-1, 128), groups, 8).reshape(rows, 1)
    input_grad = middle_grad + scale_one * (
        scaled_one - first_normalized_shard * stat_one_sum / width
    )
    rank_grads, *moe_pieces = after(normed_one_grad, rank_grads, *moe_pieces)
    moe_part = moe_planes[0].astype(f32)
    for piece in moe_pieces:
        moe_part = moe_part + piece.astype(f32)
    layer_out = (middle + moe_part).astype(bf16)
    rank_grads = unfolded(rank_grads)
    rank_grads = rank_grads.reshape((repeats, experts_local) + rank_grads.shape[1:])
    wide_sum = jnp.stack(
        [
            dot("semk,srk->emr", rank_grads[:, :, c * dl : (c + 1) * dl], set_pick)
            for c in range(3)
        ],
        axis=2,
    )
    hidden_sum = jnp.stack(
        [
            dot(
                "semk,srk->emr",
                rank_grads[:, :, 3 * dl + c * hl : 3 * dl + (c + 1) * hl],
                set_pick,
            )
            for c in range(3)
        ],
        axis=2,
    )

    pack_grad = jnp.concatenate(
        [
            pack_b_grad.transpose(1, 2, 0, 3),
            pack_out_grad[:, None],
        ],
        axis=1,
    )
    small = jnp.concatenate(
        [
            a_rows_grad.reshape(compact, 3 * width_local),
            b_out_sum,
            pack_grad.transpose(2, 0, 1, 3).reshape(compact, heads_local * 4 * head_width),
        ],
        axis=1,
    )
    small_all = gather_planes(small.astype(bf16), planes, 9)
    small_all = small_all.reshape(planes * compact, small.shape[1])
    row_at = (
        adapters_all[:, :, None] * RANK + jnp.arange(RANK, dtype=jnp.int32)[None, None, :]
    ).reshape(-1)
    put = (jnp.arange(rank_cols, dtype=jnp.int32)[:, None] == row_at[None, :]).astype(bf16)
    small_sum = jnp.dot(put, small_all, preferred_element_type=f32)
    a_end = 3 * width_local
    b_end = a_end + width_local
    a_sum = small_sum[:, :a_end].reshape(rank_cols, 3, width_local).transpose(1, 2, 0)
    b_sum = small_sum[:, a_end:b_end]
    head_sum = small_sum[:, b_end:].reshape(rank_cols, heads_local, 4, head_width)
    head_sum = head_sum.transpose(1, 2, 0, 3)
    return (layer_out, input_grad, a_sum, b_sum, head_sum, wide_sum, hidden_sum)


def solution(mesh):
    return jax.shard_map(
        shards,
        mesh=mesh,
        in_specs=(
            P("gx", "gy"),
            P("gx", "gy"),
            P("gx", None),
            P("gx"),
            P("gx", None),
            P(),
            P(),
            P(),
            P("gx", "gy", None, None),
            P("gy", None, "gx"),
            P(None, "gy", None),
            P(None, "gy"),
            P("gy", None, None, None),
            P(),
            P("gy", "gx", None, None),
            P("gy", "gx", None),
            P("gy", "gx", None, None),
            P("gy", "gx", None, None),
        ),
        out_specs=(
            P("gx", "gy"),
            P("gx", "gy"),
            P(None, "gy", None),
            P(None, "gy"),
            P("gy", None, None, None),
            P("gy", "gx", None, None),
            P("gy", "gx", None, None),
        ),
        check_vma=False,
    )
```

```python
import functools
import jax
import jax.numpy as jnp
from jax import lax
from jax.experimental import pallas as pl
from jax.experimental.pallas import tpu as pltpu
from jax.sharding import PartitionSpec as P

RANK = 16
SEQ = 1024
PIECE = 256
CAP = 288


norm_eps = 1e-05
rope_theta = 10000.0
rank_scale = 0.5
down_scale = 4.0
bf16 = jnp.bfloat16
f32 = jnp.float32
VMEM = pl.BlockSpec(memory_space=pltpu.VMEM)
DMA = pltpu.SemaphoreType.DMA
MESH = pl.DeviceIdType.MESH
SMALL = pl.CostEstimate(flops=0, bytes_accessed=1 << 16, transcendentals=0)
CAP = 288
SMALL = pl.CostEstimate(flops=0, bytes_accessed=1 << 16, transcendentals=0)


def place_in_column():
    me = lax.axis_index("gy")
    chip, core = lax.div(me, 2), lax.rem(me, 2)
    return me, chip, core, me + 1 - 2 * core


def chip_peer(chip, core, step, chips):
    return lax.rem(chip + step, chips) * 2 + core


def greet_chips(chip, core, sibling, chips, planes=1):
    barrier = pltpu.get_barrier_semaphore()
    for step in range(1, planes):
        target = lax.rem(lax.axis_index("gx") + step, planes)
        pl.semaphore_signal(barrier, inc=1, device_id={"gx": target}, device_id_type=MESH)
    pl.semaphore_signal(barrier, inc=1, device_id={"gy": sibling}, device_id_type=MESH)
    for step in range(1, chips):
        pl.semaphore_signal(
            barrier,
            inc=1,
            device_id={"gy": chip_peer(chip, core, step, chips)},
            device_id_type=MESH,
        )
    pl.semaphore_wait(barrier, chips + planes - 1)


def remote(src, dst, send_sem, recv_sem, target):
    return pltpu.make_async_remote_copy(
        src_ref=src,
        dst_ref=dst,
        send_sem=send_sem,
        recv_sem=recv_sem,
        device_id={"gy": target},
        device_id_type=MESH,
    )


def gather_kernel(
    chips,
    rows,
    tile,
    x_ref,
    gain_ref,
    normed_ref,
    scale_ref,
    rest_ref,
    whole,
    own_sem,
    send_sem,
    recv_sem,
    pass_sem,
    passed_sem,
):
    me, chip, core, sibling = place_in_column()
    width = x_ref.shape[1]

    def columns(owner):
        return whole.at[:, pl.ds(pl.multiple_of(owner * width, width), width)]

    own = pltpu.make_async_copy(x_ref, columns(me), own_sem)
    own.start()
    greet_chips(chip, core, sibling, chips)
    out = []
    for step in list(range(1, chips)) + [0]:
        target = sibling if step == 0 else chip_peer(chip, core, step, chips)
        copy = remote(x_ref, columns(me), send_sem.at[step], recv_sem.at[step], target)
        copy.start()
        out.append(copy)
    for step in range(1, chips):
        out[step - 1].wait_recv()
        source = chip_peer(chip, core, chips - step, chips)
        copy = remote(
            columns(source), columns(source), pass_sem.at[step], passed_sem.at[step], sibling
        )
        copy.start()
        out.append(copy)
    own.wait()
    out[chips - 1].wait_recv()
    for copy in out[chips:]:
        copy.wait_recv()

    @pl.loop(0, rows // tile)
    def _(i):
        at = pl.ds(pl.multiple_of(i * tile, tile), tile)
        values = whole[at, :].astype(f32)
        scale = lax.rsqrt(jnp.mean(values * values, axis=-1, keepdims=True) + norm_eps)
        scale_ref[at, :] = jnp.broadcast_to(scale, (tile, 128))
        normed_ref[at, :] = (values * scale * gain_ref[...]).astype(bf16)

    rest_ref[...] = whole[pl.ds(rows, rest_ref.shape[0]), :]
    for copy in out:
        copy.wait_send()


def gather_normed(x, gain, rows, groups, collective_id):
    chips = groups // 2
    total, width = x.shape
    full = groups * width
    return pl.pallas_call(
        functools.partial(gather_kernel, chips, rows, 64),
        out_shape=(
            jax.ShapeDtypeStruct((rows, full), bf16),
            jax.ShapeDtypeStruct((rows, 128), f32),
            jax.ShapeDtypeStruct((total - rows, full), bf16),
        ),
        in_specs=[VMEM, VMEM],
        out_specs=(VMEM, VMEM, VMEM),
        scratch_shapes=[
            pltpu.VMEM((total, full), bf16),
            DMA,
            DMA((chips,)),
            DMA((chips,)),
            DMA((chips,)),
            DMA((chips,)),
        ],
        compiler_params=pltpu.CompilerParams(
            collective_id=collective_id, has_side_effects=True, vmem_limit_bytes=48 << 20
        ),
        cost_estimate=SMALL,
    )(x, gain.reshape(1, full))


def scatter_and_carry_kernel(
    planes, first, chips, tile, l_ref, r_ref, w_ref, o_ref, w_out, *rest
):
    *scratch, w_own, w_send, w_recv = rest
    plane = lax.axis_index("gx")
    in_set, count = w_ref.shape[0], w_out.shape[1]

    def piece(target):
        return w_ref.at[lax.rem(target, in_set), pl.ds(first, count), :]

    def carry():
        own = pltpu.make_async_copy(piece(plane), w_out.at[plane], w_own)
        own.start()
        copies = []
        for step in range(1, planes):
            target = lax.rem(plane + step, planes)
            copy = to_plane(
                piece(target), w_out.at[plane], w_send.at[step - 1], w_recv.at[step - 1], target
            )
            copy.start()
            copies.append(copy)
        return own, copies

    own, copies = scatter_kernel(
        chips, tile, l_ref, r_ref, o_ref, *scratch, planes=planes, after_greeting=carry
    )
    own.wait()
    for copy in copies:
        copy.wait_recv()
        copy.wait_send()


def scatter_kernel(
    chips,
    tile,
    l_ref,
    r_ref,
    o_ref,
    part,
    got,
    pair,
    far,
    part_s,
    got_s,
    pair_s,
    far_s,
    planes=1,
    after_greeting=None,
):
    me, chip, core, sibling = place_in_column()
    rows, width = o_ref.shape
    greet_chips(chip, core, sibling, chips, planes)
    carried = after_greeting() if after_greeting else None
    steps = list(range(1, chips)) + [0]

    def product(owner, row):
        chunk = r_ref[pl.ds(pl.multiple_of(owner * width, width), width), :]
        return lax.dot_general(
            l_ref[pl.ds(row, tile), :],
            chunk,
            (((1,), (1,)), ((), ())),
            preferred_element_type=f32,
        )

    copies = []
    for step in steps:
        owner = chip_peer(chip, 1 - core, step, chips)

        @pl.loop(0, rows // tile)
        def _(i, owner=owner, step=step):
            row = pl.multiple_of(i * tile, tile)
            part[step, pl.ds(row, tile), :] = product(owner, row).astype(bf16)

        copy = remote(part.at[step], got.at[step], part_s.at[step], got_s.at[step], sibling)
        copy.start()
        copies.append(copy)
    for step in steps:
        owner = chip_peer(chip, core, step, chips)
        copies[steps.index(step)].wait_recv()

        @pl.loop(0, rows // tile)
        def _(i, owner=owner, step=step):
            row = pl.multiple_of(i * tile, tile)
            total = product(owner, row) + got[step, pl.ds(row, tile), :].astype(f32)
            if step == 0:
                o_ref[pl.ds(row, tile), :] = total
            else:
                pair[step - 1, pl.ds(row, tile), :] = total.astype(bf16)

        if step > 0:
            copy = remote(
                pair.at[step - 1], far.at[step - 1], pair_s.at[step - 1], far_s.at[step - 1], owner
            )
            copy.start()
            copies.append(copy)
    for step in range(1, chips):
        copies[chips + step - 1].wait_recv()

        @pl.loop(0, rows // tile)
        def _(i, step=step):
            row = pl.multiple_of(i * tile, tile)
            o_ref[pl.ds(row, tile), :] += far[step - 1, pl.ds(row, tile), :].astype(f32)

    for copy in copies:
        copy.wait_send()
    return carried


def scatter_product(left, right, groups, collective_id, weight=None, first=0, planes=1):
    chips = groups // 2
    rows, inner = left.shape
    width = right.shape[0] // groups
    tile = min(256, rows)
    body = functools.partial(scatter_kernel, chips, tile)
    out_shape = (jax.ShapeDtypeStruct((rows, width), f32),)
    in_specs, out_specs = [VMEM, VMEM], (VMEM,)
    scratch = [
        pltpu.VMEM((chips, rows, width), bf16),
        pltpu.VMEM((chips, rows, width), bf16),
        pltpu.VMEM((chips - 1, rows, width), bf16),
        pltpu.VMEM((chips - 1, rows, width), bf16),
        DMA((chips,)),
        DMA((chips,)),
        DMA((chips - 1,)),
        DMA((chips - 1,)),
    ]
    operands = (left, right)
    if weight is not None:
        body = functools.partial(scatter_and_carry_kernel, planes, first, chips, tile)
        carried = (planes, weight.shape[1] - first, weight.shape[2])
        out_shape += (jax.ShapeDtypeStruct(carried, bf16),)
        in_specs = in_specs + [pl.BlockSpec(memory_space=pl.ANY)]
        out_specs += (pl.BlockSpec(memory_space=pl.ANY),)
        scratch = scratch + [DMA, DMA((planes - 1,)), DMA((planes - 1,))]
        operands += (weight,)
    return pl.pallas_call(
        body,
        out_shape=out_shape,
        in_specs=in_specs,
        out_specs=out_specs,
        scratch_shapes=scratch,
        compiler_params=pltpu.CompilerParams(
            collective_id=collective_id, has_side_effects=True, vmem_limit_bytes=48 << 20
        ),
        cost_estimate=SMALL,
    )(*operands)


def add_kernel(groups, x_ref, o_ref, got, send_sem, recv_sem):
    me = lax.axis_index("gy")
    barrier = pltpu.get_barrier_semaphore()
    for step in range(1, groups):
        target = lax.rem(me + step, groups)
        pl.semaphore_signal(barrier, inc=1, device_id={"gy": target}, device_id_type=MESH)
    pl.semaphore_wait(barrier, groups - 1)
    copies = []
    for step in range(1, groups):
        target = lax.rem(me + step, groups)
        copy = remote(
            x_ref, got.at[step - 1], send_sem.at[step - 1], recv_sem.at[step - 1], target
        )
        copy.start()
        copies.append(copy)
    total = x_ref[...]
    for step in range(1, groups):
        copies[step - 1].wait_recv()
        total = total + got[step - 1]
    o_ref[...] = total
    for copy in copies:
        copy.wait_send()


def add_small(x, groups, collective_id):
    return pl.pallas_call(
        functools.partial(add_kernel, groups),
        out_shape=jax.ShapeDtypeStruct(x.shape, f32),
        in_specs=[VMEM],
        out_specs=VMEM,
        scratch_shapes=[
            pltpu.VMEM((groups - 1,) + x.shape, f32),
            DMA((groups - 1,)),
            DMA((groups - 1,)),
        ],
        compiler_params=pltpu.CompilerParams(collective_id=collective_id, has_side_effects=True),
        cost_estimate=SMALL,
    )(x)


def add_pairs_kernel(
    chips, x_ref, o_ref, got, pair, far, done, got_s, far_s, done_s
):
    me, chip, core, sibling = place_in_column()
    half = x_ref.shape[0] // 2
    greet_chips(chip, core, sibling, chips)
    first = remote(x_ref, got, got_s.at[0], got_s.at[1], sibling)
    first.start()
    first.wait_recv()
    own = pl.ds(pl.multiple_of(core * half, 16), half)
    total = x_ref[own, :].astype(f32) + got[own, :].astype(f32)
    pair[...] = total.astype(bf16)
    copies = []
    for step in range(1, chips):
        copy = remote(
            pair,
            far.at[step - 1],
            far_s.at[0, step - 1],
            far_s.at[1, step - 1],
            chip_peer(chip, core, step, chips),
        )
        copy.start()
        copies.append(copy)
    for step in range(1, chips):
        copies[step - 1].wait_recv()
        total = total + far[step - 1].astype(f32)
    done[own, :] = total.astype(bf16)
    last = remote(done.at[own, :], done.at[own, :], done_s.at[0], done_s.at[1], sibling)
    last.start()
    last.wait_recv()
    o_ref[...] = done[...].astype(f32)
    first.wait_send()
    for copy in copies:
        copy.wait_send()
    last.wait_send()


def add_pairs(x, groups, collective_id):
    chips = groups // 2
    rows, width = x.shape
    return pl.pallas_call(
        functools.partial(add_pairs_kernel, chips),
        out_shape=jax.ShapeDtypeStruct(x.shape, f32),
        in_specs=[VMEM],
        out_specs=VMEM,
        scratch_shapes=[
            pltpu.VMEM(x.shape, bf16),
            pltpu.VMEM((rows // 2, width), bf16),
            pltpu.VMEM((chips - 1, rows // 2, width), bf16),
            pltpu.VMEM(x.shape, bf16),
            DMA((2,)),
            DMA((2, chips - 1)),
            DMA((2,)),
        ],
        compiler_params=pltpu.CompilerParams(collective_id=collective_id, has_side_effects=True),
        cost_estimate=SMALL,
    )(x)


def plane_place(planes_in_set):
    plane = lax.axis_index("gx")
    own = lax.rem(plane, planes_in_set)
    return plane, own, plane - own


def to_plane(src, dst, send_sem, recv_sem, target):
    return pltpu.make_async_remote_copy(
        src_ref=src,
        dst_ref=dst,
        send_sem=send_sem,
        recv_sem=recv_sem,
        device_id={"gx": target},
        device_id_type=MESH,
    )


def greet_all(planes, groups):
    barrier = pltpu.get_barrier_semaphore()
    plane, me = lax.axis_index("gx"), lax.axis_index("gy")

    @pl.loop(1, planes)
    def _(step):
        target = lax.rem(plane + step, planes)
        pl.semaphore_signal(barrier, inc=1, device_id={"gx": target}, device_id_type=MESH)

    @pl.loop(1, groups)
    def _(step):
        target = lax.rem(me + step, groups)
        pl.semaphore_signal(barrier, inc=1, device_id={"gy": target}, device_id_type=MESH)

    pl.semaphore_wait(barrier, planes + groups - 2)


def spread_kernel(
    planes,
    groups,
    in_set,
    x_ref,
    key_ref,
    w_ref,
    o_ref,
    full_ref,
    from_plane,
    picked,
    own_sem,
    w_send,
    w_recv,
    z_send,
    z_recv,
    g_send,
    g_recv,
):
    plane, own, base = plane_place(in_set)
    me = lax.axis_index("gy")
    width = x_ref.shape[1] // 2
    depth, inner = w_ref.shape[1], w_ref.shape[2]
    greet_all(planes, groups)
    last = in_set - 1

    def handed(step, up):
        side = 0 if up else 1
        distance = step if up else in_set - step
        there = own + (1 if up else -1)
        holds = own - (step - 1) if up else own + (step - 1)
        here = own - step if up else own + step
        sends = (there <= last) & (there >= 0) & (holds >= 0) & (holds <= last)
        waits = (here >= 0) & (here <= last)
        before = step - 1 if up else in_set - (step - 1)
        source = x_ref if step == 1 else from_plane.at[before - 1]
        copy = to_plane(
            source,
            from_plane.at[distance - 1],
            z_send.at[side, step - 1],
            z_recv.at[side, step - 1],
            base + lax.rem(there + in_set, in_set),
        )
        return copy, sends, waits

    def start_hand(step):
        for up in (True, False):
            copy, sends, _ = handed(step, up)
            pl.when(sends)(copy.start)

    def await_hand(step):
        for up in (True, False):
            copy, _, waits = handed(step, up)
            pl.when(waits)(copy.wait_recv)

    def end_hands():
        for step in range(1, in_set):
            for up in (True, False):
                copy, sends, _ = handed(step, up)
                pl.when(sends)(copy.wait_send)

    start_hand(1)
    mine = full_ref.at[pl.ds(pl.multiple_of(plane * depth, depth), depth), pl.ds(0, inner)]
    own_copy = pltpu.make_async_copy(w_ref.at[own], mine, own_sem)
    own_copy.start()

    def sent(step, turn):
        target = lax.rem(me + turn, groups)
        return remote(
            picked.at[step, turn],
            o_ref.at[
                :,
                pl.ds(step * CAP, CAP),
                pl.ds(pl.multiple_of(me * width, width), width),
            ],
            g_send.at[step, turn],
            g_recv.at[step, turn],
            target,
        )

    def work(step):
        block = from_plane.at[step - 1] if step else x_ref

        def choose(target):
            key = key_ref[step, pl.ds(target, 1), :]
            slot = lax.broadcasted_iota(jnp.int32, (CAP, key.shape[1]), 0)
            pick = jnp.where(slot == key, 1.0, 0.0).astype(bf16)
            return jnp.dot(pick, block[...], preferred_element_type=f32).astype(bf16)

        @pl.loop(1, groups)
        def _(turn):
            rows = choose(lax.rem(me + turn, groups))
            picked[step, turn, 0] = rows[:, :width]
            picked[step, turn, 1] = rows[:, width:]
            sent(step, turn).start()

        rows = choose(me)
        columns = pl.ds(pl.multiple_of(me * width, width), width)
        o_ref[0, pl.ds(step * CAP, CAP), columns] = rows[:, :width]
        o_ref[1, pl.ds(step * CAP, CAP), columns] = rows[:, width:]

    for step in range(1, in_set - 1):
        await_hand(step)
        start_hand(step + 1)
    w_copies = []
    for step in range(1, planes):
        target = lax.rem(plane + step, planes)
        copy = to_plane(
            w_ref.at[lax.rem(target, in_set)],
            mine,
            w_send.at[step - 1],
            w_recv.at[step - 1],
            target,
        )
        copy.start()
        w_copies.append(copy)
    work(0)
    await_hand(in_set - 1)
    for step in range(1, in_set):
        work(step)

    for step in range(in_set):

        @pl.loop(1, groups)
        def _(turn, step=step):
            copy = sent(step, turn)
            copy.wait_recv()
            copy.wait_send()

    end_hands()
    own_copy.wait()
    for copy in w_copies:
        copy.wait_recv()
        copy.wait_send()


def spread(x, key, weight, planes, groups, pad_to, collective_id):
    in_set, depth, inner = weight.shape
    rows, two = x.shape
    width = two // 2
    return pl.pallas_call(
        functools.partial(spread_kernel, planes, groups, in_set),
        out_shape=(
            jax.ShapeDtypeStruct((2, in_set * CAP, groups * width), bf16),
            jax.ShapeDtypeStruct((planes * depth, pad_to), bf16),
        ),
        in_specs=[VMEM, VMEM, pl.BlockSpec(memory_space=pl.ANY)],
        out_specs=(VMEM, pl.BlockSpec(memory_space=pl.ANY)),
        scratch_shapes=[
            pltpu.VMEM((in_set - 1, rows, two), bf16),
            pltpu.VMEM((in_set, groups, 2, CAP, width), bf16),
            DMA,
            DMA((planes - 1,)),
            DMA((planes - 1,)),
            DMA((2, in_set - 1)),
            DMA((2, in_set - 1)),
            DMA((in_set, groups)),
            DMA((in_set, groups)),
        ],
        compiler_params=pltpu.CompilerParams(
            collective_id=collective_id, has_side_effects=True, vmem_limit_bytes=48 << 20
        ),
        cost_estimate=SMALL,
    )(x, key, weight)


def experts_kernel(
    planes,
    groups,
    in_set,
    tile,
    names,
    slots_ref,
    w1_main_ref,
    w1_tail_ref,
    late_ref,
    w2_tail_ref,
    hg_ref,
    hu_ref,
    hd_ref,
    mask_ref,
    mask_down_ref,
    own_ref,
    gain_ref,
    key_ref,
    *rest,
):
    early_refs = rest[:planes]
    (
        shard_ref,
        rows_ref,
        placed_ref,
        wide_ref,
        wide_down_ref,
        hg_grad_ref,
        hu_grad_ref,
        hd_grad_ref,
        w1_ref,
        w2_ref,
        slot_buf,
        u_stage,
        m_stage,
        got,
        other,
        out_z,
        in_z,
        low,
        w1_sem,
        w2_sem,
        slot_sem,
        g_send,
        g_recv,
        m_send,
        m_recv,
        own_sem,
        z_send,
        z_recv,
        c_own,
        c_send,
        c_recv,
        p_send,
        p_recv,
    ) = rest[planes:]
    plane, own, base = plane_place(in_set)
    me, chip, core, sibling = place_in_column()
    chips = groups // 2
    rows, width = shard_ref.shape
    hidden = hd_ref.shape[0]
    rank = mask_ref.shape[1]
    order = list(range(1, in_set)) + [0]
    last = in_set - 1

    def columns_of(owner):
        return pl.ds(pl.multiple_of(owner * width, width), width)

    def slots_of(buffer, step, owner):
        return buffer.at[step, pl.ds(pl.multiple_of(owner * CAP, 16), CAP), :]

    def load(index):
        return pltpu.make_async_copy(
            slots_ref.at[:, pl.ds(order[index] * CAP, CAP), :],
            slot_buf.at[index % 2],
            slot_sem.at[index % 2],
        )

    def sent(index, turn, stage, landing, send_sem, recv_sem):
        target = lax.rem(me + turn, groups)
        step = order[index]
        return remote(
            stage.at[index % 2, :, columns_of(target)],
            slots_of(landing, step, me),
            send_sem.at[step, turn],
            recv_sem.at[step, turn],
            target,
        )

    def kept(index, stage, landing, which):
        step = order[index]
        return pltpu.make_async_copy(
            stage.at[index % 2, :, columns_of(me)],
            slots_of(landing, step, me),
            own_sem.at[which, step],
        )

    flows = (
        (u_stage, got, g_send, g_recv, 0),
        (m_stage, other, m_send, m_recv, 1),
    )

    def start_flow(index, flow):
        stage, landing, send_sem, recv_sem, which = flow

        @pl.loop(1, groups)
        def _(turn):
            sent(index, turn, stage, landing, send_sem, recv_sem).start()

        kept(index, stage, landing, which).start()

    def left_flow(index, flow):
        stage, landing, send_sem, recv_sem, which = flow

        @pl.loop(1, groups)
        def _(turn):
            sent(index, turn, stage, landing, send_sem, recv_sem).wait_send()

        if index < last - 1:
            kept(index, stage, landing, which).wait()

    def await_flow(index, flow):
        stage, landing, send_sem, recv_sem, which = flow

        @pl.loop(1, groups)
        def _(turn):
            sent(index, turn, stage, landing, send_sem, recv_sem).wait_recv()

        if index >= last - 1:
            kept(index, stage, landing, which).wait()

    def mul(left, right, over_left, over_right):
        return lax.dot_general(
            left, right, (((over_left,), (over_right,)), ((), ())), preferred_element_type=f32
        )

    def placed(step, row, buffer):
        keys = jnp.transpose(key_ref[step, :, pl.ds(row, tile)])
        pieces = []
        for start in range(0, groups * CAP, 128):
            slot = lax.broadcasted_iota(jnp.int32, (tile, 128), 1) + start
            hit = None
            for owner in range(start // CAP, min(groups, (start + 127) // CAP + 1)):
                same = slot == keys[:, owner : owner + 1]
                hit = same if hit is None else hit | same
            pieces.append(jnp.where(hit, 1.0, 0.0).astype(bf16))
        return jnp.dot(
            jnp.concatenate(pieces, axis=1), buffer[step], preferred_element_type=f32
        )

    def back(step):
        return to_plane(
            out_z.at[step - 1],
            in_z.at[step - 1],
            z_send.at[step - 1],
            z_recv.at[step - 1],
            base + lax.rem(own - step + in_set, in_set),
        )

    def gather_own(index):
        step = order[index]
        await_flow(index, flows[0])

        @pl.loop(0, rows // tile)
        def _(i):
            row = pl.multiple_of(i * tile, tile)
            total = placed(step, row, got)
            if step:
                out_z[step - 1, pl.ds(row, tile), :] = total.astype(bf16)
            else:
                shard_ref[pl.ds(row, tile), :] = total

        if step:
            back(step).start()

    def gather_other(index):
        step = order[index]
        await_flow(index, flows[1])

        @pl.loop(0, rows // tile)
        def _(i):
            row = pl.multiple_of(i * tile, tile)
            placed_ref[step, pl.ds(row, tile), :] = placed(step, row, other).astype(bf16)

    load(0).start()
    load(1).start()
    first_cols = w1_main_ref.shape[1]
    w1_loads = [
        pltpu.make_async_copy(w1_main_ref, w1_ref.at[:, pl.ds(0, first_cols)], w1_sem.at[0]),
        pltpu.make_async_copy(
            w1_tail_ref,
            w1_ref.at[:, pl.ds(first_cols, w1_tail_ref.shape[1])],
            w1_sem.at[1],
        ),
    ]
    early_rows, late_rows = early_refs[0].shape[0], late_ref.shape[1]
    depth = early_rows + late_rows
    w2_loads = [
        pltpu.make_async_copy(
            w2_tail_ref, w2_ref.at[:, pl.ds(hidden, w2_tail_ref.shape[1])], w2_sem.at[2 * planes]
        )
    ]
    for number in range(planes):
        source = lax.rem(plane - number + planes, planes)
        w2_loads.append(
            pltpu.make_async_copy(
                early_refs[number],
                w2_ref.at[
                    pl.ds(pl.multiple_of(source * depth, 16), early_rows), pl.ds(0, hidden)
                ],
                w2_sem.at[number],
            )
        )
        w2_loads.append(
            pltpu.make_async_copy(
                late_ref.at[number],
                w2_ref.at[pl.ds(number * depth + early_rows, late_rows), pl.ds(0, hidden)],
                w2_sem.at[planes + number],
            )
        )
    for copy in w1_loads + w2_loads:
        copy.start()
    greet_all(planes, groups)
    lane = lax.broadcasted_iota(jnp.int32, (CAP, 128), 1)
    for index, step in enumerate(order):
        at = pl.ds(step * CAP, CAP)
        load(index).wait()
        middle = slot_buf[index % 2, 0].astype(f32)
        scale = lax.rsqrt(jnp.mean(middle * middle, axis=-1, keepdims=True) + norm_eps)
        expert_in = (middle * scale * gain_ref[...]).astype(bf16)
        if index == 0:
            for copy in w1_loads:
                copy.wait()
        pre = mul(expert_in, w1_ref[...], 1, 0)
        both_masks = mask_ref[at, :]
        mask_down = mask_down_ref[at, :]
        valid = jnp.max(mask_down, axis=1, keepdims=True)
        rank_gu = (pre[:, 2 * hidden : 2 * hidden + rank] * both_masks).astype(bf16)
        logits = pre[:, 2 * hidden + rank :]
        first = lane < names // 2
        peak = jnp.max(jnp.where(first, logits, -1e30), axis=1, keepdims=True)
        raised = jnp.exp(jnp.where(lane < names, logits, -1e30) - peak)
        probs = raised / jnp.sum(jnp.where(first, raised, 0.0), axis=1, keepdims=True)
        is_own = own_ref[...]
        gate = jnp.sum(jnp.where(first, probs * is_own, 0.0), axis=1, keepdims=True) * valid
        gate_pre = pre[:, :hidden] + rank_scale * mul(rank_gu, hg_ref[...], 1, 1)
        up_pre = pre[:, hidden : 2 * hidden] + rank_scale * mul(rank_gu, hu_ref[...], 1, 1)
        sigma = 1.0 / (1.0 + jnp.exp(-gate_pre))
        activated = gate_pre * sigma
        inner = (activated * up_pre).astype(bf16)
        rank_down = (mul(inner, hd_ref[...], 1, 0) * mask_down).astype(bf16)
        inner_wide = jnp.concatenate(
            [inner, (down_scale * rank_down.astype(f32)).astype(bf16)], axis=1
        )
        if index == 0:
            for copy in w2_loads:
                copy.wait()
        output = mul(inner_wide, w2_ref[...], 1, 1)
        cotangent = slot_buf[index % 2, 1].astype(f32)
        gate_grad = jnp.sum(cotangent * output, axis=1, keepdims=True)
        if index >= 2:
            left_flow(index - 2, flows[1])
            left_flow(index - 2, flows[0])
        m_stage[index % 2] = (gate * output).astype(bf16)
        if index < last:
            start_flow(index, flows[1])
        weighted = (gate * cotangent).astype(bf16)
        inner_grads = mul(weighted, w2_ref[...], 1, 0)
        rank_down_grad = (down_scale * inner_grads[:, hidden:] * mask_down).astype(bf16)
        inner_grad = inner_grads[:, :hidden] + mul(rank_down_grad, hd_ref[...], 1, 1)
        gate_pre_grad = (
            inner_grad * up_pre * sigma * (1.0 + gate_pre * (1.0 - sigma))
        ).astype(bf16)
        up_pre_grad = (inner_grad * activated).astype(bf16)
        rank_gu_grad = (
            rank_scale
            * (mul(gate_pre_grad, hg_ref[...], 1, 0) + mul(up_pre_grad, hu_ref[...], 1, 0))
            * both_masks
        ).astype(bf16)
        logit_grad = (is_own - probs) * (gate * gate_grad)
        logit_high = logit_grad.astype(bf16)
        logit_rest = logit_grad - logit_high.astype(f32)
        logit_two = jnp.where(first, logit_high.astype(f32), logit_rest)
        logit_two = jnp.where(lane < names, logit_two, 0.0).astype(bf16)
        wide = jnp.concatenate([gate_pre_grad, up_pre_grad, rank_gu_grad, logit_two], axis=1)
        u_stage[index % 2] = mul(wide, w1_ref[...], 1, 1).astype(bf16)
        start_flow(index, flows[0])
        if index == last:
            start_flow(index, flows[1])
        if index + 2 <= last:
            load(index + 2).start()

        def add(ref, value):
            if index:
                ref[...] += value
            else:
                ref[...] = value

        add(wide_ref, mul(rank_gu_grad, expert_in, 0, 0))
        add(wide_down_ref, down_scale * mul(rank_down, weighted, 0, 0))
        add(hg_grad_ref, rank_scale * mul(rank_gu, gate_pre_grad, 0, 0))
        add(hu_grad_ref, rank_scale * mul(rank_gu, up_pre_grad, 0, 0))
        add(hd_grad_ref, mul(rank_down_grad, inner, 0, 0))
        if index >= 2:
            gather_own(index - 2)
    for index in range(max(0, last - 1), last):
        gather_own(index)
    for index in range(max(0, last - 1)):
        gather_other(index)
    gather_own(last)
    for step in range(1, in_set):
        back(step).wait_recv()

    @pl.loop(0, rows // tile)
    def _(i):
        row = pl.multiple_of(i * tile, tile)
        total = shard_ref[pl.ds(row, tile), :]
        for step in range(1, in_set):
            total = total + in_z[step - 1, pl.ds(row, tile), :].astype(f32)
        shard_ref[pl.ds(row, tile), :] = total
        low[pl.ds(row, tile), :] = total.astype(bf16)

    def columns(owner):
        return rows_ref.at[:, columns_of(owner)]

    mine = pltpu.make_async_copy(low, columns(me), c_own)
    mine.start()
    out = []
    for step in list(range(1, chips)) + [0]:
        target = sibling if step == 0 else chip_peer(chip, core, step, chips)
        copy = remote(low, columns(me), c_send.at[step], c_recv.at[step], target)
        copy.start()
        out.append(copy)
    for index in range(max(0, last - 1), last + 1):
        gather_other(index)
    for step in range(1, chips):
        out[step - 1].wait_recv()
        source = chip_peer(chip, core, chips - step, chips)
        copy = remote(
            columns(source), columns(source), p_send.at[step], p_recv.at[step], sibling
        )
        copy.start()
        out.append(copy)
    mine.wait()
    out[chips - 1].wait_recv()
    for copy in out[chips:]:
        copy.wait_recv()
    for copy in out:
        copy.wait_send()
    for step in range(1, in_set):
        back(step).wait_send()
    for index in range(max(0, last - 1), last + 1):
        left_flow(index, flows[0])
        left_flow(index, flows[1])


def experts(
    slots,
    w1_main,
    w1_tail,
    early,
    late,
    w2_tail,
    hg,
    hu,
    hd,
    masks,
    mask_down,
    own,
    gain,
    key,
    names,
    planes,
    groups,
    collective_id,
):
    in_set, rows = key.shape[0], key.shape[2]
    full = slots.shape[2]
    width = full // groups
    chips = groups // 2
    tile = min(256, rows)
    hidden, rank = hg.shape
    down = hd.shape[1]
    anywhere = pl.BlockSpec(memory_space=pl.ANY)
    return pl.pallas_call(
        functools.partial(experts_kernel, planes, groups, in_set, tile, names),
        out_shape=(
            jax.ShapeDtypeStruct((rows, width), f32),
            jax.ShapeDtypeStruct((rows, full), bf16),
            jax.ShapeDtypeStruct((in_set, rows, width), bf16),
            jax.ShapeDtypeStruct((rank, full), f32),
            jax.ShapeDtypeStruct((down, full), f32),
            jax.ShapeDtypeStruct((rank, hidden), f32),
            jax.ShapeDtypeStruct((rank, hidden), f32),
            jax.ShapeDtypeStruct((down, hidden), f32),
        ),
        in_specs=[anywhere] * 5 + [VMEM] * 8 + [anywhere] * planes,
        out_specs=(VMEM, anywhere) + (VMEM,) * 6,
        scratch_shapes=[
            pltpu.VMEM((full, w1_main.shape[1] + w1_tail.shape[1]), bf16),
            pltpu.VMEM((full, hidden + w2_tail.shape[1]), bf16),
            pltpu.VMEM((2, 2, CAP, full), bf16),
            pltpu.VMEM((2, CAP, full), bf16),
            pltpu.VMEM((2, CAP, full), bf16),
            pltpu.VMEM((in_set, groups * CAP, width), bf16),
            pltpu.VMEM((in_set, groups * CAP, width), bf16),
            pltpu.VMEM((in_set - 1, rows, width), bf16),
            pltpu.VMEM((in_set - 1, rows, width), bf16),
            pltpu.VMEM((rows, width), bf16),
            DMA((2,)),
            DMA((2 * planes + 1,)),
            DMA((2,)),
            DMA((in_set, groups)),
            DMA((in_set, groups)),
            DMA((in_set, groups)),
            DMA((in_set, groups)),
            DMA((2, in_set)),
            DMA((in_set - 1,)),
            DMA((in_set - 1,)),
            DMA,
            DMA((chips,)),
            DMA((chips,)),
            DMA((chips,)),
            DMA((chips,)),
        ],
        compiler_params=pltpu.CompilerParams(
            collective_id=collective_id, has_side_effects=True, vmem_limit_bytes=62 << 20
        ),
        cost_estimate=SMALL,
    )(
        slots, w1_main, w1_tail, late, w2_tail, hg, hu, hd, masks, mask_down, own, gain, key, *early
    )


def planes_kernel(planes, x_ref, o_ref, own_sem, send_sem, recv_sem):
    plane = lax.axis_index("gx")
    barrier = pltpu.get_barrier_semaphore()
    own = pltpu.make_async_copy(x_ref, o_ref.at[plane], own_sem)
    own.start()
    for step in range(1, planes):
        target = lax.rem(plane + step, planes)
        pl.semaphore_signal(barrier, inc=1, device_id={"gx": target}, device_id_type=MESH)
    pl.semaphore_wait(barrier, planes - 1)
    copies = []
    for step in range(1, planes):
        copy = to_plane(
            x_ref,
            o_ref.at[plane],
            send_sem.at[step - 1],
            recv_sem.at[step - 1],
            lax.rem(plane + step, planes),
        )
        copy.start()
        copies.append(copy)
    own.wait()
    for copy in copies:
        copy.wait_recv()
        copy.wait_send()


def gather_planes(x, planes, collective_id):
    return pl.pallas_call(
        functools.partial(planes_kernel, planes),
        out_shape=jax.ShapeDtypeStruct((planes,) + x.shape, x.dtype),
        in_specs=[VMEM],
        out_specs=VMEM,
        scratch_shapes=[DMA, DMA((planes - 1,)), DMA((planes - 1,))],
        compiler_params=pltpu.CompilerParams(collective_id=collective_id, has_side_effects=True),
        cost_estimate=SMALL,
    )(x)


def rope_tables(length, width):
    half_width = width // 2
    frequency = rope_theta ** (-2.0 * jnp.arange(half_width, dtype=f32) / width)
    angles = jnp.arange(length, dtype=f32)[:, None] * frequency[None, :]
    return (jnp.cos(angles), jnp.sin(angles))


def apply_rotary(values, cosine, sine):
    half_width = values.shape[-1] // 2
    first = values[..., :half_width]
    second = values[..., half_width:]
    return jnp.concatenate(
        [first * cosine - second * sine, second * cosine + first * sine], axis=-1
    )


def unrotate(grads, cosine, sine):
    half_width = grads.shape[-1] // 2
    first = grads[..., :half_width]
    second = grads[..., half_width:]
    return jnp.concatenate(
        [first * cosine + second * sine, second * cosine - first * sine], axis=-1
    )


def allowed_mask(piece_starts):
    places = jnp.arange(SEQ, dtype=jnp.int32)
    causal = places[None, :] <= places[:, None]
    inside = (places[None, None, :] >= piece_starts[:, :, None]) & (
        places[None, None, :] < piece_starts[:, :, None] + PIECE
    )
    same_piece = jnp.any(inside[:, :, :, None] & inside[:, :, None, :], axis=1)
    return causal[None] | same_piece


def dot(spec, left, right):
    return jnp.einsum(spec, left, right, preferred_element_type=f32)


def after(first, *later):
    return lax.optimization_barrier((first,) + later)[1:]


def shards(
    block_input,
    out_grad,
    routes,
    adapter_ids,
    piece_starts,
    attn_gain,
    qk_gain,
    mlp_gain,
    w_qkv,
    w_out,
    a_qkv,
    b_out,
    head_pack,
    router,
    w_gate_up,
    w_down,
    exp_wide,
    exp_hidden,
):
    planes = lax.axis_size("gx")
    groups = lax.axis_size("gy")
    plane = lax.axis_index("gx")
    column = lax.axis_index("gy")
    rows, width_local = block_input.shape
    width = width_local * groups
    heads_local = head_pack.shape[0]
    rank_cols = head_pack.shape[2]
    head_width = head_pack.shape[3]
    experts_local = w_gate_up.shape[0]
    hidden_width = w_gate_up.shape[3]
    nseq = adapter_ids.shape[0]
    inv_root = head_width ** (-0.5)
    repeats = planes // experts_local
    steps = range(experts_local)
    own = lax.rem(plane, experts_local)

    def shifted(x, step):
        if step % experts_local == 0:
            return x
        pairs = []
        for p in range(planes):
            base = p // experts_local * experts_local
            pairs.append((p, base + (p - base + step) % experts_local))
        return lax.ppermute(x, "gx", pairs)

    def own_pieces(piece_for):
        pieces = []
        for step in range(planes):
            piece = piece_for(lax.rem(plane + step, planes))
            if step:
                pairs = [(p, (p + step) % planes) for p in range(planes)]
                piece = lax.ppermute(piece, "gx", pairs)
            pieces.append((lax.rem(plane - step + planes, planes), piece))
        return pieces

    compact = nseq * RANK

    def pick(x, axis):
        return jnp.concatenate(
            [
                lax.dynamic_slice_in_dim(x, adapter_ids[n] * RANK, RANK, axis=axis)
                for n in range(nseq)
            ],
            axis=axis,
        )

    token_seq = jnp.arange(rows, dtype=jnp.int32) // SEQ
    col_seq = jnp.arange(compact, dtype=jnp.int32) // RANK
    compact_mask = (token_seq[:, None] == col_seq[None, :]).astype(f32)
    a_pick = pick(a_qkv, 2)
    b_pick = pick(b_out, 0)
    pack_pick = pick(head_pack, 2)

    top = routes.shape[1]
    whole = jnp.concatenate(
        [routes.reshape(rows * top // 128, 128), jnp.zeros((8, 128), jnp.int32)], axis=0
    )
    whole = lax.dynamic_update_slice(whole, adapter_ids[None, :], (rows * top // 128, 0))
    whole = gather_planes(whole, planes, 10)
    routes_all = whole[:, : rows * top // 128].reshape(planes, rows, top)
    adapters_all = whole[:, rows * top // 128, :nseq]
    dl = w_gate_up.shape[1]
    hl = exp_hidden.shape[1]
    qkv_width = 3 * heads_local * head_width
    weight_shard = jnp.concatenate(
        [
            w_qkv.reshape(w_qkv.shape[0], qkv_width),
            w_out.reshape(heads_local * head_width, w_out.shape[2]).T,
        ],
        axis=1,
    )
    attn_weight = lax.all_gather(weight_shard, "gx", axis=0, tiled=True)
    normed_bf, scale_one, gathered = gather_normed(
        jnp.concatenate(
            [block_input, a_pick.transpose(0, 2, 1).reshape(3 * compact, width_local), b_pick],
            axis=0,
        ),
        attn_gain,
        rows,
        groups,
        1,
    )
    scale_one = scale_one[:, :1]
    a_full = gathered[: 3 * compact]
    b_full = gathered[3 * compact :]

    set_cols = experts_local * compact
    fold = max(1, 128 // set_cols)
    sets_adapters = adapters_all.reshape(repeats, experts_local * nseq)
    rank_index = jnp.arange(rank_cols, dtype=jnp.int32)
    set_index = jnp.arange(set_cols, dtype=jnp.int32)
    set_pick = (
        (rank_index // RANK)[None, :, None] == jnp.repeat(sets_adapters, RANK, axis=1)[:, None, :]
    ) & ((rank_index % RANK)[None, :, None] == (set_index % RANK)[None, None, :])
    set_pick = set_pick.astype(bf16)

    def folded(x):
        return jnp.concatenate(jnp.split(x, fold, axis=1), axis=2)

    def unfolded(x):
        return jnp.concatenate(jnp.split(x, fold, axis=2), axis=1)

    rank_rows = jnp.concatenate(
        [exp_wide[:, :, c] for c in range(3)] + [exp_hidden[:, :, c] for c in range(3)], axis=1
    )
    rank_shard = folded(
        dot("emr,srk->semk", rank_rows, set_pick)
        .reshape(planes, rank_rows.shape[1], set_cols)
        .astype(bf16)
    )
    expert_ids = own + experts_local * jnp.arange(groups, dtype=jnp.int32)
    set_start = (plane // experts_local) * experts_local
    step_plane = lax.rem(own - jnp.arange(experts_local) + experts_local, experts_local)
    routes_set = routes_all[set_start + step_plane]
    hits = jnp.any(routes_set[:, :, :, None] == expert_ids, axis=2)
    order = jnp.arange(rows, dtype=jnp.int32)
    earlier = (order[None, :] < order[:, None]).astype(bf16)
    places = dot("ts,gsc->gct", earlier, hits.astype(bf16))
    slot_key = jnp.where(hits.transpose(0, 2, 1), places.astype(jnp.int32), -1)
    slots = jnp.arange(CAP, dtype=jnp.int32)
    column_key = slot_key + CAP * jnp.arange(groups, dtype=jnp.int32)[None, :, None]
    column_key = jnp.where(slot_key >= 0, column_key, -1)
    own_key = lax.dynamic_index_in_dim(slot_key, column, 1, keepdims=False)
    own_pick = (own_key[:, None, :] == slots[None, :, None]).astype(bf16)
    rank_mask = (
        (step_plane[:, None] * nseq + token_seq[None, :])[:, :, None]
        == (set_index // RANK)[None, None, :]
    ).astype(bf16)
    slot_total = experts_local * CAP
    mask_slot = dot("gst,gtr->gsr", own_pick, rank_mask).reshape(slot_total, set_cols)

    gate_up_flat = w_gate_up.reshape(experts_local, dl, 2 * hidden_width)
    names = 2 * router.shape[1]
    down_pad = -set_cols % 128
    own_id = column * experts_local + own
    is_own = (jnp.arange(names, dtype=jnp.int32) % router.shape[1] == own_id).astype(f32)
    is_own = jnp.pad(is_own, (0, 128 - names)).reshape(1, 128)
    two_masks = jnp.concatenate([mask_slot, mask_slot], axis=1)
    down_mask = jnp.pad(mask_slot, ((0, 0), (0, down_pad)))
    router_twice = jnp.pad(
        jnp.concatenate([router, router], axis=1), ((0, 0), (0, 128 - names))
    )
    (
        attn_weight,
        slot_key,
        column_key,
        two_masks,
        down_mask,
        is_own,
        router_twice,
        gate_up_flat,
        rank_shard,
    ) = lax.optimization_barrier(
        (
            attn_weight,
            slot_key,
            column_key,
            two_masks,
            down_mask,
            is_own,
            router_twice,
            gate_up_flat,
            rank_shard,
        )
    )
    rank_sent = lax.all_to_all(rank_shard, "gx", 0, 0, tiled=True)

    (down_later,) = after(rank_sent, w_down)
    early_rows = dl * 5 // 8
    early_pieces = own_pieces(
        lambda p: lax.dynamic_slice(
            down_later, (lax.rem(p, experts_local), 0, 0), (1, early_rows, hidden_width)
        )[0]
    )
    rank_weight = unfolded(rank_sent)

    def rank_part(start, count):
        return rank_weight[:, start : start + count].reshape(planes * count, set_cols)

    wide_parts = [rank_part(c * dl, dl) for c in range(3)]
    hidden_gate, hidden_up, hidden_down = [rank_part(3 * dl + c * hl, hl) for c in range(3)]
    no_rank = jnp.zeros((hidden_width, set_cols), bf16)
    rank_operands = (
        jnp.concatenate([wide_parts[0], wide_parts[1], router_twice], axis=1),
        jnp.pad(wide_parts[2], ((0, 0), (0, down_pad))),
        jnp.concatenate([hidden_gate, no_rank], axis=1),
        jnp.concatenate([no_rank, hidden_up], axis=1),
        jnp.pad(hidden_down, ((0, 0), (0, down_pad))),
    )

    col_start = column * width_local
    first_norm_gain = lax.dynamic_slice_in_dim(attn_gain, col_start, width_local)
    base = dot("td,de->te", normed_bf, attn_weight[:, :qkv_width]).reshape(
        rows, heads_local, 3, head_width
    )
    rank_in = dot("td,kd->tk", normed_bf, a_full).reshape(rows, 3, compact)
    rank_low = (rank_in * compact_mask[:, None, :]).astype(bf16)
    projected = base + rank_scale * dot("tcr,hcre->thce", rank_low, pack_pick[:, :3])
    query_pre = projected[:, :, 0]
    key_pre = projected[:, :, 1]
    value_bf = projected[:, :, 2].astype(bf16)
    square_sums = jnp.stack(
        [jnp.sum(query_pre * query_pre, axis=(1, 2)), jnp.sum(key_pre * key_pre, axis=(1, 2))]
    )
    (square_sums,) = after(rank_sent, square_sums)
    square_sums = add_small(square_sums.reshape(-1, 128), groups, 2).reshape(2, rows)
    query_scale = lax.rsqrt(square_sums[0] / width + norm_eps)[:, None, None]
    key_scale = lax.rsqrt(square_sums[1] / width + norm_eps)[:, None, None]
    head_start = column * heads_local * head_width
    gains_local = lax.dynamic_slice_in_dim(
        qk_gain, head_start, heads_local * head_width, axis=1
    ).reshape(2, heads_local, head_width)
    query_hat = query_pre * query_scale
    key_hat = key_pre * key_scale
    cosine, sine = rope_tables(SEQ, head_width)
    cosine = cosine[None, :, None, :]
    sine = sine[None, :, None, :]
    query_bf = apply_rotary(
        (query_hat * gains_local[0]).reshape(nseq, SEQ, heads_local, head_width), cosine, sine
    ).astype(bf16)
    key_bf = apply_rotary(
        (key_hat * gains_local[1]).reshape(nseq, SEQ, heads_local, head_width), cosine, sine
    ).astype(bf16)
    values_seq = value_bf.reshape(nseq, SEQ, heads_local, head_width)
    allowed = allowed_mask(piece_starts)[:, None]
    scores = dot("nqhe,nkhe->nhqk", query_bf, key_bf) * inv_root
    scores = jnp.where(allowed, scores, -1e30)
    row_peak = jnp.max(scores, axis=-1, keepdims=True)
    raised = jnp.exp(scores - row_peak)
    row_total = jnp.sum(raised, axis=-1, keepdims=True)
    log_total = row_peak + jnp.log(row_total)
    weights = raised / row_total
    attended = dot("nhqk,nkhe->nqhe", weights.astype(bf16), values_seq)
    attn_bf = attended.reshape(rows, heads_local, head_width).astype(bf16)
    rank_out = dot("the,hre->thr", attn_bf, pack_pick[:, 3])
    rank_out_low = (rank_out * compact_mask[:, None, :]).astype(bf16)
    out_weight = attn_weight[:, qkv_width:]
    b_turned = (rank_scale * b_full.T).astype(bf16)
    branch_left = jnp.concatenate(
        [
            attn_bf.reshape(rows, heads_local * head_width),
            rank_out_low.reshape(rows, heads_local * compact),
        ],
        axis=1,
    )
    branch_left, *rank_operands = lax.optimization_barrier((branch_left,) + rank_operands)
    branch_left, *early = lax.optimization_barrier(
        (branch_left,) + tuple(piece for _, piece in early_pieces)
    )
    branch, late_pieces = scatter_product(
        branch_left,
        jnp.concatenate([out_weight] + [b_turned] * heads_local, axis=1),
        groups,
        3,
        w_down,
        early_rows,
        planes,
    )
    middle = block_input.astype(f32) + branch
    middle_low = middle.astype(bf16)

    slot_rows, gate_up_weight = spread(
        jnp.concatenate([middle_low, out_grad], axis=1),
        slot_key,
        gate_up_flat,
        planes,
        groups,
        2 * hidden_width,
        4,
    )
    both_rows = lax.all_gather(
        jnp.concatenate([middle_low, out_grad], axis=0), "gy", axis=1, tiled=True
    )
    (
        normed_two_part,
        normed_two_rows,
        moe_planes,
        wide_gu_grad,
        wide_down_grad,
        gate_rank_grad,
        up_rank_grad,
        down_rank_grad,
    ) = experts(
        slot_rows,
        gate_up_weight,
        rank_operands[0],
        early,
        late_pieces,
        *rank_operands[1:],
        two_masks,
        down_mask,
        is_own,
        mlp_gain.reshape(1, width),
        column_key,
        names,
        planes,
        groups,
        5,
    )
    moe_pieces = [
        shifted(moe_planes[step], experts_local - step) for step in range(1, experts_local)
    ]

    wide_grads = [
        wide_gu_grad[:set_cols],
        wide_gu_grad[set_cols:],
        wide_down_grad[:set_cols],
    ]
    hidden_grads = [
        gate_rank_grad[:set_cols],
        up_rank_grad[set_cols:],
        down_rank_grad[:set_cols],
    ]
    rank_grads = jnp.concatenate(
        [x.astype(bf16).T.reshape(planes, dl, set_cols) for x in wide_grads]
        + [x.astype(bf16).T.reshape(planes, hl, set_cols) for x in hidden_grads],
        axis=1,
    )
    rank_grads = lax.all_to_all(folded(rank_grads), "gx", 0, 0, tiled=True)

    middle_rows = both_rows[:rows].astype(f32)
    grad_rows = both_rows[rows:].astype(f32)
    scale_two = lax.rsqrt(jnp.mean(middle_rows * middle_rows, axis=-1, keepdims=True) + norm_eps)
    normed_two_grad = normed_two_rows.astype(f32)
    hat_two = middle_rows * scale_two
    scaled_two = normed_two_grad * mlp_gain
    stat_two = jnp.mean(scaled_two * hat_two, axis=-1, keepdims=True)
    branch_rows = (grad_rows + scale_two * (scaled_two - hat_two * stat_two)).astype(bf16)
    gain_two_local = lax.dynamic_slice_in_dim(mlp_gain, col_start, width_local)
    middle_grad = out_grad.astype(f32) + scale_two * (
        normed_two_part * gain_two_local - middle_low.astype(f32) * scale_two * stat_two
    )
    rank_out_grad = rank_scale * dot("td,rd->tr", branch_rows, b_full)
    rank_out_bf = (rank_out_grad * compact_mask).astype(bf16)
    pack_out_grad = dot("the,tr->hre", attn_bf, rank_out_bf)
    attention_gradient = dot("td,de->te", branch_rows, out_weight).reshape(
        rows, heads_local, head_width
    ) + dot(
        "tr,hre->the", rank_out_bf, pack_pick[:, 3]
    )
    attn_grad_bf = attention_gradient.reshape(nseq, SEQ, heads_local, head_width).astype(bf16)
    scores_again = dot("nqhe,nkhe->nhqk", query_bf, key_bf) * inv_root
    scores_again = jnp.where(allowed, scores_again, -1e30)
    weights_again = jnp.exp(scores_again - log_total)
    value_grad = dot("nhqk,nqhe->nkhe", weights_again.astype(bf16), attn_grad_bf)
    weight_grad = dot("nqhe,nkhe->nhqk", attn_grad_bf, values_seq)
    row_dot = jnp.sum(weight_grad * weights_again, axis=-1, keepdims=True)
    score_grad = (weights_again * (weight_grad - row_dot)).astype(bf16)
    query_grad = dot("nhqk,nkhe->nqhe", score_grad, key_bf) * inv_root
    key_grad = dot("nhqk,nqhe->nkhe", score_grad, query_bf) * inv_root
    query_hat_grad = (
        unrotate(query_grad, cosine, sine).reshape(rows, heads_local, head_width) * gains_local[0]
    )
    key_hat_grad = (
        unrotate(key_grad, cosine, sine).reshape(rows, heads_local, head_width) * gains_local[1]
    )
    value_pre_grad = value_grad.reshape(rows, heads_local, head_width)
    stat_query = jnp.sum(query_hat_grad * query_hat, axis=(1, 2))
    stat_key = jnp.sum(key_hat_grad * key_hat, axis=(1, 2))

    def rank_terms(values, which):
        return dot("the,hre->rt", values.astype(bf16), pack_pick[:, which])

    pad_rows = -6 * compact % 32 or 32
    sums = jnp.concatenate(
        [
            piece.astype(bf16)
            for piece in (
                rank_terms(query_hat_grad, 0),
                rank_terms(key_hat_grad, 1),
                rank_terms(value_pre_grad, 2),
                rank_terms(query_hat, 0),
                rank_terms(key_hat, 1),
                jnp.sum(rank_out_low.astype(f32), axis=1).T,
                jnp.pad(jnp.stack([stat_query, stat_key]), ((0, pad_rows - 2), (0, 0))),
            )
        ],
        axis=0,
    )
    sums = add_pairs(sums, groups, 6)
    first_total = sums[: 3 * compact].reshape(3, compact, rows)
    second_total = sums[3 * compact : 5 * compact].reshape(2, compact, rows)
    mean_qk = sums[6 * compact : 6 * compact + 2] / width
    branch_local = lax.dynamic_slice_in_dim(branch_rows, col_start, width_local, axis=1)
    b_out_sum = rank_scale * dot(
        "rt,td->rd", sums[5 * compact : 6 * compact].astype(bf16), branch_local
    )
    scales_qk = jnp.stack([query_scale[:, 0, 0], key_scale[:, 0, 0]])
    rank_qk = scales_qk[:, None, :] * (first_total[:2] - second_total * mean_qk[:, None, :])
    rank_grad_full = rank_scale * jnp.concatenate([rank_qk, first_total[2:]], axis=0)
    rank_grad_bf = (rank_grad_full * compact_mask.T[None]).astype(bf16)
    query_pre_grad = query_scale * (query_hat_grad - query_hat * mean_qk[0][:, None, None])
    key_pre_grad = key_scale * (key_hat_grad - key_hat * mean_qk[1][:, None, None])
    pre_grad = jnp.stack([query_pre_grad, key_pre_grad, value_pre_grad], axis=2).astype(bf16)
    pack_b_grad = rank_scale * dot("tcr,thce->rhce", rank_low, pre_grad)
    normed_one_grad = scatter_product(
        pre_grad.reshape(rows, qkv_width), attn_weight[:, :qkv_width], groups, 7
    )[0]
    adapter_input_gradient = dot("crt,cdr->td", rank_grad_bf, a_pick)
    first_normalized_shard = block_input.astype(f32) * scale_one
    normed_local_bf = lax.dynamic_slice_in_dim(normed_bf, col_start, width_local, axis=1)
    a_rows_grad = dot("td,crt->rcd", normed_local_bf, rank_grad_bf)
    scaled_one = (normed_one_grad + adapter_input_gradient) * first_norm_gain
    stat_one = jnp.sum(scaled_one * first_normalized_shard, axis=-1)
    stat_one_sum = add_small(stat_one.reshape(-1, 128), groups, 8).reshape(rows, 1)
    input_grad = middle_grad + scale_one * (
        scaled_one - first_normalized_shard * stat_one_sum / width
    )
    rank_grads, *moe_pieces = after(normed_one_grad, rank_grads, *moe_pieces)
    moe_part = moe_planes[0].astype(f32)
    for piece in moe_pieces:
        moe_part = moe_part + piece.astype(f32)
    layer_out = (middle + moe_part).astype(bf16)
    rank_grads = unfolded(rank_grads)
    rank_grads = rank_grads.reshape((repeats, experts_local) + rank_grads.shape[1:])
    wide_sum = jnp.stack(
        [
            dot("semk,srk->emr", rank_grads[:, :, c * dl : (c + 1) * dl], set_pick)
            for c in range(3)
        ],
        axis=2,
    )
    hidden_sum = jnp.stack(
        [
            dot(
                "semk,srk->emr",
                rank_grads[:, :, 3 * dl + c * hl : 3 * dl + (c + 1) * hl],
                set_pick,
            )
            for c in range(3)
        ],
        axis=2,
    )

    pack_grad = jnp.concatenate(
        [
            pack_b_grad.transpose(1, 2, 0, 3),
            pack_out_grad[:, None],
        ],
        axis=1,
    )
    small = jnp.concatenate(
        [
            a_rows_grad.reshape(compact, 3 * width_local),
            b_out_sum,
            pack_grad.transpose(2, 0, 1, 3).reshape(compact, heads_local * 4 * head_width),
        ],
        axis=1,
    )
    small_all = gather_planes(small.astype(bf16), planes, 9)
    small_all = small_all.reshape(planes * compact, small.shape[1])
    row_at = (
        adapters_all[:, :, None] * RANK + jnp.arange(RANK, dtype=jnp.int32)[None, None, :]
    ).reshape(-1)
    put = (jnp.arange(rank_cols, dtype=jnp.int32)[:, None] == row_at[None, :]).astype(bf16)
    small_sum = jnp.dot(put, small_all, preferred_element_type=f32)
    a_end = 3 * width_local
    b_end = a_end + width_local
    a_sum = small_sum[:, :a_end].reshape(rank_cols, 3, width_local).transpose(1, 2, 0)
    b_sum = small_sum[:, a_end:b_end]
    head_sum = small_sum[:, b_end:].reshape(rank_cols, heads_local, 4, head_width)
    head_sum = head_sum.transpose(1, 2, 0, 3)
    return (layer_out, input_grad, a_sum, b_sum, head_sum, wide_sum, hidden_sum)


def solution(mesh):
    return jax.shard_map(
        shards,
        mesh=mesh,
        in_specs=(
            P("gx", "gy"),
            P("gx", "gy"),
            P("gx", None),
            P("gx"),
            P("gx", None),
            P(),
            P(),
            P(),
            P("gx", "gy", None, None),
            P("gy", None, "gx"),
            P(None, "gy", None),
            P(None, "gy"),
            P("gy", None, None, None),
            P(),
            P("gy", "gx", None, None),
            P("gy", "gx", None),
            P("gy", "gx", None, None),
            P("gy", "gx", None, None),
        ),
        out_specs=(
            P("gx", "gy"),
            P("gx", "gy"),
            P(None, "gy", None),
            P(None, "gy"),
            P("gy", None, None, None),
            P("gy", "gx", None, None),
            P("gy", "gx", None, None),
        ),
        check_vma=False,
    )
```

```python
import functools
import jax
import jax.numpy as jnp
from jax import lax
from jax.experimental import pallas as pl
from jax.experimental.pallas import tpu as pltpu
from jax.sharding import PartitionSpec as P

RANK = 16
SEQ = 1024
PIECE = 256
CAP = 288
EARLY_PARTS = 2


norm_eps = 1e-05
rope_theta = 10000.0
rank_scale = 0.5
down_scale = 4.0
bf16 = jnp.bfloat16
f32 = jnp.float32
VMEM = pl.BlockSpec(memory_space=pltpu.VMEM)
DMA = pltpu.SemaphoreType.DMA
MESH = pl.DeviceIdType.MESH
SMALL = pl.CostEstimate(flops=0, bytes_accessed=1 << 16, transcendentals=0)
CAP = 288
SMALL = pl.CostEstimate(flops=0, bytes_accessed=1 << 16, transcendentals=0)


def place_in_column():
    me = lax.axis_index("gy")
    chip, core = lax.div(me, 2), lax.rem(me, 2)
    return me, chip, core, me + 1 - 2 * core


def chip_peer(chip, core, step, chips):
    return lax.rem(chip + step, chips) * 2 + core


def greet_chips(chip, core, sibling, chips, planes=1):
    barrier = pltpu.get_barrier_semaphore()
    for step in range(1, planes):
        target = lax.rem(lax.axis_index("gx") + step, planes)
        pl.semaphore_signal(barrier, inc=1, device_id={"gx": target}, device_id_type=MESH)
    pl.semaphore_signal(barrier, inc=1, device_id={"gy": sibling}, device_id_type=MESH)
    for step in range(1, chips):
        pl.semaphore_signal(
            barrier,
            inc=1,
            device_id={"gy": chip_peer(chip, core, step, chips)},
            device_id_type=MESH,
        )
    pl.semaphore_wait(barrier, chips + planes - 1)


def remote(src, dst, send_sem, recv_sem, target):
    return pltpu.make_async_remote_copy(
        src_ref=src,
        dst_ref=dst,
        send_sem=send_sem,
        recv_sem=recv_sem,
        device_id={"gy": target},
        device_id_type=MESH,
    )


def gather_kernel(
    chips,
    rows,
    tile,
    x_ref,
    gain_ref,
    normed_ref,
    scale_ref,
    rest_ref,
    whole,
    own_sem,
    send_sem,
    recv_sem,
    pass_sem,
    passed_sem,
):
    me, chip, core, sibling = place_in_column()
    width = x_ref.shape[1]

    def columns(owner):
        return whole.at[:, pl.ds(pl.multiple_of(owner * width, width), width)]

    own = pltpu.make_async_copy(x_ref, columns(me), own_sem)
    own.start()
    greet_chips(chip, core, sibling, chips)
    out = []
    for step in list(range(1, chips)) + [0]:
        target = sibling if step == 0 else chip_peer(chip, core, step, chips)
        copy = remote(x_ref, columns(me), send_sem.at[step], recv_sem.at[step], target)
        copy.start()
        out.append(copy)
    for step in range(1, chips):
        out[step - 1].wait_recv()
        source = chip_peer(chip, core, chips - step, chips)
        copy = remote(
            columns(source), columns(source), pass_sem.at[step], passed_sem.at[step], sibling
        )
        copy.start()
        out.append(copy)
    own.wait()
    out[chips - 1].wait_recv()
    for copy in out[chips:]:
        copy.wait_recv()

    @pl.loop(0, rows // tile)
    def _(i):
        at = pl.ds(pl.multiple_of(i * tile, tile), tile)
        values = whole[at, :].astype(f32)
        scale = lax.rsqrt(jnp.mean(values * values, axis=-1, keepdims=True) + norm_eps)
        scale_ref[at, :] = jnp.broadcast_to(scale, (tile, 128))
        normed_ref[at, :] = (values * scale * gain_ref[...]).astype(bf16)

    rest_ref[...] = whole[pl.ds(rows, rest_ref.shape[0]), :]
    for copy in out:
        copy.wait_send()


def gather_normed(x, gain, rows, groups, collective_id):
    chips = groups // 2
    total, width = x.shape
    full = groups * width
    return pl.pallas_call(
        functools.partial(gather_kernel, chips, rows, 64),
        out_shape=(
            jax.ShapeDtypeStruct((rows, full), bf16),
            jax.ShapeDtypeStruct((rows, 128), f32),
            jax.ShapeDtypeStruct((total - rows, full), bf16),
        ),
        in_specs=[VMEM, VMEM],
        out_specs=(VMEM, VMEM, VMEM),
        scratch_shapes=[
            pltpu.VMEM((total, full), bf16),
            DMA,
            DMA((chips,)),
            DMA((chips,)),
            DMA((chips,)),
            DMA((chips,)),
        ],
        compiler_params=pltpu.CompilerParams(
            collective_id=collective_id, has_side_effects=True, vmem_limit_bytes=48 << 20
        ),
        cost_estimate=SMALL,
    )(x, gain.reshape(1, full))


def scatter_and_carry_kernel(
    planes, first, chips, tile, l_ref, r_ref, w_ref, o_ref, w_out, *rest
):
    *scratch, w_own, w_send, w_recv = rest
    plane = lax.axis_index("gx")
    in_set, count = w_ref.shape[0], w_out.shape[1]

    def piece(target):
        return w_ref.at[lax.rem(target, in_set), pl.ds(first, count), :]

    def carry():
        own = pltpu.make_async_copy(piece(plane), w_out.at[plane], w_own)
        own.start()
        copies = []
        for step in range(1, planes):
            target = lax.rem(plane + step, planes)
            copy = to_plane(
                piece(target), w_out.at[plane], w_send.at[step - 1], w_recv.at[step - 1], target
            )
            copy.start()
            copies.append(copy)
        return own, copies

    own, copies = scatter_kernel(
        chips, tile, l_ref, r_ref, o_ref, *scratch, planes=planes, after_greeting=carry
    )
    own.wait()
    for copy in copies:
        copy.wait_recv()
        copy.wait_send()


def scatter_kernel(
    chips,
    tile,
    l_ref,
    r_ref,
    o_ref,
    part,
    got,
    pair,
    far,
    part_s,
    got_s,
    pair_s,
    far_s,
    planes=1,
    after_greeting=None,
):
    me, chip, core, sibling = place_in_column()
    rows, width = o_ref.shape
    greet_chips(chip, core, sibling, chips, planes)
    carried = after_greeting() if after_greeting else None
    steps = list(range(1, chips)) + [0]

    def product(owner, row):
        chunk = r_ref[pl.ds(pl.multiple_of(owner * width, width), width), :]
        return lax.dot_general(
            l_ref[pl.ds(row, tile), :],
            chunk,
            (((1,), (1,)), ((), ())),
            preferred_element_type=f32,
        )

    copies = []
    for step in steps:
        owner = chip_peer(chip, 1 - core, step, chips)

        @pl.loop(0, rows // tile)
        def _(i, owner=owner, step=step):
            row = pl.multiple_of(i * tile, tile)
            part[step, pl.ds(row, tile), :] = product(owner, row).astype(bf16)

        copy = remote(part.at[step], got.at[step], part_s.at[step], got_s.at[step], sibling)
        copy.start()
        copies.append(copy)
    for step in steps:
        owner = chip_peer(chip, core, step, chips)
        copies[steps.index(step)].wait_recv()

        @pl.loop(0, rows // tile)
        def _(i, owner=owner, step=step):
            row = pl.multiple_of(i * tile, tile)
            total = product(owner, row) + got[step, pl.ds(row, tile), :].astype(f32)
            if step == 0:
                o_ref[pl.ds(row, tile), :] = total
            else:
                pair[step - 1, pl.ds(row, tile), :] = total.astype(bf16)

        if step > 0:
            copy = remote(
                pair.at[step - 1], far.at[step - 1], pair_s.at[step - 1], far_s.at[step - 1], owner
            )
            copy.start()
            copies.append(copy)
    for step in range(1, chips):
        copies[chips + step - 1].wait_recv()

        @pl.loop(0, rows // tile)
        def _(i, step=step):
            row = pl.multiple_of(i * tile, tile)
            o_ref[pl.ds(row, tile), :] += far[step - 1, pl.ds(row, tile), :].astype(f32)

    for copy in copies:
        copy.wait_send()
    return carried


def scatter_product(left, right, groups, collective_id, weight=None, first=0, planes=1):
    chips = groups // 2
    rows, inner = left.shape
    width = right.shape[0] // groups
    tile = min(256, rows)
    body = functools.partial(scatter_kernel, chips, tile)
    out_shape = (jax.ShapeDtypeStruct((rows, width), f32),)
    in_specs, out_specs = [VMEM, VMEM], (VMEM,)
    scratch = [
        pltpu.VMEM((chips, rows, width), bf16),
        pltpu.VMEM((chips, rows, width), bf16),
        pltpu.VMEM((chips - 1, rows, width), bf16),
        pltpu.VMEM((chips - 1, rows, width), bf16),
        DMA((chips,)),
        DMA((chips,)),
        DMA((chips - 1,)),
        DMA((chips - 1,)),
    ]
    operands = (left, right)
    if weight is not None:
        body = functools.partial(scatter_and_carry_kernel, planes, first, chips, tile)
        carried = (planes, weight.shape[1] - first, weight.shape[2])
        out_shape += (jax.ShapeDtypeStruct(carried, bf16),)
        in_specs = in_specs + [pl.BlockSpec(memory_space=pl.ANY)]
        out_specs += (pl.BlockSpec(memory_space=pl.ANY),)
        scratch = scratch + [DMA, DMA((planes - 1,)), DMA((planes - 1,))]
        operands += (weight,)
    return pl.pallas_call(
        body,
        out_shape=out_shape,
        in_specs=in_specs,
        out_specs=out_specs,
        scratch_shapes=scratch,
        compiler_params=pltpu.CompilerParams(
            collective_id=collective_id, has_side_effects=True, vmem_limit_bytes=48 << 20
        ),
        cost_estimate=SMALL,
    )(*operands)


def add_kernel(groups, x_ref, o_ref, got, send_sem, recv_sem):
    me = lax.axis_index("gy")
    barrier = pltpu.get_barrier_semaphore()
    for step in range(1, groups):
        target = lax.rem(me + step, groups)
        pl.semaphore_signal(barrier, inc=1, device_id={"gy": target}, device_id_type=MESH)
    pl.semaphore_wait(barrier, groups - 1)
    copies = []
    for step in range(1, groups):
        target = lax.rem(me + step, groups)
        copy = remote(
            x_ref, got.at[step - 1], send_sem.at[step - 1], recv_sem.at[step - 1], target
        )
        copy.start()
        copies.append(copy)
    total = x_ref[...]
    for step in range(1, groups):
        copies[step - 1].wait_recv()
        total = total + got[step - 1]
    o_ref[...] = total
    for copy in copies:
        copy.wait_send()


def add_small(x, groups, collective_id):
    return pl.pallas_call(
        functools.partial(add_kernel, groups),
        out_shape=jax.ShapeDtypeStruct(x.shape, f32),
        in_specs=[VMEM],
        out_specs=VMEM,
        scratch_shapes=[
            pltpu.VMEM((groups - 1,) + x.shape, f32),
            DMA((groups - 1,)),
            DMA((groups - 1,)),
        ],
        compiler_params=pltpu.CompilerParams(collective_id=collective_id, has_side_effects=True),
        cost_estimate=SMALL,
    )(x)


def add_pairs_kernel(
    chips, x_ref, o_ref, got, pair, far, done, got_s, far_s, done_s
):
    me, chip, core, sibling = place_in_column()
    half = x_ref.shape[0] // 2
    greet_chips(chip, core, sibling, chips)
    first = remote(x_ref, got, got_s.at[0], got_s.at[1], sibling)
    first.start()
    first.wait_recv()
    own = pl.ds(pl.multiple_of(core * half, 16), half)
    total = x_ref[own, :].astype(f32) + got[own, :].astype(f32)
    pair[...] = total.astype(bf16)
    copies = []
    for step in range(1, chips):
        copy = remote(
            pair,
            far.at[step - 1],
            far_s.at[0, step - 1],
            far_s.at[1, step - 1],
            chip_peer(chip, core, step, chips),
        )
        copy.start()
        copies.append(copy)
    for step in range(1, chips):
        copies[step - 1].wait_recv()
        total = total + far[step - 1].astype(f32)
    done[own, :] = total.astype(bf16)
    last = remote(done.at[own, :], done.at[own, :], done_s.at[0], done_s.at[1], sibling)
    last.start()
    last.wait_recv()
    o_ref[...] = done[...].astype(f32)
    first.wait_send()
    for copy in copies:
        copy.wait_send()
    last.wait_send()


def add_pairs(x, groups, collective_id):
    chips = groups // 2
    rows, width = x.shape
    return pl.pallas_call(
        functools.partial(add_pairs_kernel, chips),
        out_shape=jax.ShapeDtypeStruct(x.shape, f32),
        in_specs=[VMEM],
        out_specs=VMEM,
        scratch_shapes=[
            pltpu.VMEM(x.shape, bf16),
            pltpu.VMEM((rows // 2, width), bf16),
            pltpu.VMEM((chips - 1, rows // 2, width), bf16),
            pltpu.VMEM(x.shape, bf16),
            DMA((2,)),
            DMA((2, chips - 1)),
            DMA((2,)),
        ],
        compiler_params=pltpu.CompilerParams(collective_id=collective_id, has_side_effects=True),
        cost_estimate=SMALL,
    )(x)


def plane_place(planes_in_set):
    plane = lax.axis_index("gx")
    own = lax.rem(plane, planes_in_set)
    return plane, own, plane - own


def to_plane(src, dst, send_sem, recv_sem, target):
    return pltpu.make_async_remote_copy(
        src_ref=src,
        dst_ref=dst,
        send_sem=send_sem,
        recv_sem=recv_sem,
        device_id={"gx": target},
        device_id_type=MESH,
    )


def greet_all(planes, groups):
    barrier = pltpu.get_barrier_semaphore()
    plane, me = lax.axis_index("gx"), lax.axis_index("gy")

    @pl.loop(1, planes)
    def _(step):
        target = lax.rem(plane + step, planes)
        pl.semaphore_signal(barrier, inc=1, device_id={"gx": target}, device_id_type=MESH)

    @pl.loop(1, groups)
    def _(step):
        target = lax.rem(me + step, groups)
        pl.semaphore_signal(barrier, inc=1, device_id={"gy": target}, device_id_type=MESH)

    pl.semaphore_wait(barrier, planes + groups - 2)


def spread_kernel(
    planes,
    groups,
    in_set,
    x_ref,
    key_ref,
    w_ref,
    o_ref,
    full_ref,
    from_plane,
    picked,
    own_sem,
    w_send,
    w_recv,
    z_send,
    z_recv,
    g_send,
    g_recv,
):
    plane, own, base = plane_place(in_set)
    me = lax.axis_index("gy")
    width = x_ref.shape[1] // 2
    depth, inner = w_ref.shape[1], w_ref.shape[2]
    greet_all(planes, groups)
    last = in_set - 1

    def handed(step, up):
        side = 0 if up else 1
        distance = step if up else in_set - step
        there = own + (1 if up else -1)
        holds = own - (step - 1) if up else own + (step - 1)
        here = own - step if up else own + step
        sends = (there <= last) & (there >= 0) & (holds >= 0) & (holds <= last)
        waits = (here >= 0) & (here <= last)
        before = step - 1 if up else in_set - (step - 1)
        source = x_ref if step == 1 else from_plane.at[before - 1]
        copy = to_plane(
            source,
            from_plane.at[distance - 1],
            z_send.at[side, step - 1],
            z_recv.at[side, step - 1],
            base + lax.rem(there + in_set, in_set),
        )
        return copy, sends, waits

    def start_hand(step):
        for up in (True, False):
            copy, sends, _ = handed(step, up)
            pl.when(sends)(copy.start)

    def await_hand(step):
        for up in (True, False):
            copy, _, waits = handed(step, up)
            pl.when(waits)(copy.wait_recv)

    def end_hands():
        for step in range(1, in_set):
            for up in (True, False):
                copy, sends, _ = handed(step, up)
                pl.when(sends)(copy.wait_send)

    start_hand(1)
    mine = full_ref.at[pl.ds(pl.multiple_of(plane * depth, depth), depth), pl.ds(0, inner)]
    own_copy = pltpu.make_async_copy(w_ref.at[own], mine, own_sem)
    own_copy.start()

    def sent(step, turn):
        target = lax.rem(me + turn, groups)
        return remote(
            picked.at[step, turn],
            o_ref.at[
                :,
                pl.ds(step * CAP, CAP),
                pl.ds(pl.multiple_of(me * width, width), width),
            ],
            g_send.at[step, turn],
            g_recv.at[step, turn],
            target,
        )

    def work(step):
        block = from_plane.at[step - 1] if step else x_ref

        def choose(target):
            key = key_ref[step, pl.ds(target, 1), :]
            slot = lax.broadcasted_iota(jnp.int32, (CAP, key.shape[1]), 0)
            pick = jnp.where(slot == key, 1.0, 0.0).astype(bf16)
            return jnp.dot(pick, block[...], preferred_element_type=f32).astype(bf16)

        @pl.loop(1, groups)
        def _(turn):
            rows = choose(lax.rem(me + turn, groups))
            picked[step, turn, 0] = rows[:, :width]
            picked[step, turn, 1] = rows[:, width:]
            sent(step, turn).start()

        rows = choose(me)
        columns = pl.ds(pl.multiple_of(me * width, width), width)
        o_ref[0, pl.ds(step * CAP, CAP), columns] = rows[:, :width]
        o_ref[1, pl.ds(step * CAP, CAP), columns] = rows[:, width:]

    for step in range(1, in_set - 1):
        await_hand(step)
        start_hand(step + 1)
    w_copies = []
    for step in range(1, planes):
        target = lax.rem(plane + step, planes)
        copy = to_plane(
            w_ref.at[lax.rem(target, in_set)],
            mine,
            w_send.at[step - 1],
            w_recv.at[step - 1],
            target,
        )
        copy.start()
        w_copies.append(copy)
    work(0)
    await_hand(in_set - 1)
    for step in range(1, in_set):
        work(step)

    for step in range(in_set):

        @pl.loop(1, groups)
        def _(turn, step=step):
            copy = sent(step, turn)
            copy.wait_recv()
            copy.wait_send()

    end_hands()
    own_copy.wait()
    for copy in w_copies:
        copy.wait_recv()
        copy.wait_send()


def spread(x, key, weight, planes, groups, pad_to, collective_id):
    in_set, depth, inner = weight.shape
    rows, two = x.shape
    width = two // 2
    return pl.pallas_call(
        functools.partial(spread_kernel, planes, groups, in_set),
        out_shape=(
            jax.ShapeDtypeStruct((2, in_set * CAP, groups * width), bf16),
            jax.ShapeDtypeStruct((planes * depth, pad_to), bf16),
        ),
        in_specs=[VMEM, VMEM, pl.BlockSpec(memory_space=pl.ANY)],
        out_specs=(VMEM, pl.BlockSpec(memory_space=pl.ANY)),
        scratch_shapes=[
            pltpu.VMEM((in_set - 1, rows, two), bf16),
            pltpu.VMEM((in_set, groups, 2, CAP, width), bf16),
            DMA,
            DMA((planes - 1,)),
            DMA((planes - 1,)),
            DMA((2, in_set - 1)),
            DMA((2, in_set - 1)),
            DMA((in_set, groups)),
            DMA((in_set, groups)),
        ],
        compiler_params=pltpu.CompilerParams(
            collective_id=collective_id, has_side_effects=True, vmem_limit_bytes=48 << 20
        ),
        cost_estimate=SMALL,
    )(x, key, weight)


def experts_kernel(
    planes,
    groups,
    in_set,
    tile,
    names,
    slots_ref,
    w1_main_ref,
    w1_tail_ref,
    late_ref,
    w2_tail_ref,
    hg_ref,
    hu_ref,
    hd_ref,
    mask_ref,
    mask_down_ref,
    own_ref,
    gain_ref,
    key_ref,
    *rest,
):
    early_refs = rest[: planes * EARLY_PARTS]
    (
        shard_ref,
        rows_ref,
        placed_ref,
        wide_ref,
        wide_down_ref,
        hg_grad_ref,
        hu_grad_ref,
        hd_grad_ref,
        w1_ref,
        w2_ref,
        slot_buf,
        u_stage,
        m_stage,
        got,
        other,
        out_z,
        in_z,
        low,
        w1_sem,
        w2_sem,
        slot_sem,
        g_send,
        g_recv,
        m_send,
        m_recv,
        own_sem,
        z_send,
        z_recv,
        c_own,
        c_send,
        c_recv,
        p_send,
        p_recv,
    ) = rest[planes * EARLY_PARTS :]
    plane, own, base = plane_place(in_set)
    me, chip, core, sibling = place_in_column()
    chips = groups // 2
    rows, width = shard_ref.shape
    hidden = hd_ref.shape[0]
    rank = mask_ref.shape[1]
    order = list(range(1, in_set)) + [0]
    last = in_set - 1

    def columns_of(owner):
        return pl.ds(pl.multiple_of(owner * width, width), width)

    def slots_of(buffer, step, owner):
        return buffer.at[step, pl.ds(pl.multiple_of(owner * CAP, 16), CAP), :]

    def load(index):
        return pltpu.make_async_copy(
            slots_ref.at[:, pl.ds(order[index] * CAP, CAP), :],
            slot_buf.at[index % 2],
            slot_sem.at[index % 2],
        )

    def sent(index, turn, stage, landing, send_sem, recv_sem):
        target = lax.rem(me + turn, groups)
        step = order[index]
        return remote(
            stage.at[index % 2, :, columns_of(target)],
            slots_of(landing, step, me),
            send_sem.at[step, turn],
            recv_sem.at[step, turn],
            target,
        )

    def kept(index, stage, landing, which):
        step = order[index]
        return pltpu.make_async_copy(
            stage.at[index % 2, :, columns_of(me)],
            slots_of(landing, step, me),
            own_sem.at[which, step],
        )

    flows = (
        (u_stage, got, g_send, g_recv, 0),
        (m_stage, other, m_send, m_recv, 1),
    )

    def start_flow(index, flow):
        stage, landing, send_sem, recv_sem, which = flow

        @pl.loop(1, groups)
        def _(turn):
            sent(index, turn, stage, landing, send_sem, recv_sem).start()

        kept(index, stage, landing, which).start()

    def left_flow(index, flow):
        stage, landing, send_sem, recv_sem, which = flow

        @pl.loop(1, groups)
        def _(turn):
            sent(index, turn, stage, landing, send_sem, recv_sem).wait_send()

        if index < last - 1:
            kept(index, stage, landing, which).wait()

    def await_flow(index, flow):
        stage, landing, send_sem, recv_sem, which = flow

        @pl.loop(1, groups)
        def _(turn):
            sent(index, turn, stage, landing, send_sem, recv_sem).wait_recv()

        if index >= last - 1:
            kept(index, stage, landing, which).wait()

    def mul(left, right, over_left, over_right):
        return lax.dot_general(
            left, right, (((over_left,), (over_right,)), ((), ())), preferred_element_type=f32
        )

    def placed(step, row, buffer):
        keys = jnp.transpose(key_ref[step, :, pl.ds(row, tile)])
        pieces = []
        for start in range(0, groups * CAP, 128):
            slot = lax.broadcasted_iota(jnp.int32, (tile, 128), 1) + start
            hit = None
            for owner in range(start // CAP, min(groups, (start + 127) // CAP + 1)):
                same = slot == keys[:, owner : owner + 1]
                hit = same if hit is None else hit | same
            pieces.append(jnp.where(hit, 1.0, 0.0).astype(bf16))
        return jnp.dot(
            jnp.concatenate(pieces, axis=1), buffer[step], preferred_element_type=f32
        )

    def back(step):
        return to_plane(
            out_z.at[step - 1],
            in_z.at[step - 1],
            z_send.at[step - 1],
            z_recv.at[step - 1],
            base + lax.rem(own - step + in_set, in_set),
        )

    def gather_own(index):
        step = order[index]
        await_flow(index, flows[0])

        @pl.loop(0, rows // tile)
        def _(i):
            row = pl.multiple_of(i * tile, tile)
            total = placed(step, row, got)
            if step:
                out_z[step - 1, pl.ds(row, tile), :] = total.astype(bf16)
            else:
                shard_ref[pl.ds(row, tile), :] = total

        if step:
            back(step).start()

    def gather_other(index):
        step = order[index]
        await_flow(index, flows[1])

        @pl.loop(0, rows // tile)
        def _(i):
            row = pl.multiple_of(i * tile, tile)
            placed_ref[step, pl.ds(row, tile), :] = placed(step, row, other).astype(bf16)

    load(0).start()
    load(1).start()
    first_cols = w1_main_ref.shape[1]
    w1_loads = [
        pltpu.make_async_copy(w1_main_ref, w1_ref.at[:, pl.ds(0, first_cols)], w1_sem.at[0]),
        pltpu.make_async_copy(
            w1_tail_ref,
            w1_ref.at[:, pl.ds(first_cols, w1_tail_ref.shape[1])],
            w1_sem.at[1],
        ),
    ]
    late_rows = late_ref.shape[1]
    early_rows = sum(early_refs[planes * part].shape[0] for part in range(EARLY_PARTS))
    depth = early_rows + late_rows
    w2_loads = [
        pltpu.make_async_copy(
            w2_tail_ref, w2_ref.at[:, pl.ds(hidden, w2_tail_ref.shape[1])], w2_sem.at[0]
        )
    ]

    def place_rows(piece_ref, start):
        w2_loads.append(
            pltpu.make_async_copy(
                piece_ref,
                w2_ref.at[pl.ds(pl.multiple_of(start, 16), piece_ref.shape[0]), pl.ds(0, hidden)],
                w2_sem.at[len(w2_loads)],
            )
        )

    for number in range(planes):
        source = lax.rem(plane - number + planes, planes)
        start = source * depth
        for part in range(EARLY_PARTS):
            piece_ref = early_refs[planes * part + number]
            place_rows(piece_ref, start)
            start = start + piece_ref.shape[0]
        place_rows(late_ref.at[number], number * depth + early_rows)
    for copy in w1_loads + w2_loads:
        copy.start()
    greet_all(planes, groups)
    lane = lax.broadcasted_iota(jnp.int32, (CAP, 128), 1)
    for index, step in enumerate(order):
        at = pl.ds(step * CAP, CAP)
        load(index).wait()
        middle = slot_buf[index % 2, 0].astype(f32)
        scale = lax.rsqrt(jnp.mean(middle * middle, axis=-1, keepdims=True) + norm_eps)
        expert_in = (middle * scale * gain_ref[...]).astype(bf16)
        if index == 0:
            for copy in w1_loads:
                copy.wait()
        pre = mul(expert_in, w1_ref[...], 1, 0)
        both_masks = mask_ref[at, :]
        mask_down = mask_down_ref[at, :]
        valid = jnp.max(mask_down, axis=1, keepdims=True)
        rank_gu = (pre[:, 2 * hidden : 2 * hidden + rank] * both_masks).astype(bf16)
        logits = pre[:, 2 * hidden + rank :]
        first = lane < names // 2
        peak = jnp.max(jnp.where(first, logits, -1e30), axis=1, keepdims=True)
        raised = jnp.exp(jnp.where(lane < names, logits, -1e30) - peak)
        probs = raised / jnp.sum(jnp.where(first, raised, 0.0), axis=1, keepdims=True)
        is_own = own_ref[...]
        gate = jnp.sum(jnp.where(first, probs * is_own, 0.0), axis=1, keepdims=True) * valid
        gate_pre = pre[:, :hidden] + rank_scale * mul(rank_gu, hg_ref[...], 1, 1)
        up_pre = pre[:, hidden : 2 * hidden] + rank_scale * mul(rank_gu, hu_ref[...], 1, 1)
        sigma = 1.0 / (1.0 + jnp.exp(-gate_pre))
        activated = gate_pre * sigma
        inner = (activated * up_pre).astype(bf16)
        rank_down = (mul(inner, hd_ref[...], 1, 0) * mask_down).astype(bf16)
        inner_wide = jnp.concatenate(
            [inner, (down_scale * rank_down.astype(f32)).astype(bf16)], axis=1
        )
        if index == 0:
            for copy in w2_loads:
                copy.wait()
        output = mul(inner_wide, w2_ref[...], 1, 1)
        cotangent = slot_buf[index % 2, 1].astype(f32)
        gate_grad = jnp.sum(cotangent * output, axis=1, keepdims=True)
        if index >= 2:
            left_flow(index - 2, flows[1])
            left_flow(index - 2, flows[0])
        m_stage[index % 2] = (gate * output).astype(bf16)
        if index < last:
            start_flow(index, flows[1])
        weighted = (gate * cotangent).astype(bf16)
        inner_grads = mul(weighted, w2_ref[...], 1, 0)
        rank_down_grad = (down_scale * inner_grads[:, hidden:] * mask_down).astype(bf16)
        inner_grad = inner_grads[:, :hidden] + mul(rank_down_grad, hd_ref[...], 1, 1)
        gate_pre_grad = (
            inner_grad * up_pre * sigma * (1.0 + gate_pre * (1.0 - sigma))
        ).astype(bf16)
        up_pre_grad = (inner_grad * activated).astype(bf16)
        rank_gu_grad = (
            rank_scale
            * (mul(gate_pre_grad, hg_ref[...], 1, 0) + mul(up_pre_grad, hu_ref[...], 1, 0))
            * both_masks
        ).astype(bf16)
        logit_grad = (is_own - probs) * (gate * gate_grad)
        logit_high = logit_grad.astype(bf16)
        logit_rest = logit_grad - logit_high.astype(f32)
        logit_two = jnp.where(first, logit_high.astype(f32), logit_rest)
        logit_two = jnp.where(lane < names, logit_two, 0.0).astype(bf16)
        wide = jnp.concatenate([gate_pre_grad, up_pre_grad, rank_gu_grad, logit_two], axis=1)
        u_stage[index % 2] = mul(wide, w1_ref[...], 1, 1).astype(bf16)
        start_flow(index, flows[0])
        if index == last:
            start_flow(index, flows[1])
        if index + 2 <= last:
            load(index + 2).start()

        def add(ref, value):
            if index:
                ref[...] += value
            else:
                ref[...] = value

        add(wide_ref, mul(rank_gu_grad, expert_in, 0, 0))
        add(wide_down_ref, down_scale * mul(rank_down, weighted, 0, 0))
        add(hg_grad_ref, rank_scale * mul(rank_gu, gate_pre_grad, 0, 0))
        add(hu_grad_ref, rank_scale * mul(rank_gu, up_pre_grad, 0, 0))
        add(hd_grad_ref, mul(rank_down_grad, inner, 0, 0))
        if index >= 2:
            gather_own(index - 2)
    for index in range(max(0, last - 1), last):
        gather_own(index)
    for index in range(max(0, last - 1)):
        gather_other(index)
    gather_own(last)
    for step in range(1, in_set):
        back(step).wait_recv()

    @pl.loop(0, rows // tile)
    def _(i):
        row = pl.multiple_of(i * tile, tile)
        total = shard_ref[pl.ds(row, tile), :]
        for step in range(1, in_set):
            total = total + in_z[step - 1, pl.ds(row, tile), :].astype(f32)
        shard_ref[pl.ds(row, tile), :] = total
        low[pl.ds(row, tile), :] = total.astype(bf16)

    def columns(owner):
        return rows_ref.at[:, columns_of(owner)]

    mine = pltpu.make_async_copy(low, columns(me), c_own)
    mine.start()
    out = []
    for step in list(range(1, chips)) + [0]:
        target = sibling if step == 0 else chip_peer(chip, core, step, chips)
        copy = remote(low, columns(me), c_send.at[step], c_recv.at[step], target)
        copy.start()
        out.append(copy)
    for index in range(max(0, last - 1), last + 1):
        gather_other(index)
    for step in range(1, chips):
        out[step - 1].wait_recv()
        source = chip_peer(chip, core, chips - step, chips)
        copy = remote(
            columns(source), columns(source), p_send.at[step], p_recv.at[step], sibling
        )
        copy.start()
        out.append(copy)
    mine.wait()
    out[chips - 1].wait_recv()
    for copy in out[chips:]:
        copy.wait_recv()
    for copy in out:
        copy.wait_send()
    for step in range(1, in_set):
        back(step).wait_send()
    for index in range(max(0, last - 1), last + 1):
        left_flow(index, flows[0])
        left_flow(index, flows[1])


def experts(
    slots,
    w1_main,
    w1_tail,
    early,
    late,
    w2_tail,
    hg,
    hu,
    hd,
    masks,
    mask_down,
    own,
    gain,
    key,
    names,
    planes,
    groups,
    collective_id,
):
    in_set, rows = key.shape[0], key.shape[2]
    full = slots.shape[2]
    width = full // groups
    chips = groups // 2
    tile = min(256, rows)
    hidden, rank = hg.shape
    down = hd.shape[1]
    anywhere = pl.BlockSpec(memory_space=pl.ANY)
    return pl.pallas_call(
        functools.partial(experts_kernel, planes, groups, in_set, tile, names),
        out_shape=(
            jax.ShapeDtypeStruct((rows, width), f32),
            jax.ShapeDtypeStruct((rows, full), bf16),
            jax.ShapeDtypeStruct((in_set, rows, width), bf16),
            jax.ShapeDtypeStruct((rank, full), f32),
            jax.ShapeDtypeStruct((down, full), f32),
            jax.ShapeDtypeStruct((rank, hidden), f32),
            jax.ShapeDtypeStruct((rank, hidden), f32),
            jax.ShapeDtypeStruct((down, hidden), f32),
        ),
        in_specs=[anywhere] * 5 + [VMEM] * 8 + [anywhere] * (planes * EARLY_PARTS),
        out_specs=(VMEM, anywhere) + (VMEM,) * 6,
        scratch_shapes=[
            pltpu.VMEM((full, w1_main.shape[1] + w1_tail.shape[1]), bf16),
            pltpu.VMEM((full, hidden + w2_tail.shape[1]), bf16),
            pltpu.VMEM((2, 2, CAP, full), bf16),
            pltpu.VMEM((2, CAP, full), bf16),
            pltpu.VMEM((2, CAP, full), bf16),
            pltpu.VMEM((in_set, groups * CAP, width), bf16),
            pltpu.VMEM((in_set, groups * CAP, width), bf16),
            pltpu.VMEM((in_set - 1, rows, width), bf16),
            pltpu.VMEM((in_set - 1, rows, width), bf16),
            pltpu.VMEM((rows, width), bf16),
            DMA((2,)),
            DMA(((EARLY_PARTS + 1) * planes + 1,)),
            DMA((2,)),
            DMA((in_set, groups)),
            DMA((in_set, groups)),
            DMA((in_set, groups)),
            DMA((in_set, groups)),
            DMA((2, in_set)),
            DMA((in_set - 1,)),
            DMA((in_set - 1,)),
            DMA,
            DMA((chips,)),
            DMA((chips,)),
            DMA((chips,)),
            DMA((chips,)),
        ],
        compiler_params=pltpu.CompilerParams(
            collective_id=collective_id, has_side_effects=True, vmem_limit_bytes=62 << 20
        ),
        cost_estimate=SMALL,
    )(
        slots, w1_main, w1_tail, late, w2_tail, hg, hu, hd, masks, mask_down, own, gain, key, *early
    )


def planes_kernel(planes, x_ref, o_ref, own_sem, send_sem, recv_sem):
    plane = lax.axis_index("gx")
    barrier = pltpu.get_barrier_semaphore()
    own = pltpu.make_async_copy(x_ref, o_ref.at[plane], own_sem)
    own.start()
    for step in range(1, planes):
        target = lax.rem(plane + step, planes)
        pl.semaphore_signal(barrier, inc=1, device_id={"gx": target}, device_id_type=MESH)
    pl.semaphore_wait(barrier, planes - 1)
    copies = []
    for step in range(1, planes):
        copy = to_plane(
            x_ref,
            o_ref.at[plane],
            send_sem.at[step - 1],
            recv_sem.at[step - 1],
            lax.rem(plane + step, planes),
        )
        copy.start()
        copies.append(copy)
    own.wait()
    for copy in copies:
        copy.wait_recv()
        copy.wait_send()


def gather_planes(x, planes, collective_id):
    return pl.pallas_call(
        functools.partial(planes_kernel, planes),
        out_shape=jax.ShapeDtypeStruct((planes,) + x.shape, x.dtype),
        in_specs=[VMEM],
        out_specs=VMEM,
        scratch_shapes=[DMA, DMA((planes - 1,)), DMA((planes - 1,))],
        compiler_params=pltpu.CompilerParams(collective_id=collective_id, has_side_effects=True),
        cost_estimate=SMALL,
    )(x)


def rope_tables(length, width):
    half_width = width // 2
    frequency = rope_theta ** (-2.0 * jnp.arange(half_width, dtype=f32) / width)
    angles = jnp.arange(length, dtype=f32)[:, None] * frequency[None, :]
    return (jnp.cos(angles), jnp.sin(angles))


def apply_rotary(values, cosine, sine):
    half_width = values.shape[-1] // 2
    first = values[..., :half_width]
    second = values[..., half_width:]
    return jnp.concatenate(
        [first * cosine - second * sine, second * cosine + first * sine], axis=-1
    )


def unrotate(grads, cosine, sine):
    half_width = grads.shape[-1] // 2
    first = grads[..., :half_width]
    second = grads[..., half_width:]
    return jnp.concatenate(
        [first * cosine + second * sine, second * cosine - first * sine], axis=-1
    )


def allowed_mask(piece_starts):
    places = jnp.arange(SEQ, dtype=jnp.int32)
    causal = places[None, :] <= places[:, None]
    inside = (places[None, None, :] >= piece_starts[:, :, None]) & (
        places[None, None, :] < piece_starts[:, :, None] + PIECE
    )
    same_piece = jnp.any(inside[:, :, :, None] & inside[:, :, None, :], axis=1)
    return causal[None] | same_piece


def dot(spec, left, right):
    return jnp.einsum(spec, left, right, preferred_element_type=f32)


def after(first, *later):
    return lax.optimization_barrier((first,) + later)[1:]


def shards(
    block_input,
    out_grad,
    routes,
    adapter_ids,
    piece_starts,
    attn_gain,
    qk_gain,
    mlp_gain,
    w_qkv,
    w_out,
    a_qkv,
    b_out,
    head_pack,
    router,
    w_gate_up,
    w_down,
    exp_wide,
    exp_hidden,
):
    planes = lax.axis_size("gx")
    groups = lax.axis_size("gy")
    plane = lax.axis_index("gx")
    column = lax.axis_index("gy")
    rows, width_local = block_input.shape
    width = width_local * groups
    heads_local = head_pack.shape[0]
    rank_cols = head_pack.shape[2]
    head_width = head_pack.shape[3]
    experts_local = w_gate_up.shape[0]
    hidden_width = w_gate_up.shape[3]
    nseq = adapter_ids.shape[0]
    inv_root = head_width ** (-0.5)
    repeats = planes // experts_local
    steps = range(experts_local)
    own = lax.rem(plane, experts_local)

    def shifted(x, step):
        if step % experts_local == 0:
            return x
        pairs = []
        for p in range(planes):
            base = p // experts_local * experts_local
            pairs.append((p, base + (p - base + step) % experts_local))
        return lax.ppermute(x, "gx", pairs)

    def own_pieces(piece_for):
        pieces = []
        for step in range(planes):
            piece = piece_for(lax.rem(plane + step, planes))
            if step:
                pairs = [(p, (p + step) % planes) for p in range(planes)]
                piece = lax.ppermute(piece, "gx", pairs)
            pieces.append((lax.rem(plane - step + planes, planes), piece))
        return pieces

    compact = nseq * RANK

    def pick(x, axis):
        return jnp.concatenate(
            [
                lax.dynamic_slice_in_dim(x, adapter_ids[n] * RANK, RANK, axis=axis)
                for n in range(nseq)
            ],
            axis=axis,
        )

    token_seq = jnp.arange(rows, dtype=jnp.int32) // SEQ
    col_seq = jnp.arange(compact, dtype=jnp.int32) // RANK
    compact_mask = (token_seq[:, None] == col_seq[None, :]).astype(f32)
    a_pick = pick(a_qkv, 2)
    b_pick = pick(b_out, 0)
    pack_pick = pick(head_pack, 2)

    top = routes.shape[1]
    whole = jnp.concatenate(
        [routes.reshape(rows * top // 128, 128), jnp.zeros((8, 128), jnp.int32)], axis=0
    )
    whole = lax.dynamic_update_slice(whole, adapter_ids[None, :], (rows * top // 128, 0))
    whole = gather_planes(whole, planes, 10)
    routes_all = whole[:, : rows * top // 128].reshape(planes, rows, top)
    adapters_all = whole[:, rows * top // 128, :nseq]
    dl = w_gate_up.shape[1]
    hl = exp_hidden.shape[1]
    qkv_width = 3 * heads_local * head_width
    weight_shard = jnp.concatenate(
        [
            w_qkv.reshape(w_qkv.shape[0], qkv_width),
            w_out.reshape(heads_local * head_width, w_out.shape[2]).T,
        ],
        axis=1,
    )
    attn_weight = lax.all_gather(weight_shard, "gx", axis=0, tiled=True)
    normed_bf, scale_one, gathered = gather_normed(
        jnp.concatenate(
            [block_input, a_pick.transpose(0, 2, 1).reshape(3 * compact, width_local), b_pick],
            axis=0,
        ),
        attn_gain,
        rows,
        groups,
        1,
    )
    scale_one = scale_one[:, :1]
    a_full = gathered[: 3 * compact]
    b_full = gathered[3 * compact :]

    set_cols = experts_local * compact
    fold = max(1, 128 // set_cols)
    sets_adapters = adapters_all.reshape(repeats, experts_local * nseq)
    rank_index = jnp.arange(rank_cols, dtype=jnp.int32)
    set_index = jnp.arange(set_cols, dtype=jnp.int32)
    set_pick = (
        (rank_index // RANK)[None, :, None] == jnp.repeat(sets_adapters, RANK, axis=1)[:, None, :]
    ) & ((rank_index % RANK)[None, :, None] == (set_index % RANK)[None, None, :])
    set_pick = set_pick.astype(bf16)

    def folded(x):
        return jnp.concatenate(jnp.split(x, fold, axis=1), axis=2)

    def unfolded(x):
        return jnp.concatenate(jnp.split(x, fold, axis=2), axis=1)

    rank_rows = jnp.concatenate(
        [exp_wide[:, :, c] for c in range(3)] + [exp_hidden[:, :, c] for c in range(3)], axis=1
    )
    rank_shard = folded(
        dot("emr,srk->semk", rank_rows, set_pick)
        .reshape(planes, rank_rows.shape[1], set_cols)
        .astype(bf16)
    )
    expert_ids = own + experts_local * jnp.arange(groups, dtype=jnp.int32)
    set_start = (plane // experts_local) * experts_local
    step_plane = lax.rem(own - jnp.arange(experts_local) + experts_local, experts_local)
    routes_set = routes_all[set_start + step_plane]
    hits = jnp.any(routes_set[:, :, :, None] == expert_ids, axis=2)
    order = jnp.arange(rows, dtype=jnp.int32)
    earlier = (order[None, :] < order[:, None]).astype(bf16)
    places = dot("ts,gsc->gct", earlier, hits.astype(bf16))
    slot_key = jnp.where(hits.transpose(0, 2, 1), places.astype(jnp.int32), -1)
    slots = jnp.arange(CAP, dtype=jnp.int32)
    column_key = slot_key + CAP * jnp.arange(groups, dtype=jnp.int32)[None, :, None]
    column_key = jnp.where(slot_key >= 0, column_key, -1)
    own_key = lax.dynamic_index_in_dim(slot_key, column, 1, keepdims=False)
    own_pick = (own_key[:, None, :] == slots[None, :, None]).astype(bf16)
    rank_mask = (
        (step_plane[:, None] * nseq + token_seq[None, :])[:, :, None]
        == (set_index // RANK)[None, None, :]
    ).astype(bf16)
    slot_total = experts_local * CAP
    mask_slot = dot("gst,gtr->gsr", own_pick, rank_mask).reshape(slot_total, set_cols)

    gate_up_flat = w_gate_up.reshape(experts_local, dl, 2 * hidden_width)
    names = 2 * router.shape[1]
    down_pad = -set_cols % 128
    own_id = column * experts_local + own
    is_own = (jnp.arange(names, dtype=jnp.int32) % router.shape[1] == own_id).astype(f32)
    is_own = jnp.pad(is_own, (0, 128 - names)).reshape(1, 128)
    two_masks = jnp.concatenate([mask_slot, mask_slot], axis=1)
    down_mask = jnp.pad(mask_slot, ((0, 0), (0, down_pad)))
    router_twice = jnp.pad(
        jnp.concatenate([router, router], axis=1), ((0, 0), (0, 128 - names))
    )
    (
        attn_weight,
        slot_key,
        column_key,
        two_masks,
        down_mask,
        is_own,
        router_twice,
        rank_shard,
    ) = lax.optimization_barrier(
        (
            attn_weight,
            slot_key,
            column_key,
            two_masks,
            down_mask,
            is_own,
            router_twice,
            rank_shard,
        )
    )
    rank_sent = lax.all_to_all(rank_shard, "gx", 0, 0, tiled=True)

    (down_later,) = after(rank_sent, w_down)
    early_rows = 0
    early_parts = []
    for eighths in (2, 3):
        count = dl * eighths // 8
        pieces = own_pieces(
            lambda p: lax.dynamic_slice(
                down_later,
                (lax.rem(p, experts_local), early_rows, 0),
                (1, count, hidden_width),
            )[0]
        )
        early_parts.append([piece for _, piece in pieces])
        early_rows += count
        (down_later,) = after(early_parts[-1][-1], w_down)
    rank_weight = unfolded(rank_sent)

    def rank_part(start, count):
        return rank_weight[:, start : start + count].reshape(planes * count, set_cols)

    wide_parts = [rank_part(c * dl, dl) for c in range(3)]
    hidden_gate, hidden_up, hidden_down = [rank_part(3 * dl + c * hl, hl) for c in range(3)]
    no_rank = jnp.zeros((hidden_width, set_cols), bf16)
    rank_operands = (
        jnp.concatenate([wide_parts[0], wide_parts[1], router_twice], axis=1),
        jnp.pad(wide_parts[2], ((0, 0), (0, down_pad))),
        jnp.concatenate([hidden_gate, no_rank], axis=1),
        jnp.concatenate([no_rank, hidden_up], axis=1),
        jnp.pad(hidden_down, ((0, 0), (0, down_pad))),
    )

    col_start = column * width_local
    first_norm_gain = lax.dynamic_slice_in_dim(attn_gain, col_start, width_local)
    base = dot("td,de->te", normed_bf, attn_weight[:, :qkv_width]).reshape(
        rows, heads_local, 3, head_width
    )
    rank_in = dot("td,kd->tk", normed_bf, a_full).reshape(rows, 3, compact)
    rank_low = (rank_in * compact_mask[:, None, :]).astype(bf16)
    projected = base + rank_scale * dot("tcr,hcre->thce", rank_low, pack_pick[:, :3])
    query_pre = projected[:, :, 0]
    key_pre = projected[:, :, 1]
    value_bf = projected[:, :, 2].astype(bf16)
    square_sums = jnp.stack(
        [jnp.sum(query_pre * query_pre, axis=(1, 2)), jnp.sum(key_pre * key_pre, axis=(1, 2))]
    )
    (square_sums,) = after(rank_sent, square_sums)
    square_sums = add_small(square_sums.reshape(-1, 128), groups, 2).reshape(2, rows)
    query_scale = lax.rsqrt(square_sums[0] / width + norm_eps)[:, None, None]
    key_scale = lax.rsqrt(square_sums[1] / width + norm_eps)[:, None, None]
    head_start = column * heads_local * head_width
    gains_local = lax.dynamic_slice_in_dim(
        qk_gain, head_start, heads_local * head_width, axis=1
    ).reshape(2, heads_local, head_width)
    query_hat = query_pre * query_scale
    key_hat = key_pre * key_scale
    cosine, sine = rope_tables(SEQ, head_width)
    cosine = cosine[None, :, None, :]
    sine = sine[None, :, None, :]
    query_bf = apply_rotary(
        (query_hat * gains_local[0]).reshape(nseq, SEQ, heads_local, head_width), cosine, sine
    ).astype(bf16)
    key_bf = apply_rotary(
        (key_hat * gains_local[1]).reshape(nseq, SEQ, heads_local, head_width), cosine, sine
    ).astype(bf16)
    query_bf, *first_early = lax.optimization_barrier((query_bf, *early_parts[0]))
    values_seq = value_bf.reshape(nseq, SEQ, heads_local, head_width)
    allowed = allowed_mask(piece_starts)[:, None]
    scores = dot("nqhe,nkhe->nhqk", query_bf, key_bf) * inv_root
    scores = jnp.where(allowed, scores, -1e30)
    row_peak = jnp.max(scores, axis=-1, keepdims=True)
    raised = jnp.exp(scores - row_peak)
    row_total = jnp.sum(raised, axis=-1, keepdims=True)
    log_total = row_peak + jnp.log(row_total)
    weights = raised / row_total
    attended = dot("nhqk,nkhe->nqhe", weights.astype(bf16), values_seq)
    attn_bf = attended.reshape(rows, heads_local, head_width).astype(bf16)
    rank_out = dot("the,hre->thr", attn_bf, pack_pick[:, 3])
    rank_out_low = (rank_out * compact_mask[:, None, :]).astype(bf16)
    out_weight = attn_weight[:, qkv_width:]
    b_turned = (rank_scale * b_full.T).astype(bf16)
    branch_left = jnp.concatenate(
        [
            attn_bf.reshape(rows, heads_local * head_width),
            rank_out_low.reshape(rows, heads_local * compact),
        ],
        axis=1,
    )
    branch_left, qkv_weight, gate_up_flat, *rank_operands = lax.optimization_barrier(
        (branch_left, attn_weight[:, :qkv_width], gate_up_flat) + rank_operands
    )
    branch_left, *second_early = lax.optimization_barrier((branch_left, *early_parts[1]))
    early = first_early + second_early
    branch, late_pieces = scatter_product(
        branch_left,
        jnp.concatenate([out_weight] + [b_turned] * heads_local, axis=1),
        groups,
        3,
        w_down,
        early_rows,
        planes,
    )
    middle = block_input.astype(f32) + branch
    middle_low = middle.astype(bf16)

    slot_rows, gate_up_weight = spread(
        jnp.concatenate([middle_low, out_grad], axis=1),
        slot_key,
        gate_up_flat,
        planes,
        groups,
        2 * hidden_width,
        4,
    )
    both_rows = lax.all_gather(
        jnp.concatenate([middle_low, out_grad], axis=0), "gy", axis=1, tiled=True
    )
    (
        normed_two_part,
        normed_two_rows,
        moe_planes,
        wide_gu_grad,
        wide_down_grad,
        gate_rank_grad,
        up_rank_grad,
        down_rank_grad,
    ) = experts(
        slot_rows,
        gate_up_weight,
        rank_operands[0],
        early,
        late_pieces,
        *rank_operands[1:],
        two_masks,
        down_mask,
        is_own,
        mlp_gain.reshape(1, width),
        column_key,
        names,
        planes,
        groups,
        5,
    )
    moe_pieces = [
        shifted(moe_planes[step], experts_local - step) for step in range(1, experts_local)
    ]

    wide_grads = [
        wide_gu_grad[:set_cols],
        wide_gu_grad[set_cols:],
        wide_down_grad[:set_cols],
    ]
    hidden_grads = [
        gate_rank_grad[:set_cols],
        up_rank_grad[set_cols:],
        down_rank_grad[:set_cols],
    ]
    rank_grads = jnp.concatenate(
        [x.astype(bf16).T.reshape(planes, dl, set_cols) for x in wide_grads]
        + [x.astype(bf16).T.reshape(planes, hl, set_cols) for x in hidden_grads],
        axis=1,
    )
    middle_rows = both_rows[:rows].astype(f32)
    grad_rows = both_rows[rows:].astype(f32)
    scale_two = lax.rsqrt(jnp.mean(middle_rows * middle_rows, axis=-1, keepdims=True) + norm_eps)
    normed_two_grad = normed_two_rows.astype(f32)
    hat_two = middle_rows * scale_two
    scaled_two = normed_two_grad * mlp_gain
    stat_two = jnp.mean(scaled_two * hat_two, axis=-1, keepdims=True)
    branch_rows = (grad_rows + scale_two * (scaled_two - hat_two * stat_two)).astype(bf16)
    gain_two_local = lax.dynamic_slice_in_dim(mlp_gain, col_start, width_local)
    middle_grad = out_grad.astype(f32) + scale_two * (
        normed_two_part * gain_two_local - middle_low.astype(f32) * scale_two * stat_two
    )
    rank_out_grad = rank_scale * dot("td,rd->tr", branch_rows, b_full)
    rank_out_bf = (rank_out_grad * compact_mask).astype(bf16)
    pack_out_grad = dot("the,tr->hre", attn_bf, rank_out_bf)
    attention_gradient = dot("td,de->te", branch_rows, out_weight).reshape(
        rows, heads_local, head_width
    ) + dot(
        "tr,hre->the", rank_out_bf, pack_pick[:, 3]
    )
    attn_grad_bf = attention_gradient.reshape(nseq, SEQ, heads_local, head_width).astype(bf16)
    scores_again = dot("nqhe,nkhe->nhqk", query_bf, key_bf) * inv_root
    scores_again = jnp.where(allowed, scores_again, -1e30)
    weights_again = jnp.exp(scores_again - log_total)
    value_grad = dot("nhqk,nqhe->nkhe", weights_again.astype(bf16), attn_grad_bf)
    weight_grad = dot("nqhe,nkhe->nhqk", attn_grad_bf, values_seq)
    row_dot = jnp.sum(weight_grad * weights_again, axis=-1, keepdims=True)
    score_grad = (weights_again * (weight_grad - row_dot)).astype(bf16)
    query_grad = dot("nhqk,nkhe->nqhe", score_grad, key_bf) * inv_root
    key_grad = dot("nhqk,nqhe->nkhe", score_grad, query_bf) * inv_root
    query_hat_grad = (
        unrotate(query_grad, cosine, sine).reshape(rows, heads_local, head_width) * gains_local[0]
    )
    key_hat_grad = (
        unrotate(key_grad, cosine, sine).reshape(rows, heads_local, head_width) * gains_local[1]
    )
    value_pre_grad = value_grad.reshape(rows, heads_local, head_width)
    stat_query = jnp.sum(query_hat_grad * query_hat, axis=(1, 2))
    stat_key = jnp.sum(key_hat_grad * key_hat, axis=(1, 2))

    def rank_terms(values, which):
        return dot("the,hre->rt", values.astype(bf16), pack_pick[:, which])

    pad_rows = -6 * compact % 32 or 32
    sums = jnp.concatenate(
        [
            piece.astype(bf16)
            for piece in (
                rank_terms(query_hat_grad, 0),
                rank_terms(key_hat_grad, 1),
                rank_terms(value_pre_grad, 2),
                rank_terms(query_hat, 0),
                rank_terms(key_hat, 1),
                jnp.sum(rank_out_low.astype(f32), axis=1).T,
                jnp.pad(jnp.stack([stat_query, stat_key]), ((0, pad_rows - 2), (0, 0))),
            )
        ],
        axis=0,
    )
    sums = add_pairs(sums, groups, 6)
    first_total = sums[: 3 * compact].reshape(3, compact, rows)
    second_total = sums[3 * compact : 5 * compact].reshape(2, compact, rows)
    mean_qk = sums[6 * compact : 6 * compact + 2] / width
    branch_local = lax.dynamic_slice_in_dim(branch_rows, col_start, width_local, axis=1)
    b_out_sum = rank_scale * dot(
        "rt,td->rd", sums[5 * compact : 6 * compact].astype(bf16), branch_local
    )
    scales_qk = jnp.stack([query_scale[:, 0, 0], key_scale[:, 0, 0]])
    rank_qk = scales_qk[:, None, :] * (first_total[:2] - second_total * mean_qk[:, None, :])
    rank_grad_full = rank_scale * jnp.concatenate([rank_qk, first_total[2:]], axis=0)
    rank_grad_bf = (rank_grad_full * compact_mask.T[None]).astype(bf16)
    query_pre_grad = query_scale * (query_hat_grad - query_hat * mean_qk[0][:, None, None])
    key_pre_grad = key_scale * (key_hat_grad - key_hat * mean_qk[1][:, None, None])
    pre_grad = jnp.stack([query_pre_grad, key_pre_grad, value_pre_grad], axis=2).astype(bf16)
    pack_b_grad = rank_scale * dot("tcr,thce->rhce", rank_low, pre_grad)
    adapter_input_gradient = dot("crt,cdr->td", rank_grad_bf, a_pick)
    first_normalized_shard = block_input.astype(f32) * scale_one
    normed_local_bf = lax.dynamic_slice_in_dim(normed_bf, col_start, width_local, axis=1)
    a_rows_grad = dot("td,crt->rcd", normed_local_bf, rank_grad_bf)
    pack_grad = jnp.concatenate(
        [
            pack_b_grad.transpose(1, 2, 0, 3),
            pack_out_grad[:, None],
        ],
        axis=1,
    )
    small = jnp.concatenate(
        [
            a_rows_grad.reshape(compact, 3 * width_local),
            b_out_sum,
            pack_grad.transpose(2, 0, 1, 3).reshape(compact, heads_local * 4 * head_width),
        ],
        axis=1,
    )
    small_rows = small.astype(bf16).reshape(-1, 128)
    rank_grads = folded(rank_grads)
    rank_row_count = rank_grads.shape[1]
    carried = jnp.concatenate(
        [rank_grads, jnp.broadcast_to(small_rows, (planes,) + small_rows.shape)], axis=1
    )
    normed_one_grad, came = scatter_product(
        pre_grad.reshape(rows, qkv_width), qkv_weight, groups, 7, carried, 0, planes
    )
    scaled_one = (normed_one_grad + adapter_input_gradient) * first_norm_gain
    stat_one = jnp.sum(scaled_one * first_normalized_shard, axis=-1)
    stat_one_sum = add_small(stat_one.reshape(-1, 128), groups, 8).reshape(rows, 1)
    input_grad = middle_grad + scale_one * (
        scaled_one - first_normalized_shard * stat_one_sum / width
    )
    moe_pieces = after(normed_one_grad, *moe_pieces)
    rank_grads = came[:, :rank_row_count]
    moe_part = moe_planes[0].astype(f32)
    for piece in moe_pieces:
        moe_part = moe_part + piece.astype(f32)
    layer_out = (middle + moe_part).astype(bf16)
    rank_grads = unfolded(rank_grads)
    rank_grads = rank_grads.reshape((repeats, experts_local) + rank_grads.shape[1:])
    wide_sum = jnp.stack(
        [
            dot("semk,srk->emr", rank_grads[:, :, c * dl : (c + 1) * dl], set_pick)
            for c in range(3)
        ],
        axis=2,
    )
    hidden_sum = jnp.stack(
        [
            dot(
                "semk,srk->emr",
                rank_grads[:, :, 3 * dl + c * hl : 3 * dl + (c + 1) * hl],
                set_pick,
            )
            for c in range(3)
        ],
        axis=2,
    )

    small_all = came[:, rank_row_count:].reshape(planes * compact, small.shape[1])
    row_at = (
        adapters_all[:, :, None] * RANK + jnp.arange(RANK, dtype=jnp.int32)[None, None, :]
    ).reshape(-1)
    put = (jnp.arange(rank_cols, dtype=jnp.int32)[:, None] == row_at[None, :]).astype(bf16)
    small_sum = jnp.dot(put, small_all, preferred_element_type=f32)
    a_end = 3 * width_local
    b_end = a_end + width_local
    a_sum = small_sum[:, :a_end].reshape(rank_cols, 3, width_local).transpose(1, 2, 0)
    b_sum = small_sum[:, a_end:b_end]
    head_sum = small_sum[:, b_end:].reshape(rank_cols, heads_local, 4, head_width)
    head_sum = head_sum.transpose(1, 2, 0, 3)
    return (layer_out, input_grad, a_sum, b_sum, head_sum, wide_sum, hidden_sum)


def solution(mesh):
    return jax.shard_map(
        shards,
        mesh=mesh,
        in_specs=(
            P("gx", "gy"),
            P("gx", "gy"),
            P("gx", None),
            P("gx"),
            P("gx", None),
            P(),
            P(),
            P(),
            P("gx", "gy", None, None),
            P("gy", None, "gx"),
            P(None, "gy", None),
            P(None, "gy"),
            P("gy", None, None, None),
            P(),
            P("gy", "gx", None, None),
            P("gy", "gx", None),
            P("gy", "gx", None, None),
            P("gy", "gx", None, None),
        ),
        out_specs=(
            P("gx", "gy"),
            P("gx", "gy"),
            P(None, "gy", None),
            P(None, "gy"),
            P("gy", None, None, None),
            P("gy", "gx", None, None),
            P("gy", "gx", None, None),
        ),
        check_vma=False,
    )
```
